32 devices in a mesh: ctx: 8 (over y, x, core), fsdp: 4 (over z).
Axes of the slice: x: 2, y: 2, z: 4, core: 2. Of those that a mesh axis runs over, the one named last changes fastest.
Arguments:
- tokens: bfloat16 [8, 4096, 1024], P('fsdp', 'ctx'), may hold values from -10 to 10, as said below
- document_ids: int32 [8, 4096], P('fsdp', 'ctx'), may hold values from 0 to 3, as said below
- mixer_weight: bfloat16 [1024, 2048], P(('ctx', 'fsdp')), may hold values from -0.1875 to 0.1875
- output_weight: bfloat16 [1024, 1024], P(('ctx', 'fsdp')), may hold values from -3 to 3
- mixer_gain: bfloat16 [1024], P(('ctx', 'fsdp')), may hold values from 0.5 to 1.5
- expand_weight: bfloat16 [1024, 9216], P(('ctx', 'fsdp')), may hold values from -0.1875 to 0.1875
- shrink_weight: bfloat16 [4608, 1024], P(('ctx', 'fsdp')), may hold values from -0.09375 to 0.09375
- feed_gain: bfloat16 [1024], P(('ctx', 'fsdp')), may hold values from 0.5 to 1.5
- head_gains: float32 [2, 64], replicated, may hold values from 0.5 to 1.5
- cotangent: bfloat16 [8, 4096, 1024], P('fsdp', 'ctx'), may hold values from -6 to 6
Outputs:
- result: bfloat16 [8, 4096, 1024], P('fsdp', 'ctx')
- tokens_gradient: bfloat16 [8, 4096, 1024], P('fsdp', 'ctx')
- mixer_gradient: float32 [1024, 2048], P(('ctx', 'fsdp'))
- output_gradient: float32 [1024, 1024], P(('ctx', 'fsdp'))
- mixer_gain_gradient: float32 [1024], P(('ctx', 'fsdp'))
- expand_gradient: float32 [1024, 9216], P(('ctx', 'fsdp'))
- shrink_gradient: float32 [4608, 1024], P(('ctx', 'fsdp'))
- feed_gain_gradient: float32 [1024], P(('ctx', 'fsdp'))
- head_gains_gradient: float32 [2, 64], replicated
- statistics: float32 [3], replicated
The draws below stay inside these ranges and needn't reach their ends.
Inputs may be any that keep to these rules, and one draw needn't show every extreme that they name: `tokens`: the block's input. `document_ids`: within each sequence the numbers never fall, start at 0 and end at 3 (a document may be empty). In every 2 consecutive sequences one document starts in the first 512 positions and ends in the last 512.
All inputs are finite; a program needn't handle non-finite values.
Results may differ from the reference program's by a relative error of at most 0.02.
Values may be sent and summed in bfloat16 or wider, within the bound.
No kernel may reach another device: no remote copies, remote signals or barrier semaphores. Data moves between devices by JAX's collectives and lax.ppermute only.
A program may use at most 384 MiB of HBM per device.

```python
import math
import jax
import jax.numpy as jnp
from jax import lax

D = 1024
QUERY_HEADS = 16
KEY_VALUE_HEADS = 8
HEAD_DIMENSION = 64
FF = 4608
SEQS = 2
SEQ_LEN = 4096
QKV = 2048
SEQ_DEV = 512
NSEQ = 8


def draw_tokens(key, part):
    first_key = jax.random.fold_in(key, 0)
    fraction = jnp.arange(SEQ_LEN, dtype=jnp.float32) / (SEQ_LEN - 1)
    envelope = 0.4 + 2.0 * fraction
    values = jax.random.truncated_normal(first_key, -4.0, 4.0, (NSEQ, SEQ_LEN, D), jnp.float32)
    return (values * envelope[None, :, None]).astype(jnp.bfloat16)


def draw_document_ids(key, part):
    subkeys = jax.random.split(key, 4)
    spread_cuts = jax.random.randint(subkeys[0], (NSEQ, 3), 1, SEQ_LEN)
    early_cuts = jax.random.randint(subkeys[1], (NSEQ, 2), 1, SEQ_DEV)
    late_cut = jax.random.randint(subkeys[2], (NSEQ, 1), SEQ_LEN - SEQ_DEV + 1, SEQ_LEN)
    spanning = jnp.concatenate([early_cuts, late_cut], axis=1)
    chosen_row = jax.random.randint(subkeys[3], (NSEQ // SEQS,), 0, SEQS)
    row_index = jnp.arange(NSEQ, dtype=jnp.int32)
    special = row_index % SEQS == chosen_row[row_index // SEQS]
    boundary = jnp.where(special[:, None], spanning, spread_cuts)
    position = jnp.arange(SEQ_LEN, dtype=jnp.int32)
    return jnp.sum((position[None, :, None] >= boundary[:, None, :]).astype(jnp.int32), axis=2)


def raised(drawn, stream_key, source, target, shards_of, factor):
    def block_of(dim):
        return (jnp.arange(drawn.shape[dim]) // (drawn.shape[dim] // shards_of)).reshape((-1,) + (1,) * (drawn.ndim - 1 - dim))

    near = jax.random.permutation(stream_key, shards_of)[block_of(target)]
    other_side = (block_of(target) + shards_of // 2) % shards_of
    return jnp.where((block_of(source) == near) | (block_of(source) == other_side), factor * drawn, drawn)


def steps_of(own_key, extent, pieces, low, largest):
    def one(dim, shards_of):
        heights = jax.random.uniform(jax.random.fold_in(jax.random.fold_in(own_key, 6), dim), (shards_of,), jnp.float32, low / len(pieces), largest / len(pieces))
        return jnp.repeat(jnp.exp(heights), extent[dim] // shards_of).reshape((-1,) + (1,) * (len(extent) - dim - 1))

    factor_of = one(*pieces[0])
    for cut in pieces[1:]:
        factor_of = factor_of * one(*cut)
    return factor_of


def centred(key, shape, scale, bound, cuts=(), kind=jnp.bfloat16):
    values = jax.random.normal(key, shape, jnp.float32) * scale
    if len(cuts) > 0:
        values = steps_of(key, shape, cuts, -0.22, 0.18) * values
    return jnp.clip(values, min=-bound, max=bound).astype(kind)


def gaussian_with(stream_key, extent, spread, limit, shards, heavy, held_as=jnp.bfloat16):
    array = spread * jax.random.normal(stream_key, extent, jnp.float32)
    if shards:
        array = array * steps_of(stream_key, extent, shards, -0.22, 0.18)
    return jnp.clip(raised(array, jax.random.fold_in(stream_key, 3), *heavy), -limit, limit).astype(held_as)


def setup_inputs(seed: int = 0) -> dict:
    key_of = jax.random.split(jax.random.key(seed), 11)
    return {
        "tokens": draw_tokens(jax.random.fold_in(key_of[10], 71), 0),
        "document_ids": draw_document_ids(jax.random.fold_in(key_of[10], 71), 0),
        "mixer_weight": centred(key_of[2], (D, QKV), D ** -0.5, 0.1875, ((0, 32),)),
        "output_weight": centred(key_of[3], (QUERY_HEADS * HEAD_DIMENSION, D), 4 ** -0.5, 3.0, ((0, 32),)),
        "mixer_gain": jnp.clip(1.0 + 0.1 * jax.random.normal(key_of[4], (D,), jnp.float32), 0.5, 1.5).astype(jnp.bfloat16),
        "expand_weight": centred(key_of[5], (D, 2 * FF), D ** -0.5, 0.1875, ((0, 32),)),
        "shrink_weight": centred(key_of[6], (FF, D), FF ** -0.5, 0.09375, ((0, 32),)),
        "feed_gain": jnp.clip(1.0 + 0.1 * jax.random.normal(key_of[7], (D,), jnp.float32), 0.5, 1.5).astype(jnp.bfloat16),
        "head_gains": jnp.clip(1.0 + 0.1 * jax.random.normal(key_of[8], (2, HEAD_DIMENSION), jnp.float32), 0.5, 1.5),
        "cotangent": gaussian_with(key_of[9], (NSEQ, SEQ_LEN, D), 1.0, 6.0, ((0, 4), (1, 8)), (1, 2, 8, 2.0)),
    }


epsilon = 1e-05
rope_base = 1000000.0
masked_score = -1e+30
highest = lax.Precision.HIGHEST

@jax.custom_vjp
def low(v):
    return lax.optimization_barrier(v.astype(jnp.bfloat16)).astype(jnp.float32)

@jax.custom_vjp
def low_back(v):
    return v

def low_keep(v):
    return (low(v), None)

def low_pass(kept, grad):
    return (grad,)

def back_keep(v):
    return (v, None)

def back_low(kept, grad):
    return (low(grad),)
low.defvjp(low_keep, low_pass)
low_back.defvjp(back_keep, back_low)

def normalize_rows(values):
    return values * lax.rsqrt(lax.optimization_barrier(jnp.mean(values * values, axis=-1, keepdims=True)) + epsilon)

def rotary_tables(positions, head_size):
    halfway = head_size // 2
    inverse = rope_base ** (-(jnp.arange(halfway, dtype=jnp.float32) * 2.0 / head_size))
    angles = positions.astype(jnp.float32)[..., None] * inverse
    angles = jnp.concatenate([angles, angles], axis=-1)
    return (jnp.cos(angles), jnp.sin(angles))

def rotate(values, cosine_table, sine_table):
    halfway = values.shape[-1] // 2
    turned = jnp.concatenate([-values[..., halfway:], values[..., :halfway]], axis=-1)
    return values * cosine_table + turned * sine_table

def document_positions(document_row):
    sequence_length = document_row.shape[0]
    earlier = lax.optimization_barrier(jnp.sum((document_row[None, :] < document_row[:, None]).astype(jnp.int32), axis=1))
    return jnp.arange(sequence_length, dtype=jnp.int32) - earlier

def attention(query, key, value_matrix, documents):
    sequence_length = query.shape[0]
    query_groups = QUERY_HEADS // KEY_VALUE_HEADS
    block_extent = math.gcd(sequence_length, 512)
    key_heads = key.transpose(1, 0, 2)
    value_heads = value_matrix.transpose(1, 0, 2)
    key_index = jnp.arange(sequence_length, dtype=jnp.int32)

    def one_block(block_start):
        current_query_block = lax.dynamic_slice_in_dim(query, block_start, block_extent, 0)
        current_query_block = current_query_block.reshape(block_extent, KEY_VALUE_HEADS, query_groups, HEAD_DIMENSION).transpose(1, 2, 0, 3)
        scores = jnp.einsum('kgrd,kjd->kgrj', current_query_block, key_heads, precision=highest) * 0.125
        scores = low_back(scores)
        query_index = block_start + jnp.arange(block_extent, dtype=jnp.int32)
        query_docs = lax.dynamic_slice_in_dim(documents, block_start, block_extent, 0)
        allowed = jnp.logical_and(query_docs[:, None] == documents[None, :], query_index[:, None] >= key_index[None, :])
        masked = jnp.where(allowed, scores, masked_score)
        row_max = lax.optimization_barrier(jnp.max(masked, axis=-1, keepdims=True))
        softmax_terms = jnp.where(allowed, jnp.exp(masked - row_max), 0.0)
        probability = low(softmax_terms / lax.optimization_barrier(jnp.sum(softmax_terms, axis=-1, keepdims=True)))
        block_out = jnp.einsum('kgrj,kjd->kgrd', probability, value_heads, precision=highest)
        return block_out.transpose(2, 0, 1, 3).reshape(block_extent, QUERY_HEADS * HEAD_DIMENSION)
    starts = jnp.arange(sequence_length // block_extent, dtype=jnp.int32) * block_extent
    outputs = lax.map(jax.checkpoint(one_block), starts)
    return outputs.reshape(sequence_length, QUERY_HEADS * HEAD_DIMENSION)

def layer(stream, documents, positions, weights):
    mixer_weight, output_weight, mixer_gain, expand_weight, shrink_weight, feed_gain, head_gains = weights
    sequence_length = stream.shape[0]
    query_feature_width = QUERY_HEADS * HEAD_DIMENSION
    key_feature_width = KEY_VALUE_HEADS * HEAD_DIMENSION
    normed_in = low(normalize_rows(stream) * mixer_gain)
    projected_heads = jnp.dot(normed_in, mixer_weight, precision=highest)
    query_raw = low_back(projected_heads[:, :query_feature_width]).reshape(sequence_length, QUERY_HEADS, HEAD_DIMENSION)
    unrotated_key = low_back(projected_heads[:, query_feature_width:query_feature_width + key_feature_width]).reshape(sequence_length, KEY_VALUE_HEADS, HEAD_DIMENSION)
    value_matrix = low(low_back(projected_heads[:, query_feature_width + key_feature_width:])).reshape(sequence_length, KEY_VALUE_HEADS, HEAD_DIMENSION)
    cosine_table, sine_table = rotary_tables(positions, HEAD_DIMENSION)
    cosine_table = cosine_table[:, None, :]
    sine_table = sine_table[:, None, :]
    query = low(rotate(normalize_rows(query_raw) * head_gains[0], cosine_table, sine_table))
    key = low(rotate(normalize_rows(unrotated_key) * head_gains[1], cosine_table, sine_table))
    attended = low(low_back(attention(query, key, value_matrix, documents)))
    attn_branch = low_back(jnp.dot(attended, output_weight, precision=highest))
    middle = stream + attn_branch
    normed_mid = low(normalize_rows(middle) * feed_gain)
    gate_up = jnp.dot(normed_mid, expand_weight, precision=highest)
    gate_rows = low_back(gate_up[:, :FF])
    up_rows = low_back(gate_up[:, FF:])
    hidden = low(jax.nn.silu(gate_rows) * up_rows)
    feed_branch = low_back(jnp.dot(hidden, shrink_weight, precision=highest))
    return (middle + feed_branch, attn_branch, feed_branch)

def reference(tokens, document_ids, mixer_weight, output_weight, mixer_gain, expand_weight, shrink_weight, feed_gain, head_gains, cotangent):
    params = tuple((item.astype(jnp.float32) for item in (mixer_weight, output_weight, mixer_gain, expand_weight, shrink_weight, feed_gain, head_gains)))
    zeros = tuple((jnp.zeros(item.shape, jnp.float32) for item in params))

    def per_sequence(carry, item):
        gradients, squares = carry
        stream, documents, upstream = item
        positions = document_positions(documents)

        def forward(stream_in, *weights):
            layer_out, attn_branch, feed_branch = layer(stream_in, documents, positions, weights)
            return (layer_out, (attn_branch, feed_branch))
        layer_out, pullback, branches = jax.vjp(forward, stream, *params, has_aux=True)
        pulled = pullback(upstream)
        gradients = tuple((total + term for total, term in zip(gradients, pulled[1:])))
        attn_branch, feed_branch = branches
        squares = squares + jnp.stack([jnp.sum(attn_branch * attn_branch), jnp.sum(feed_branch * feed_branch), jnp.sum(layer_out * layer_out)])
        return ((gradients, squares), (layer_out, pulled[0]))
    initial = (zeros, jnp.zeros((3,), jnp.float32))
    (gradients, squares), (layer_outs, input_grads) = lax.scan(per_sequence, initial, (tokens.astype(jnp.float32), document_ids, cotangent.astype(jnp.float32)))
    statistics = jnp.sqrt(squares / (NSEQ * SEQ_LEN * D))
    return (layer_outs.astype(jnp.bfloat16), input_grads.astype(jnp.bfloat16), gradients[0], gradients[1], gradients[2], gradients[3], gradients[4], gradients[5], gradients[6], statistics)
```

```python
import functools
import math

import jax
import jax.numpy as jnp
from jax import lax
from jax.experimental import pallas as pl
from jax.experimental.pallas import tpu as pltpu
from jax.sharding import PartitionSpec as P

QUERY_HEADS = 16
KEY_VALUE_HEADS = 8
HEAD_DIMENSION = 64
FF = 4608

epsilon = 1e-05
rope_base = 1000000.0
masked_score = -1e30
LOG2E = math.log2(math.e)
QUERY_SCALE = 0.125 * LOG2E
MASK = 256.0
VMEM = 60 * 2**20
BF, F32 = jnp.bfloat16, jnp.float32

NN = (((1,), (0,)), ((), ()))
NT = (((1,), (1,)), ((), ()))
TN = (((0,), (0,)), ((), ()))


def dot(a, b, dims=NN):
    return lax.dot_general(a, b, dims, preferred_element_type=F32)


def params(**kw):
    return pltpu.CompilerParams(vmem_limit_bytes=VMEM, **kw)


def cost(flops, nbytes):
    return pl.CostEstimate(flops=int(flops), bytes_accessed=int(nbytes), transcendentals=0)


def project_kernel(x_ref, w_ref, gain_ref, cos_ref, sin_ref, hg_ref, qkv_ref, raw_ref, nx_ref):
    x = x_ref[...].astype(F32)
    r = lax.rsqrt(jnp.mean(x * x, axis=-1, keepdims=True) + epsilon)
    nx = (x * r * gain_ref[...].astype(F32)).astype(BF)
    nx_ref[...] = nx
    nxt = nx.T
    cos, sin = cos_ref[...], sin_ref[...]
    hd, half = HEAD_DIMENSION, HEAD_DIMENSION // 2
    bt = x.shape[0]
    gains = [jnp.broadcast_to(hg_ref[:, j : j + 1], (hd, bt)) for j in (0, 1)]
    for h in range(KEY_VALUE_HEADS):
        p = dot(w_ref[:, h * 256 : (h + 1) * 256], nxt, TN)
        raw_ref[h] = p.astype(BF)
        for slot in range(3):
            v = p[slot * hd : (slot + 1) * hd]
            factor = lax.rsqrt(jnp.mean(v * v, axis=0, keepdims=True) + epsilon)
            u = v * factor * gains[0 if slot < 2 else 1]
            a, b = u[:half], u[half:]
            qkv_ref[h, slot * hd : slot * hd + half, :] = (a * cos - b * sin).astype(BF)
            qkv_ref[h, slot * hd + half : (slot + 1) * hd, :] = (b * cos + a * sin).astype(BF)
        qkv_ref[h, 3 * hd :, :] = p[3 * hd :].astype(BF)


def project(x, w, gain, cos, sin, hg, bt):
    tokens, d = x.shape
    kv = KEY_VALUE_HEADS
    return pl.pallas_call(
        project_kernel,
        grid=(tokens // bt,),
        in_specs=[
            pl.BlockSpec((bt, d), lambda i: (i, 0)),
            pl.BlockSpec((d, kv * 256), lambda i: (0, 0)),
            pl.BlockSpec((1, d), lambda i: (0, 0)),
            pl.BlockSpec((32, bt), lambda i: (0, i)),
            pl.BlockSpec((32, bt), lambda i: (0, i)),
            pl.BlockSpec((64, 2), lambda i: (0, 0)),
        ],
        out_specs=[
            pl.BlockSpec((kv, 256, bt), lambda i: (0, 0, i)),
            pl.BlockSpec((kv, 256, bt), lambda i: (0, 0, i)),
            pl.BlockSpec((bt, d), lambda i: (i, 0)),
        ],
        out_shape=[
            jax.ShapeDtypeStruct((kv, 256, tokens), BF),
            jax.ShapeDtypeStruct((kv, 256, tokens), BF),
            jax.ShapeDtypeStruct((tokens, d), BF),
        ],
        compiler_params=params(),
        cost_estimate=cost(2 * tokens * d * kv * 256, 20e6),
        name="project",
    )(x, w, gain, cos, sin, hg)


def first_start(starts_ref, s, t):
    out = jnp.int32(0)
    for d in range(1, 4):
        b = starts_ref[s * 4 + d]
        out = jnp.where(t >= b, b, out)
    return out


def next_start(starts_ref, s, t, total):
    out = jnp.int32(total)
    for d in range(3, 0, -1):
        b = starts_ref[s * 4 + d]
        out = jnp.where(t < b, b, out)
    return out


def member(starts_ref, s, base, rows, width, total):
    pos = base + lax.broadcasted_iota(jnp.int32, (rows, width), 1)
    row = lax.broadcasted_iota(jnp.int32, (rows, width), 0)
    out = jnp.zeros((rows, width), F32)
    for d in range(4):
        lo = starts_ref[s * 4 + d]
        hi = starts_ref[s * 4 + d + 1] if d < 3 else jnp.int32(total)
        out = jnp.where((row == d) & (pos >= lo) & (pos < hi), 1.0, out)
    return out


def attend_kernel(starts_ref, q_ref, seq_ref, out_ref, lse_ref, kx, vt, acc):
    s, i = pl.program_id(0), pl.program_id(1)
    blocks, _, width = seq_ref.shape
    total = blocks * width

    @pl.when(i == 0)
    def _():
        for j in range(blocks):
            aux = member(starts_ref, s, j * width, 64, width, total)
            kk = jnp.concatenate([seq_ref[j, 128:192, :].astype(F32), aux], axis=0)
            kx[j] = kk.T.astype(BF)
            vt[j, 0:64, :] = seq_ref[j, 192:256, :]
            ones = (lax.broadcasted_iota(jnp.int32, (16, width), 0) == 0).astype(F32)
            vt[j, 64:80, :] = ones.astype(BF)

    aux = ((member(starts_ref, s, i * width, 64, width, total) - 1.0) * MASK).astype(BF)
    row = lax.broadcasted_iota(jnp.int32, (64, width), 0)
    aux = jnp.where(row < 4, aux.astype(F32), 0.0).astype(BF)
    q = [jnp.concatenate([q_ref[0, g * 64 : g * 64 + 64, :], aux], axis=0) for g in (0, 1)]
    acc[...] = jnp.zeros_like(acc)

    def block(j, diagonal):
        k, v = kx[j], vt[j]
        sc = [dot(k, q[g]) for g in (0, 1)]
        if diagonal:
            keep = lax.broadcasted_iota(jnp.int32, (width, width), 0) <= lax.broadcasted_iota(
                jnp.int32, (width, width), 1
            )
            sc = [jnp.where(keep, x, -MASK) for x in sc]
        p = [jnp.exp2(x).astype(BF) for x in sc]
        for g in (0, 1):
            acc[g] += dot(v, p[g])

    lo = first_start(starts_ref, s, i * width) // width
    lax.fori_loop(lo, i, lambda j, c: (block(j, False), c)[1], 0)
    block(i, True)
    for g in (0, 1):
        a = acc[g]
        total_weight = a[64:65]
        out_ref[0, g * 64 : g * 64 + 64, :] = (a[0:64] / total_weight).astype(BF)
        lse_ref[0, g : g + 1, :] = jnp.log2(total_weight)
    lse_ref[0, 2:8, :] = jnp.zeros((6, width), F32)


def attend(starts, qkv, seqs):
    blocks, _, rows = qkv.shape
    width = rows // seqs
    return pl.pallas_call(
        attend_kernel,
        grid_spec=pltpu.PrefetchScalarGridSpec(
            num_scalar_prefetch=1,
            grid=(seqs, blocks),
            in_specs=[
                pl.BlockSpec((1, 256, width), lambda s, i, st: (i, 0, s)),
                pl.BlockSpec((blocks, 256, width), lambda s, i, st: (0, 0, s)),
            ],
            out_specs=[
                pl.BlockSpec((1, 128, width), lambda s, i, st: (i, 0, s)),
                pl.BlockSpec((1, 8, width), lambda s, i, st: (i, 0, s)),
            ],
            scratch_shapes=[
                pltpu.VMEM((blocks, width, 128), BF),
                pltpu.VMEM((blocks, 80, width), BF),
                pltpu.VMEM((2, 80, width), F32),
            ],
        ),
        out_shape=[
            jax.ShapeDtypeStruct((blocks, 128, rows), BF),
            jax.ShapeDtypeStruct((blocks, 8, rows), F32),
        ],
        compiler_params=params(),
        cost_estimate=cost(60e9, 8e6),
        name="attend",
    )(starts, qkv, qkv)


def split3(x):
    hi = x.astype(BF).astype(F32)
    mid = (x - hi).astype(BF).astype(F32)
    return hi, mid, x - hi - mid


def attend_back_kernel(
    starts_ref, seq_ref, do_ref, o_ref, lse_ref, out_ref, kx, vx, kt, qx, dox, dq, dk, dv
):
    s, j = pl.program_id(0), pl.program_id(1)
    blocks, _, width = seq_ref.shape
    total = blocks * width

    @pl.when(j == 0)
    def _():
        row = lax.broadcasted_iota(jnp.int32, (64, width), 0)
        minus = jnp.where((row >= 4) & (row < 7), -1.0, 0.0)
        for b in range(blocks):
            mem = member(starts_ref, s, b * width, 64, width, total)
            aux = mem + minus
            kk = jnp.concatenate([seq_ref[b, 128:192, :].astype(F32), aux], axis=0)
            kx[b] = kk.T.astype(BF)
            vv = jnp.concatenate([seq_ref[b, 192:256, :].astype(F32), minus], axis=0)
            vx[b] = vv.T.astype(BF)
            qmask = jnp.where(row < 4, (mem - 1.0) * MASK, 0.0)
            for g in (0, 1):
                h1, h2, h3 = split3(lse_ref[b, g : g + 1, :])
                ax = jnp.where(row == 4, h1, jnp.where(row == 5, h2, jnp.where(row == 6, h3, qmask)))
                qx[b, g, 0:64, :] = seq_ref[b, g * 64 : g * 64 + 64, :]
                qx[b, g, 64:128, :] = ax.astype(BF)
                d_out = do_ref[b, g * 64 : g * 64 + 64, :]
                out = o_ref[b, g * 64 : g * 64 + 64, :]
                delta = jnp.sum(d_out.astype(F32) * out.astype(F32), axis=0, keepdims=True)
                h1, h2, h3 = split3(delta)
                ax = jnp.where(row == 4, h1, jnp.where(row == 5, h2, jnp.where(row == 6, h3, 0.0)))
                dox[b, g, 0:64, :] = d_out
                dox[b, g, 64:128, :] = ax.astype(BF)
        dq[...] = jnp.zeros_like(dq)

    dk[...] = jnp.zeros_like(dk)
    dv[...] = jnp.zeros_like(dv)
    k, v, ktr = kx[j], vx[j], seq_ref[j, 128:192, :]

    def block(i, diagonal):
        sc = [dot(k, qx[i, g]) for g in (0, 1)]
        dp = [dot(v, dox[i, g]) for g in (0, 1)]
        if diagonal:
            keep = lax.broadcasted_iota(jnp.int32, (width, width), 0) <= lax.broadcasted_iota(
                jnp.int32, (width, width), 1
            )
            sc = [jnp.where(keep, x, -MASK) for x in sc]
        p = [jnp.exp2(x) for x in sc]
        ds = [(p[g] * dp[g]).astype(BF) for g in (0, 1)]
        pb = [x.astype(BF) for x in p]
        for g in (0, 1):
            dv[...] += dot(dox[i, g, 0:64, :], pb[g], NT)
            dk[...] += dot(qx[i, g, 0:64, :], ds[g], NT)
            dq[i, g] += dot(ktr, ds[g])

    block(j, True)
    hi = (next_start(starts_ref, s, j * width + width - 1, total) - 1) // width
    lax.fori_loop(j + 1, hi + 1, lambda i, c: (block(i, False), c)[1], 0)
    out_ref[j, 128:192, :] = (dk[...] * (0.125 / QUERY_SCALE)).astype(BF)
    out_ref[j, 192:256, :] = dv[...].astype(BF)

    @pl.when(j == blocks - 1)
    def _():
        for b in range(blocks):
            for g in (0, 1):
                out_ref[b, g * 64 : g * 64 + 64, :] = (dq[b, g] * 0.125).astype(BF)


def attend_back(starts, qkv, d_out, out, lse, seqs):
    blocks, _, rows = qkv.shape
    width = rows // seqs
    whole = lambda n: pl.BlockSpec((blocks, n, width), lambda s, j, st: (0, 0, s))
    return pl.pallas_call(
        attend_back_kernel,
        grid_spec=pltpu.PrefetchScalarGridSpec(
            num_scalar_prefetch=1,
            grid=(seqs, blocks),
            in_specs=[whole(256), whole(128), whole(128), whole(8)],
            out_specs=whole(256),
            scratch_shapes=[
                pltpu.VMEM((blocks, width, 128), BF),
                pltpu.VMEM((blocks, width, 128), BF),
                pltpu.VMEM((8, 128), BF),
                pltpu.VMEM((blocks, 2, 128, width), BF),
                pltpu.VMEM((blocks, 2, 128, width), BF),
                pltpu.VMEM((blocks, 2, 64, width), F32),
                pltpu.VMEM((64, width), F32),
                pltpu.VMEM((64, width), F32),
            ],
        ),
        out_shape=jax.ShapeDtypeStruct((blocks, 256, rows), BF),
        compiler_params=params(),
        cost_estimate=cost(140e9, 12e6),
        name="attend_back",
    )(starts, qkv, d_out, out, lse)


def middle_kernel(x_ref, at_ref, w_ref, gain_ref, mid_ref, nm_ref, sq_ref):
    i = pl.program_id(0)
    heads, n, bt = at_ref.shape
    branch = dot(at_ref[...].reshape(heads * n, bt), w_ref[...], TN)
    mid = x_ref[...].astype(F32) + branch
    mid_ref[...] = mid
    r = lax.rsqrt(jnp.mean(mid * mid, axis=-1, keepdims=True) + epsilon)
    nm_ref[...] = (mid * r * gain_ref[...].astype(F32)).astype(BF)

    @pl.when(i == 0)
    def _():
        sq_ref[...] = jnp.zeros_like(sq_ref)

    sq_ref[0:1, :] += jnp.sum(branch * branch, axis=0, keepdims=True)


def middle(x, at, w, gain, bt):
    tokens, d = x.shape
    heads, n, _ = at.shape
    rows = pl.BlockSpec((bt, d), lambda i: (i, 0))
    return pl.pallas_call(
        middle_kernel,
        grid=(tokens // bt,),
        in_specs=[
            rows,
            pl.BlockSpec((heads, n, bt), lambda i: (0, 0, i)),
            pl.BlockSpec((heads * n, d), lambda i: (0, 0)),
            pl.BlockSpec((1, d), lambda i: (0, 0)),
        ],
        out_specs=[rows, rows, pl.BlockSpec((8, d), lambda i: (0, 0))],
        out_shape=[
            jax.ShapeDtypeStruct((tokens, d), F32),
            jax.ShapeDtypeStruct((tokens, d), BF),
            jax.ShapeDtypeStruct((8, d), F32),
        ],
        compiler_params=params(),
        cost_estimate=cost(2 * tokens * d * heads * n, 14e6),
        name="middle",
    )(x, at, w, gain)


def feed_kernel(nm_ref, c_ref, wg_ref, wu_ref, ws_ref, fb_ref, dn_ref, gg_ref, gu_ref, gs_ref, nmt):
    f = pl.program_id(0)

    @pl.when(f == 0)
    def _():
        fb_ref[...] = jnp.zeros_like(fb_ref)
        dn_ref[...] = jnp.zeros_like(dn_ref)
        nmt[...] = nm_ref[...].T

    nm, c = nm_ref[...], c_ref[...]
    wg, wu, ws = wg_ref[...], wu_ref[...], ws_ref[...]
    gate, up = dot(nm, wg), dot(nm, wu)
    dh = dot(c, ws, NT)
    sig = 0.5 * jnp.tanh(0.5 * gate) + 0.5
    silu = gate * sig
    hidden = (silu * up).astype(BF)
    dg = (dh * up * sig * (1.0 + gate * (1.0 - sig))).astype(BF)
    du = (dh * silu).astype(BF)
    fb_ref[...] += dot(hidden, ws)
    gs_ref[...] = dot(hidden, c, TN).astype(BF)
    gg_ref[...] = dot(nmt[...], dg).astype(BF)
    gu_ref[...] = dot(nmt[...], du).astype(BF)
    dn_ref[...] += dot(dg, wg, NT) + dot(du, wu, NT)


def feed(nm, c, we, ws, bf):
    tokens, d = nm.shape
    ff = ws.shape[0]
    n = ff // bf
    whole = pl.BlockSpec((tokens, d), lambda f: (0, 0))
    return pl.pallas_call(
        feed_kernel,
        grid=(n,),
        in_specs=[
            whole,
            whole,
            pl.BlockSpec((d, bf), lambda f: (0, f)),
            pl.BlockSpec((d, bf), lambda f: (0, f + n)),
            pl.BlockSpec((bf, d), lambda f: (f, 0)),
        ],
        out_specs=[
            whole,
            whole,
            pl.BlockSpec((d, bf), lambda f: (0, f)),
            pl.BlockSpec((d, bf), lambda f: (0, f)),
            pl.BlockSpec((bf, d), lambda f: (f, 0)),
        ],
        out_shape=[
            jax.ShapeDtypeStruct((tokens, d), F32),
            jax.ShapeDtypeStruct((tokens, d), F32),
            jax.ShapeDtypeStruct((d, ff), BF),
            jax.ShapeDtypeStruct((d, ff), BF),
            jax.ShapeDtypeStruct((ff, d), BF),
        ],
        scratch_shapes=[pltpu.VMEM((d, tokens), BF)],
        compiler_params=params(),
        cost_estimate=cost(18 * tokens * d * ff, 70e6),
        name="feed",
    )(nm, c, we, we, ws)


def turn_kernel(
    mid_ref, fb_ref, dn_ref, c_ref, at_ref, w_ref, gain_ref,
    res_ref, dmid_ref, da_ref, go_ref, sums_ref, acc,
):
    i = pl.program_id(0)
    heads, n, bt = at_ref.shape
    mid, fb, dn = mid_ref[...], fb_ref[...], dn_ref[...]
    out = mid + fb
    res_ref[...] = out.astype(BF)
    r = lax.rsqrt(jnp.mean(mid * mid, axis=-1, keepdims=True) + epsilon)
    unit = mid * r
    g = dn * gain_ref[...].astype(F32)
    dmid = c_ref[...].astype(F32) + r * (g - unit * jnp.mean(g * unit, axis=-1, keepdims=True))
    dmid_ref[...] = dmid
    low = dmid.astype(BF)
    w = w_ref[...]
    da_ref[...] = dot(w, low, NT).astype(BF).reshape(heads, n, bt)

    @pl.when(i == 0)
    def _():
        sums_ref[...] = jnp.zeros_like(sums_ref)
        acc[...] = jnp.zeros_like(acc)

    acc[...] += dot(at_ref[...].reshape(heads * n, bt), low)
    sums_ref[0:1, :] += jnp.sum(dn * unit, axis=0, keepdims=True)
    sums_ref[1:2, :] += jnp.sum(fb * fb, axis=0, keepdims=True)
    sums_ref[2:3, :] += jnp.sum(out * out, axis=0, keepdims=True)

    @pl.when(i == pl.num_programs(0) - 1)
    def _():
        go_ref[...] = acc[...].astype(BF)


def turn(mid, fb, dn, c, at, w, gain, bt):
    tokens, d = mid.shape
    heads, n, _ = at.shape
    rows = pl.BlockSpec((bt, d), lambda i: (i, 0))
    fixed = lambda a, b: pl.BlockSpec((a, b), lambda i: (0, 0))
    heads_block = pl.BlockSpec((heads, n, bt), lambda i: (0, 0, i))
    return pl.pallas_call(
        turn_kernel,
        grid=(tokens // bt,),
        in_specs=[rows, rows, rows, rows, heads_block, fixed(heads * n, d), fixed(1, d)],
        out_specs=[rows, rows, heads_block, fixed(heads * n, d), fixed(8, d)],
        out_shape=[
            jax.ShapeDtypeStruct((tokens, d), BF),
            jax.ShapeDtypeStruct((tokens, d), F32),
            jax.ShapeDtypeStruct((heads, n, tokens), BF),
            jax.ShapeDtypeStruct((heads * n, d), BF),
            jax.ShapeDtypeStruct((8, d), F32),
        ],
        scratch_shapes=[pltpu.VMEM((heads * n, d), F32)],
        compiler_params=params(),
        cost_estimate=cost(4 * tokens * d * heads * n, 30e6),
        name="turn",
    )(mid, fb, dn, c, at, w, gain)


def project_back_kernel(
    dqkv_ref, raw_ref, cos_ref, sin_ref, hg_ref, nx_ref, x_ref, dmid_ref, w_ref, gain_ref,
    dx_ref, gw_ref, gain_sum_ref, head_ref, dproj, acc,
):
    i = pl.program_id(0)
    bt = x_ref.shape[0]
    hd, half = HEAD_DIMENSION, HEAD_DIMENSION // 2
    cos, sin = cos_ref[...], sin_ref[...]
    gains = [jnp.broadcast_to(hg_ref[:, j : j + 1], (hd, bt)) for j in (0, 1)]

    @pl.when(i == 0)
    def _():
        gain_sum_ref[...] = jnp.zeros_like(gain_sum_ref)
        head_ref[...] = jnp.zeros_like(head_ref)
        acc[...] = jnp.zeros_like(acc)

    head_sums = [jnp.zeros((hd, bt), F32), jnp.zeros((hd, bt), F32)]
    for h in range(KEY_VALUE_HEADS):
        parts = []
        for slot in range(3):
            kind = 0 if slot < 2 else 1
            g = dqkv_ref[h, slot * hd : (slot + 1) * hd, :].astype(F32)
            v = raw_ref[h, slot * hd : (slot + 1) * hd, :].astype(F32)
            a, b = g[:half], g[half:]
            pre = jnp.concatenate([a * cos + b * sin, b * cos - a * sin], axis=0)
            factor = lax.rsqrt(jnp.mean(v * v, axis=0, keepdims=True) + epsilon)
            unit = v * factor
            head_sums[kind] += pre * unit
            pre = pre * gains[kind]
            back = factor * (pre - unit * jnp.mean(pre * unit, axis=0, keepdims=True))
            parts.append(back)
        parts.append(dqkv_ref[h, 3 * hd :, :].astype(F32))
        dproj[:, h * 256 : (h + 1) * 256] = jnp.concatenate(parts, axis=0).T.astype(BF)
    for kind in (0, 1):
        head_ref[kind] += jnp.broadcast_to(jnp.sum(head_sums[kind], axis=1, keepdims=True), (hd, 128))
    dp = dproj[...]
    acc[...] += dot(nx_ref[...], dp, TN)
    dn = dot(dp, w_ref[...], NT)
    x = x_ref[...].astype(F32)
    r = lax.rsqrt(jnp.mean(x * x, axis=-1, keepdims=True) + epsilon)
    unit = x * r
    gain_sum_ref[0:1, :] += jnp.sum(dn * unit, axis=0, keepdims=True)
    g = dn * gain_ref[...].astype(F32)
    dx = dmid_ref[...] + r * (g - unit * jnp.mean(g * unit, axis=-1, keepdims=True))
    dx_ref[...] = dx.astype(BF)

    @pl.when(i == pl.num_programs(0) - 1)
    def _():
        gw_ref[...] = acc[...].astype(BF)


def project_back(dqkv, raw, cos, sin, hg, nx, x, dmid, w, gain, bt):
    tokens, d = x.shape
    kv = KEY_VALUE_HEADS
    rows = pl.BlockSpec((bt, d), lambda i: (i, 0))
    fixed = lambda a, b: pl.BlockSpec((a, b), lambda i: (0, 0))
    heads_block = pl.BlockSpec((kv, 256, bt), lambda i: (0, 0, i))
    lanes = pl.BlockSpec((32, bt), lambda i: (0, i))
    return pl.pallas_call(
        project_back_kernel,
        grid=(tokens // bt,),
        in_specs=[heads_block, heads_block, lanes, lanes, fixed(64, 2), rows, rows, rows, fixed(d, kv * 256), fixed(1, d)],
        out_specs=[rows, fixed(d, kv * 256), fixed(8, d), pl.BlockSpec((2, 64, 128), lambda i: (0, 0, 0))],
        out_shape=[
            jax.ShapeDtypeStruct((tokens, d), BF),
            jax.ShapeDtypeStruct((d, kv * 256), BF),
            jax.ShapeDtypeStruct((8, d), F32),
            jax.ShapeDtypeStruct((2, 64, 128), F32),
        ],
        scratch_shapes=[pltpu.VMEM((bt, kv * 256), BF), pltpu.VMEM((d, kv * 256), F32)],
        compiler_params=params(),
        cost_estimate=cost(4 * tokens * d * kv * 256, 30e6),
        name="project_back",
    )(dqkv, raw, cos, sin, hg, nx, x, dmid, w, gain)


def heads_together(w):
    rows = w.shape[0]
    kv, hd = KEY_VALUE_HEADS, HEAD_DIMENSION
    q = w[:, : 2 * kv * hd].reshape(rows, kv, 2 * hd)
    k = w[:, 2 * kv * hd : 3 * kv * hd].reshape(rows, kv, hd)
    v = w[:, 3 * kv * hd :].reshape(rows, kv, hd)
    return jnp.concatenate([q, k, v], axis=2).reshape(rows, 4 * kv * hd)


def heads_apart(w):
    rows = w.shape[0]
    kv, hd = KEY_VALUE_HEADS, HEAD_DIMENSION
    w = w.reshape(rows, kv, 4 * hd)
    return jnp.concatenate(
        [
            w[:, :, : 2 * hd].reshape(rows, -1),
            w[:, :, 2 * hd : 3 * hd].reshape(rows, -1),
            w[:, :, 3 * hd :].reshape(rows, -1),
        ],
        axis=1,
    )


def heads_per_device(
    tokens, document_ids, mixer_weight, output_weight, mixer_gain, expand_weight, shrink_weight,
    feed_gain, head_gains, cotangent,
):
    seqs, rows, d = tokens.shape
    count = seqs * rows
    both = ("ctx", "fsdp")
    cycle_index = lax.axis_index("ctx")
    device_count = lax.axis_size("ctx") * lax.axis_size("fsdp")
    slot = lax.axis_index(both)
    gain_rows = mixer_gain.shape[0]
    gather = lambda a: lax.all_gather(a, both, axis=0, tiled=True)
    swap = lambda a: lax.all_to_all(a, "ctx", 0, 0)
    reduce = lambda a: lax.psum_scatter(a, both, scatter_dimension=0, tiled=True).astype(F32)

    below = jnp.sum(document_ids[:, None, :] < jnp.arange(4, dtype=jnp.int32)[None, :, None], axis=2)
    starts = jnp.sum(lax.all_gather(below.astype(jnp.int32), "ctx", axis=0), axis=0)
    earlier = jnp.zeros_like(document_ids)
    for n in range(1, 4):
        earlier = jnp.where(document_ids == n, starts[:, n][:, None], earlier)
    positions = cycle_index * rows + jnp.arange(rows, dtype=jnp.int32)[None, :] - earlier
    half = HEAD_DIMENSION // 2
    inverse = rope_base ** (-(jnp.arange(half, dtype=F32) * 2.0 / HEAD_DIMENSION))
    angles = inverse[:, None] * positions.reshape(1, count).astype(F32)
    cos, sin = jnp.cos(angles), jnp.sin(angles)
    starts = starts.reshape(-1)

    gains_all = gather(jnp.stack([mixer_gain, feed_gain], axis=1)).T.reshape(2, 1, d)
    mixer_all = gather(heads_together(mixer_weight))
    output_all = gather(output_weight)
    hg_forward = jnp.stack([head_gains[0] * QUERY_SCALE, head_gains[1]], axis=1)

    x = tokens.reshape(count, d)
    c = cotangent.reshape(count, d)
    qkv, raw, nx = project(x, mixer_all, gains_all[0], cos, sin, hg_forward, 512)
    qkv_heads = swap(qkv)
    expand_all = gather(expand_weight)
    shrink_all = gather(shrink_weight)
    out_heads, lse = attend(starts, qkv_heads, seqs)
    attended = swap(out_heads)
    mid, nm, squares = middle(x, attended, output_all, gains_all[1], 256)
    fb, dn, gg, gu, gs = feed(nm, c, expand_all, shrink_all, 512)
    shrink_gradient = reduce(gs)
    expand_gradient = jnp.concatenate([reduce(gg), reduce(gu)], axis=1)
    result, dmid, d_attended, go, sums = turn(mid, fb, dn, c, attended, output_all, gains_all[1], 256)
    d_out_heads = swap(d_attended)
    output_gradient = reduce(go)
    dqkv_heads = attend_back(starts, qkv_heads, d_out_heads, out_heads, lse, seqs)
    dqkv = swap(dqkv_heads)
    dx, gw, gain_sums, head_sums = project_back(
        dqkv, raw, cos, sin, head_gains.T, nx, x, dmid, mixer_all, gains_all[0], 512
    )
    mixer_gradient = heads_apart(reduce(gw))
    totals = jnp.stack([jnp.sum(squares[0]), jnp.sum(sums[1]), jnp.sum(sums[2])])
    totals, feed_total, mixer_total, head_total = lax.psum(
        (totals, sums[0], gain_sums[0], head_sums[:, :, 0]), both
    )
    own = lambda a: lax.dynamic_slice_in_dim(a, slot * gain_rows, gain_rows, 0)
    statistics = jnp.sqrt(totals / (device_count * count * d))
    return (
        result.reshape(seqs, rows, d),
        dx.reshape(seqs, rows, d),
        mixer_gradient,
        output_gradient,
        own(mixer_total),
        expand_gradient,
        shrink_gradient,
        own(feed_total),
        head_total,
        statistics,
    )


def passed_along(block, axis, distance):
    devices = range(lax.axis_size(axis))
    route = [((i - distance) % len(devices), i) for i in devices]
    return lax.ppermute(block, axis, route)


def normalize_rows(values):
    factor = lax.rsqrt(jnp.mean(values * values, axis=-1, keepdims=True) + epsilon)
    return (values * factor, factor)


def normalize_back(values, factor, upstream):
    inner_mean = jnp.mean(upstream * values, axis=-1, keepdims=True)
    return factor * upstream - values * (factor * factor * factor) * inner_mean


def rotary_tables(positions, head_size):
    halfway = head_size // 2
    inverse = rope_base ** (-(jnp.arange(halfway, dtype=jnp.float32) * 2.0 / head_size))
    angles = positions.astype(jnp.float32)[..., None] * inverse
    angles = jnp.concatenate([angles, angles], axis=-1)
    return (jnp.cos(angles), jnp.sin(angles))


def rotate(values, cosine_table, sine_table):
    halfway = values.shape[-1] // 2
    turned = jnp.concatenate([-values[..., halfway:], values[..., :halfway]], axis=-1)
    return values * cosine_table + turned * sine_table


def rotate_back(upstream, cosine_table, sine_table):
    halfway = upstream.shape[-1] // 2
    scaled = upstream * sine_table
    turned = jnp.concatenate([scaled[..., halfway:], -scaled[..., :halfway]], axis=-1)
    return upstream * cosine_table + turned


def document_positions(own_documents, all_documents, offset_rows):
    earlier = jnp.sum(
        (all_documents[:, None, :] < own_documents[:, :, None]).astype(jnp.int32), axis=2
    )
    index_rows = offset_rows + jnp.arange(own_documents.shape[1], dtype=jnp.int32)
    return index_rows[None, :] - earlier


def allowed_pairs(query_docs, key_docs, query_index, key_index):
    same_document = query_docs[:, :, None] == key_docs[:, None, :]
    causal = query_index[:, None] >= key_index[None, :]
    return jnp.logical_and(same_document, causal[None, :, :])[:, None, None, :, :]


def column_product(left, right):
    return jnp.einsum("nd,nf->df", left, right, preferred_element_type=jnp.float32)


def per_device(
    tokens,
    document_ids,
    mixer_weight,
    output_weight,
    mixer_gain,
    expand_weight,
    shrink_weight,
    feed_gain,
    head_gains,
    cotangent,
):
    sequence_count, sequence_rows, model_width = tokens.shape
    count_of_tokens = sequence_count * sequence_rows
    query_groups = QUERY_HEADS // KEY_VALUE_HEADS
    query_feature_width = QUERY_HEADS * HEAD_DIMENSION
    key_feature_width = KEY_VALUE_HEADS * HEAD_DIMENSION
    cycle_size = lax.axis_size("ctx")
    cycle_index = lax.axis_index("ctx")
    device_count = lax.axis_size("ctx") * lax.axis_size("fsdp")
    owner_slot = lax.axis_index(("ctx", "fsdp"))
    gain_rows = mixer_gain.shape[0]
    offset_rows = cycle_index * sequence_rows
    all_documents = lax.all_gather(document_ids, "ctx", axis=1, tiled=True)
    positions = document_positions(document_ids, all_documents, offset_rows)
    cosine_table, sine_table = rotary_tables(positions.reshape(count_of_tokens), HEAD_DIMENSION)
    cosine_table = cosine_table[:, None, :]
    sine_table = sine_table[:, None, :]
    query_index = offset_rows + jnp.arange(sequence_rows, dtype=jnp.int32)
    mixer_all, output_all, mixer_gain_all = (
        lax.all_gather(mixer_weight, ("ctx", "fsdp"), axis=0, tiled=True),
        lax.all_gather(output_weight, ("ctx", "fsdp"), axis=0, tiled=True),
        lax.all_gather(mixer_gain, ("ctx", "fsdp"), axis=0, tiled=True),
    )
    stream = tokens.reshape(count_of_tokens, model_width).astype(jnp.float32)
    unit_in, factor_in = normalize_rows(stream)
    normed_in = (unit_in * mixer_gain_all.astype(jnp.float32)).astype(jnp.bfloat16)
    projected_heads = jnp.dot(normed_in, mixer_all, preferred_element_type=jnp.float32)
    query_raw = projected_heads[:, :query_feature_width].reshape(
        count_of_tokens, QUERY_HEADS, HEAD_DIMENSION
    )
    unrotated_key = projected_heads[
        :, query_feature_width : query_feature_width + key_feature_width
    ].reshape(count_of_tokens, KEY_VALUE_HEADS, HEAD_DIMENSION)
    value_rows = projected_heads[:, query_feature_width + key_feature_width :].astype(jnp.bfloat16)
    query_unit, query_factor = normalize_rows(query_raw)
    key_unit, key_factor = normalize_rows(unrotated_key)
    query_row_block = rotate(query_unit * head_gains[0], cosine_table, sine_table).astype(
        jnp.bfloat16
    )
    key_rows = rotate(key_unit * head_gains[1], cosine_table, sine_table).astype(jnp.bfloat16)
    query_head_rows = query_row_block.reshape(
        sequence_count, sequence_rows, KEY_VALUE_HEADS, query_groups, HEAD_DIMENSION
    ).transpose(0, 2, 3, 1, 4)
    key_send = key_rows.reshape(sequence_count, sequence_rows, key_feature_width)
    value_send = value_rows.reshape(sequence_count, sequence_rows, key_feature_width)
    statistics_shape = (sequence_count, KEY_VALUE_HEADS, query_groups, sequence_rows)
    initial = (
        jnp.full(statistics_shape, masked_score, jnp.float32),
        jnp.zeros(statistics_shape, jnp.float32),
        jnp.zeros(statistics_shape + (HEAD_DIMENSION,), jnp.float32),
    )
    carried = initial
    key_portion = lax.all_gather(key_send, "ctx", axis=1, tiled=True)
    value_portion = lax.all_gather(value_send, "ctx", axis=1, tiled=True)
    piece_rows = key_portion.shape[1]
    block_extent = math.gcd(piece_rows, 512)
    count_of_blocks = piece_rows // block_extent
    split_key_blocks = jnp.moveaxis(
        key_portion.reshape(
            sequence_count, count_of_blocks, block_extent, KEY_VALUE_HEADS, HEAD_DIMENSION
        ),
        1,
        0,
    )
    value_blocks = jnp.moveaxis(
        value_portion.reshape(
            sequence_count, count_of_blocks, block_extent, KEY_VALUE_HEADS, HEAD_DIMENSION
        ),
        1,
        0,
    )
    block_starts = jnp.arange(count_of_blocks, dtype=jnp.int32) * block_extent

    def one_block(running, block_items):
        current_key_block, current_value_block, block_start = block_items
        row_max, total_weight, weighted_sum = running
        key_docs = lax.dynamic_slice_in_dim(all_documents, block_start, block_extent, 1)
        key_index = block_start + jnp.arange(block_extent, dtype=jnp.int32)
        allowed = allowed_pairs(document_ids, key_docs, query_index, key_index)
        scores = (
            jnp.einsum(
                "skgrd,sjkd->skgrj",
                query_head_rows,
                current_key_block,
                preferred_element_type=jnp.float32,
            )
            * 0.125
        )
        masked = jnp.where(allowed, scores, masked_score)
        new_max = jnp.maximum(row_max, jnp.max(masked, axis=-1))
        rescale = jnp.exp(row_max - new_max)
        softmax_terms = jnp.where(allowed, jnp.exp(masked - new_max[..., None]), 0.0)
        total_weight = total_weight * rescale + jnp.sum(softmax_terms, axis=-1)
        weighted_sum = weighted_sum * rescale[..., None] + jnp.einsum(
            "skgrj,sjkd->skgrd",
            softmax_terms.astype(jnp.bfloat16),
            current_value_block,
            preferred_element_type=jnp.float32,
        )
        return ((new_max, total_weight, weighted_sum), None)

    carried, _ = lax.scan(one_block, carried, (split_key_blocks, value_blocks, block_starts))
    row_max, total_weight, weighted_sum = carried
    attn_heads = weighted_sum / total_weight[..., None]
    log_total = row_max + jnp.log(total_weight)
    attended = attn_heads.transpose(0, 3, 1, 2, 4).reshape(count_of_tokens, query_feature_width)
    attended_low = attended.astype(jnp.bfloat16)
    attn_branch = jnp.dot(attended_low, output_all, preferred_element_type=jnp.float32)
    middle = stream + attn_branch
    expand_all, shrink_all, feed_gain_all = (
        lax.all_gather(expand_weight, ("ctx", "fsdp"), axis=0, tiled=True),
        lax.all_gather(shrink_weight, ("ctx", "fsdp"), axis=0, tiled=True),
        lax.all_gather(feed_gain, ("ctx", "fsdp"), axis=0, tiled=True),
    )
    unit_mid, factor_mid = normalize_rows(middle)
    normed_mid = (unit_mid * feed_gain_all.astype(jnp.float32)).astype(jnp.bfloat16)
    gate_up = jnp.dot(normed_mid, expand_all, preferred_element_type=jnp.float32)
    gate_rows = gate_up[:, :FF]
    up_rows = gate_up[:, FF:]
    gate_sigmoid = jax.nn.sigmoid(gate_rows)
    gate_silu = gate_rows * gate_sigmoid
    hidden = (gate_silu * up_rows).astype(jnp.bfloat16)
    feed_branch = jnp.dot(hidden, shrink_all, preferred_element_type=jnp.float32)
    layer_out = middle + feed_branch
    squares = jnp.stack(
        [
            jnp.sum(attn_branch * attn_branch),
            jnp.sum(feed_branch * feed_branch),
            jnp.sum(layer_out * layer_out),
        ]
    )
    stat_totals = lax.psum(squares, ("ctx", "fsdp"))
    grad_branch = cotangent.reshape(count_of_tokens, model_width)
    grad_result = grad_branch.astype(jnp.float32)
    shrink_gradient = lax.psum_scatter(
        column_product(hidden, grad_branch), ("ctx", "fsdp"), scatter_dimension=0, tiled=True
    )
    grad_hidden = jnp.einsum(
        "nd,fd->nf", grad_branch, shrink_all, preferred_element_type=jnp.float32
    )
    grad_gate = grad_hidden * up_rows * gate_sigmoid * (1.0 + gate_rows * (1.0 - gate_sigmoid))
    grad_up = grad_hidden * gate_silu
    grad_gate_up = jnp.concatenate([grad_gate, grad_up], axis=1).astype(jnp.bfloat16)
    expand_gradient = lax.psum_scatter(
        column_product(normed_mid, grad_gate_up), ("ctx", "fsdp"), scatter_dimension=0, tiled=True
    )
    grad_normed_mid = jnp.einsum(
        "nf,df->nd", grad_gate_up, expand_all, preferred_element_type=jnp.float32
    )
    feed_gain_term = jnp.sum(grad_normed_mid * unit_mid, axis=0)
    grad_middle = grad_result + normalize_back(
        middle, factor_mid, grad_normed_mid * feed_gain_all.astype(jnp.float32)
    )
    grad_attn_low = grad_middle.astype(jnp.bfloat16)
    output_gradient = lax.psum_scatter(
        column_product(attended_low, grad_attn_low),
        ("ctx", "fsdp"),
        scatter_dimension=0,
        tiled=True,
    )
    attended_gradient = jnp.einsum(
        "nd,qd->nq", grad_attn_low, output_all, preferred_element_type=jnp.float32
    ).astype(jnp.bfloat16)
    heads_gradient = attended_gradient.reshape(
        sequence_count, sequence_rows, KEY_VALUE_HEADS, query_groups, HEAD_DIMENSION
    ).transpose(0, 2, 3, 1, 4)
    delta_rows = jnp.sum(heads_gradient.astype(jnp.float32) * attn_heads, axis=-1)
    zero_query = jnp.zeros(query_head_rows.shape, jnp.float32)

    def pair_terms(current_key_block, current_value_block, block_start):
        rows_per_block = current_key_block.shape[1]
        key_reshaped = current_key_block.reshape(
            sequence_count, rows_per_block, KEY_VALUE_HEADS, HEAD_DIMENSION
        )
        value_reshaped = current_value_block.reshape(
            sequence_count, rows_per_block, KEY_VALUE_HEADS, HEAD_DIMENSION
        )
        key_docs = lax.dynamic_slice_in_dim(all_documents, block_start, rows_per_block, 1)
        key_index = block_start + jnp.arange(rows_per_block, dtype=jnp.int32)
        allowed = allowed_pairs(document_ids, key_docs, query_index, key_index)
        scores = (
            jnp.einsum(
                "skgrd,sjkd->skgrj",
                query_head_rows,
                key_reshaped,
                preferred_element_type=jnp.float32,
            )
            * 0.125
        )
        probability = jnp.where(
            allowed, jnp.exp(jnp.where(allowed, scores, 0.0) - log_total[..., None]), 0.0
        )
        value_term = jnp.einsum(
            "skgrj,skgrd->sjkd",
            probability.astype(jnp.bfloat16),
            heads_gradient,
            preferred_element_type=jnp.float32,
        )
        grad_probability = jnp.einsum(
            "skgrd,sjkd->skgrj", heads_gradient, value_reshaped, preferred_element_type=jnp.float32
        )
        grad_scores = (probability * (grad_probability - delta_rows[..., None])).astype(
            jnp.bfloat16
        )
        query_term = (
            jnp.einsum(
                "skgrj,sjkd->skgrd", grad_scores, key_reshaped, preferred_element_type=jnp.float32
            )
            * 0.125
        )
        key_term = (
            jnp.einsum(
                "skgrj,skgrd->sjkd",
                grad_scores,
                query_head_rows,
                preferred_element_type=jnp.float32,
            )
            * 0.125
        )
        return (
            query_term,
            key_term.reshape(sequence_count, rows_per_block, key_feature_width),
            value_term.reshape(sequence_count, rows_per_block, key_feature_width),
        )

    zero_keys = jnp.zeros((sequence_count, sequence_rows, key_feature_width), jnp.float32)

    def cycle_step(cycle_turn, running):
        (
            current_key_block,
            current_value_block,
            key_gradient_accumulator,
            value_accum,
            query_accum,
        ) = running
        owner_index = (cycle_index - cycle_turn) % cycle_size
        query_term, key_term, value_term = pair_terms(
            current_key_block.astype(jnp.bfloat16),
            current_value_block.astype(jnp.bfloat16),
            owner_index * sequence_rows,
        )
        query_accum = query_accum + query_term
        key_gradient_accumulator = key_gradient_accumulator + key_term
        value_accum = value_accum + value_term
        current_key_block, current_value_block, key_gradient_accumulator, value_accum = (
            passed_along(current_key_block.astype(jnp.bfloat16), "ctx", 1).astype(
                current_key_block.dtype
            ),
            passed_along(current_value_block.astype(jnp.bfloat16), "ctx", 1).astype(
                current_value_block.dtype
            ),
            passed_along(key_gradient_accumulator.astype(jnp.bfloat16), "ctx", 1).astype(
                key_gradient_accumulator.dtype
            ),
            passed_along(value_accum.astype(jnp.bfloat16), "ctx", 1).astype(value_accum.dtype),
        )
        return (
            current_key_block,
            current_value_block,
            key_gradient_accumulator,
            value_accum,
            query_accum,
        )

    carried = lax.fori_loop(
        0,
        cycle_size,
        cycle_step,
        (
            key_send.astype(jnp.float32),
            value_send.astype(jnp.float32),
            zero_keys,
            zero_keys,
            zero_query,
        ),
    )
    key_gradient_accumulator, value_accum, query_accum = (carried[2], carried[3], carried[4])
    grad_query = query_accum.transpose(0, 3, 1, 2, 4).reshape(
        count_of_tokens, QUERY_HEADS, HEAD_DIMENSION
    )
    key_grad_total = key_gradient_accumulator.reshape(
        count_of_tokens, KEY_VALUE_HEADS, HEAD_DIMENSION
    )
    grad_value = value_accum.reshape(count_of_tokens, key_feature_width)
    grad_query_pre = rotate_back(grad_query, cosine_table, sine_table)
    grad_key_pre = rotate_back(key_grad_total, cosine_table, sine_table)
    head_terms = jnp.stack(
        [
            jnp.sum(grad_query_pre * query_unit, axis=(0, 1)),
            jnp.sum(grad_key_pre * key_unit, axis=(0, 1)),
        ]
    )
    grad_query_raw = normalize_back(query_raw, query_factor, grad_query_pre * head_gains[0])
    grad_key_raw = normalize_back(unrotated_key, key_factor, grad_key_pre * head_gains[1])
    grad_projected = jnp.concatenate(
        [
            grad_query_raw.reshape(count_of_tokens, query_feature_width),
            grad_key_raw.reshape(count_of_tokens, key_feature_width),
            grad_value,
        ],
        axis=1,
    ).astype(jnp.bfloat16)
    mixer_gradient = lax.psum_scatter(
        column_product(normed_in, grad_projected), ("ctx", "fsdp"), scatter_dimension=0, tiled=True
    )
    grad_normed_in = jnp.einsum(
        "nq,dq->nd", grad_projected, mixer_all, preferred_element_type=jnp.float32
    )
    mixer_gain_term = jnp.sum(grad_normed_in * unit_in, axis=0)
    grad_stream = grad_middle + normalize_back(
        stream, factor_in, grad_normed_in * mixer_gain_all.astype(jnp.float32)
    )
    feed_gain_total, mixer_gain_total, head_total = lax.psum(
        (feed_gain_term, mixer_gain_term, head_terms), ("ctx", "fsdp")
    )
    feed_gain_gradient = lax.dynamic_slice_in_dim(
        feed_gain_total, owner_slot * gain_rows, gain_rows, 0
    )
    mixer_gain_gradient = lax.dynamic_slice_in_dim(
        mixer_gain_total, owner_slot * gain_rows, gain_rows, 0
    )
    statistics = jnp.sqrt(stat_totals / (device_count * count_of_tokens * model_width))
    result = layer_out.astype(jnp.bfloat16).reshape(sequence_count, sequence_rows, model_width)
    tokens_gradient = grad_stream.astype(jnp.bfloat16).reshape(
        sequence_count, sequence_rows, model_width
    )
    return (
        result,
        tokens_gradient,
        mixer_gradient,
        output_gradient,
        mixer_gain_gradient,
        expand_gradient,
        shrink_gradient,
        feed_gain_gradient,
        head_total,
        statistics,
    )


def solution(mesh):
    placed = (
        P("fsdp", "ctx", None),
        P("fsdp", "ctx"),
        P(("ctx", "fsdp"), None),
        P(("ctx", "fsdp"), None),
        P(("ctx", "fsdp")),
        P(("ctx", "fsdp"), None),
        P(("ctx", "fsdp"), None),
        P(("ctx", "fsdp")),
        P(),
        P("fsdp", "ctx", None),
    )
    by_heads = mesh.shape["ctx"] == KEY_VALUE_HEADS
    return jax.shard_map(
        heads_per_device if by_heads else per_device,
        mesh=mesh,
        in_specs=placed,
        out_specs=(
            P("fsdp", "ctx", None),
            P("fsdp", "ctx", None),
            P(("ctx", "fsdp"), None),
            P(("ctx", "fsdp"), None),
            P(("ctx", "fsdp")),
            P(("ctx", "fsdp"), None),
            P(("ctx", "fsdp"), None),
            P(("ctx", "fsdp")),
            P(),
            P(),
        ),
        check_vma=False,
    )
```

```python
import functools
import math

import jax
import jax.numpy as jnp
from jax import lax
from jax.experimental import pallas as pl
from jax.experimental.pallas import tpu as pltpu
from jax.sharding import PartitionSpec as P

QUERY_HEADS = 16
KEY_VALUE_HEADS = 8
HEAD_DIMENSION = 64
FF = 4608

epsilon = 1e-05
rope_base = 1000000.0
masked_score = -1e30
LOG2E = math.log2(math.e)
QUERY_SCALE = 0.125 * LOG2E
MASK = 256.0
VMEM = 60 * 2**20
BF, F32 = jnp.bfloat16, jnp.float32

NN = (((1,), (0,)), ((), ()))
NT = (((1,), (1,)), ((), ()))
TN = (((0,), (0,)), ((), ()))


def dot(a, b, dims=NN):
    return lax.dot_general(a, b, dims, preferred_element_type=F32)


def params(**kw):
    return pltpu.CompilerParams(vmem_limit_bytes=VMEM, **kw)


def cost(flops, nbytes):
    return pl.CostEstimate(flops=int(0.001 * flops), bytes_accessed=int(0.001 * nbytes), transcendentals=0)


def flat(x):
    return x.reshape(-1, x.shape[-1])


def both(mine, other):
    return jnp.concatenate([flat(mine), flat(other)], axis=0)


def order(core, chips):
    return [a * 2 + core for a in range(chips)] + [a * 2 + 1 - core for a in range(chips)]


def lanes(n, width=128):
    return pl.ds(pl.multiple_of(n * width, width), width)


SMALL = pl.BlockSpec(memory_space=pltpu.SMEM)


def fixed(*shape):
    return pl.BlockSpec(shape, lambda *i: (0,) * len(shape), pipeline_mode=pl.Buffered(1))


def halves(w, rows, index, **kw):
    if isinstance(w, tuple):
        block = (*w[0].shape[:2], rows, w[0].shape[-1])
        spec = pl.BlockSpec(block, lambda i, place: (0, 0, index(i), 0), **kw)
        return list(w), [spec, spec]
    block = (w.shape[0], None, w.shape[2], rows, w.shape[-1])
    return [w, w], [
        pl.BlockSpec(block, lambda i, place: (0, place[0], 0, index(i), 0), **kw),
        pl.BlockSpec(block, lambda i, place: (0, 1 - place[0], 0, index(i), 0), **kw),
    ]


def project_kernel(
    place_ref, x_ref, wm_ref, wo_ref, cos_ref, sin_ref, hg_ref, qkv_ref, raw_ref, nx_ref, gains_ref, nxt, grow
):
    core = place_ref[0]
    chips = wm_ref.shape[0]
    kv = KEY_VALUE_HEADS
    wide = kv * 256
    g = both(wm_ref[:, :, :, wide:], wo_ref[:, :, :, wide:]).astype(F32).T[0:8]
    for n, at in enumerate(order(core, chips)):
        grow[:, lanes(at)] = g[:, n * 128 : (n + 1) * 128]
    gains_ref[...] = grow[...]
    x = x_ref[...].astype(F32)
    r = lax.rsqrt(jnp.mean(x * x, axis=-1, keepdims=True) + epsilon)
    nx = (x * r * grow[0:1]).astype(BF)
    nx_ref[...] = nx
    bt = x.shape[0]
    nxt[...] = nx.T.reshape(nxt.shape)
    xt = jnp.concatenate([nxt[at] for at in order(core, chips)], axis=0)
    cos, sin = cos_ref[...], sin_ref[...]
    hd, half = HEAD_DIMENSION, HEAD_DIMENSION // 2
    gains = [jnp.broadcast_to(hg_ref[:, j : j + 1], (hd, bt)) for j in (0, 1)]
    for h in range(kv):
        cols = slice(h * 256, (h + 1) * 256)
        p = dot(both(wm_ref[:, :, :, cols], wo_ref[:, :, :, cols]), xt, TN)
        raw_ref[h] = p.astype(BF)
        for slot in range(3):
            v = p[slot * hd : (slot + 1) * hd]
            factor = lax.rsqrt(jnp.mean(v * v, axis=0, keepdims=True) + epsilon)
            u = v * factor * gains[0 if slot < 2 else 1]
            a, b = u[:half], u[half:]
            qkv_ref[h, slot * hd : slot * hd + half, :] = (a * cos - b * sin).astype(BF)
            qkv_ref[h, slot * hd + half : (slot + 1) * hd, :] = (b * cos + a * sin).astype(BF)
        qkv_ref[h, 3 * hd :, :] = p[3 * hd :].astype(BF)


def project(place, x, mine, other, cos, sin, hg, seq, bt):
    d = x.shape[1]
    kv = KEY_VALUE_HEADS
    turns = pl.BlockSpec((32, bt), lambda i: (0, seq))
    return pl.pallas_call(
        project_kernel,
        grid=(1,),
        in_specs=[
            SMALL,
            pl.BlockSpec((bt, d), lambda i: (seq, 0)),
            fixed(*mine.shape),
            fixed(*mine.shape),
            turns,
            turns,
            fixed(64, 2),
        ],
        out_specs=[fixed(kv, 256, bt), fixed(kv, 256, bt), fixed(bt, d), fixed(8, d)],
        out_shape=[
            jax.ShapeDtypeStruct((kv, 256, bt), BF),
            jax.ShapeDtypeStruct((kv, 256, bt), BF),
            jax.ShapeDtypeStruct((bt, d), BF),
            jax.ShapeDtypeStruct((8, d), F32),
        ],
        scratch_shapes=[pltpu.VMEM((d // 128, 128, bt), BF), pltpu.VMEM((8, d), F32)],
        compiler_params=params(),
        cost_estimate=cost(2 * bt * d * kv * 256, 14e6),
        name="project",
    )(place, x, mine, other, cos, sin, hg)


def first_start(starts_ref, s, t):
    out = jnp.int32(0)
    for d in range(1, 4):
        b = starts_ref[s * 4 + d]
        out = jnp.where(t >= b, b, out)
    return out


def next_start(starts_ref, s, t, total):
    out = jnp.int32(total)
    for d in range(3, 0, -1):
        b = starts_ref[s * 4 + d]
        out = jnp.where(t < b, b, out)
    return out


def member(starts_ref, s, base, rows, width, total):
    pos = base + lax.broadcasted_iota(jnp.int32, (rows, width), 1)
    row = lax.broadcasted_iota(jnp.int32, (rows, width), 0)
    out = jnp.zeros((rows, width), F32)
    for d in range(4):
        lo = starts_ref[s * 4 + d]
        hi = starts_ref[s * 4 + d + 1] if d < 3 else jnp.int32(total)
        out = jnp.where((row == d) & (pos >= lo) & (pos < hi), 1.0, out)
    return out


def attend_kernel(starts_ref, q_ref, seq_ref, out_ref, lse_ref, kx, vt, acc):
    s, i = pl.program_id(0), pl.program_id(1)
    blocks, _, width = seq_ref.shape
    total = blocks * width

    @pl.when(i == 0)
    def _():
        for j in range(blocks):
            aux = member(starts_ref, s, j * width, 64, width, total)
            kk = jnp.concatenate([seq_ref[j, 128:192, :].astype(F32), aux], axis=0)
            kx[j] = kk.T.astype(BF)
            vt[j, 0:64, :] = seq_ref[j, 192:256, :]
            ones = (lax.broadcasted_iota(jnp.int32, (16, width), 0) == 0).astype(F32)
            vt[j, 64:80, :] = ones.astype(BF)

    aux = ((member(starts_ref, s, i * width, 64, width, total) - 1.0) * MASK).astype(BF)
    row = lax.broadcasted_iota(jnp.int32, (64, width), 0)
    aux = jnp.where(row < 4, aux.astype(F32), 0.0).astype(BF)
    q = [jnp.concatenate([q_ref[0, g * 64 : g * 64 + 64, :], aux], axis=0) for g in (0, 1)]
    acc[...] = jnp.zeros_like(acc)

    def block(j, diagonal):
        k, v = kx[j], vt[j]
        sc = [dot(k, q[g]) for g in (0, 1)]
        if diagonal:
            keep = lax.broadcasted_iota(jnp.int32, (width, width), 0) <= lax.broadcasted_iota(
                jnp.int32, (width, width), 1
            )
            sc = [jnp.where(keep, x, -MASK) for x in sc]
        p = [jnp.exp2(x).astype(BF) for x in sc]
        for g in (0, 1):
            acc[g] += dot(v, p[g])

    lo = first_start(starts_ref, s, i * width) // width
    lax.fori_loop(lo, i, lambda j, c: (block(j, False), c)[1], 0)
    block(i, True)
    for g in (0, 1):
        a = acc[g]
        total_weight = a[64:65]
        out_ref[0, g * 64 : g * 64 + 64, :] = (a[0:64] / total_weight).astype(BF)
        lse_ref[0, g : g + 1, :] = jnp.log2(total_weight)
    lse_ref[0, 2:8, :] = jnp.zeros((6, width), F32)


def attend(starts, qkv, seqs=1):
    blocks, _, rows = qkv.shape
    width = rows // seqs
    return pl.pallas_call(
        attend_kernel,
        grid_spec=pltpu.PrefetchScalarGridSpec(
            num_scalar_prefetch=1,
            grid=(seqs, blocks),
            in_specs=[
                pl.BlockSpec((1, 256, width), lambda s, i, st: (i, 0, s)),
                pl.BlockSpec((blocks, 256, width), lambda s, i, st: (0, 0, s)),
            ],
            out_specs=[
                pl.BlockSpec((1, 128, width), lambda s, i, st: (i, 0, s)),
                pl.BlockSpec((1, 8, width), lambda s, i, st: (i, 0, s)),
            ],
            scratch_shapes=[
                pltpu.VMEM((blocks, width, 128), BF),
                pltpu.VMEM((blocks, 80, width), BF),
                pltpu.VMEM((2, 80, width), F32),
            ],
        ),
        out_shape=[
            jax.ShapeDtypeStruct((blocks, 128, rows), BF),
            jax.ShapeDtypeStruct((blocks, 8, rows), F32),
        ],
        compiler_params=params(),
        cost_estimate=cost(30e9, 4e6),
        name="attend",
    )(starts, qkv, qkv)


def split3(x):
    hi = x.astype(BF).astype(F32)
    mid = (x - hi).astype(BF).astype(F32)
    return hi, mid, x - hi - mid


def attend_back_kernel(
    starts_ref, seq_ref, do_ref, o_ref, lse_ref, out_ref, kx, vx, qx, dox, dq, dk, dv
):
    s, j = pl.program_id(0), pl.program_id(1)
    blocks, _, width = seq_ref.shape
    total = blocks * width

    @pl.when(j == 0)
    def _():
        row = lax.broadcasted_iota(jnp.int32, (64, width), 0)
        minus = jnp.where((row >= 4) & (row < 7), -1.0, 0.0)
        for b in range(blocks):
            mem = member(starts_ref, s, b * width, 64, width, total)
            aux = mem + minus
            kk = jnp.concatenate([seq_ref[b, 128:192, :].astype(F32), aux], axis=0)
            kx[b] = kk.T.astype(BF)
            vv = jnp.concatenate([seq_ref[b, 192:256, :].astype(F32), minus], axis=0)
            vx[b] = vv.T.astype(BF)
            qmask = jnp.where(row < 4, (mem - 1.0) * MASK, 0.0)
            for g in (0, 1):
                h1, h2, h3 = split3(lse_ref[b, g : g + 1, :])
                ax = jnp.where(row == 4, h1, jnp.where(row == 5, h2, jnp.where(row == 6, h3, qmask)))
                qx[b, g, 0:64, :] = seq_ref[b, g * 64 : g * 64 + 64, :]
                qx[b, g, 64:128, :] = ax.astype(BF)
                d_out = do_ref[b, g * 64 : g * 64 + 64, :]
                out = o_ref[b, g * 64 : g * 64 + 64, :]
                delta = jnp.sum(d_out.astype(F32) * out.astype(F32), axis=0, keepdims=True)
                h1, h2, h3 = split3(delta)
                ax = jnp.where(row == 4, h1, jnp.where(row == 5, h2, jnp.where(row == 6, h3, 0.0)))
                dox[b, g, 0:64, :] = d_out
                dox[b, g, 64:128, :] = ax.astype(BF)
        dq[...] = jnp.zeros_like(dq)

    dk[...] = jnp.zeros_like(dk)
    dv[...] = jnp.zeros_like(dv)
    k, v, ktr = kx[j], vx[j], seq_ref[j, 128:192, :]

    def block(i, diagonal):
        sc = [dot(k, qx[i, g]) for g in (0, 1)]
        dp = [dot(v, dox[i, g]) for g in (0, 1)]
        if diagonal:
            keep = lax.broadcasted_iota(jnp.int32, (width, width), 0) <= lax.broadcasted_iota(
                jnp.int32, (width, width), 1
            )
            sc = [jnp.where(keep, x, -MASK) for x in sc]
        p = [jnp.exp2(x) for x in sc]
        ds = [(p[g] * dp[g]).astype(BF) for g in (0, 1)]
        pb = [x.astype(BF) for x in p]
        for g in (0, 1):
            dv[...] += dot(dox[i, g, 0:64, :], pb[g], NT)
            dk[...] += dot(qx[i, g, 0:64, :], ds[g], NT)
            dq[i, g] += dot(ktr, ds[g])

    block(j, True)
    hi = (next_start(starts_ref, s, j * width + width - 1, total) - 1) // width
    lax.fori_loop(j + 1, hi + 1, lambda i, c: (block(i, False), c)[1], 0)
    out_ref[j, 128:192, :] = (dk[...] * (0.125 / QUERY_SCALE)).astype(BF)
    out_ref[j, 192:256, :] = dv[...].astype(BF)

    @pl.when(j == blocks - 1)
    def _():
        for b in range(blocks):
            for g in (0, 1):
                out_ref[b, g * 64 : g * 64 + 64, :] = (dq[b, g] * 0.125).astype(BF)


def attend_back(starts, qkv, d_out, out, lse, seqs=1):
    blocks, _, rows = qkv.shape
    width = rows // seqs
    whole = lambda n: pl.BlockSpec((blocks, n, width), lambda s, j, st: (0, 0, s))
    return pl.pallas_call(
        attend_back_kernel,
        grid_spec=pltpu.PrefetchScalarGridSpec(
            num_scalar_prefetch=1,
            grid=(seqs, blocks),
            in_specs=[whole(256), whole(128), whole(128), whole(8)],
            out_specs=whole(256),
            scratch_shapes=[
                pltpu.VMEM((blocks, width, 128), BF),
                pltpu.VMEM((blocks, width, 128), BF),
                pltpu.VMEM((blocks, 2, 128, width), BF),
                pltpu.VMEM((blocks, 2, 128, width), BF),
                pltpu.VMEM((blocks, 2, 64, width), F32),
                pltpu.VMEM((64, width), F32),
                pltpu.VMEM((64, width), F32),
            ],
        ),
        out_shape=jax.ShapeDtypeStruct((blocks, 256, rows), BF),
        compiler_params=params(),
        cost_estimate=cost(60e9, 6e6),
        name="attend_back",
    )(starts, qkv, d_out, out, lse)


def middle_kernel(place_ref, x_ref, at_ref, wm_ref, wo_ref, gains_ref, mid_ref, nm_ref, sq_ref):
    core = place_ref[0]
    a = jnp.concatenate([at_ref[at] for at in order(core, wm_ref.shape[0])], axis=0)
    branch = dot(a, both(wm_ref[...], wo_ref[...]), TN)
    mid = x_ref[...].astype(F32) + branch
    mid_ref[...] = mid
    r = lax.rsqrt(jnp.mean(mid * mid, axis=-1, keepdims=True) + epsilon)
    nm_ref[...] = (mid * r * gains_ref[1:2]).astype(BF)
    sq_ref[...] = jnp.zeros_like(sq_ref)
    sq_ref[0:1, :] = jnp.sum(branch * branch, axis=0, keepdims=True)


def output_rows(w):
    rows = w.shape[3]
    return halves(w, 32, lambda i: rows // 32 - 1, pipeline_mode=pl.Buffered(1))


def middle(place, x, at, w, gains, seq):
    d = x.shape[1]
    heads, n, bt = at.shape
    arrays, specs = output_rows(w)
    return pl.pallas_call(
        middle_kernel,
        grid_spec=pltpu.PrefetchScalarGridSpec(
            num_scalar_prefetch=1,
            grid=(1,),
            in_specs=[pl.BlockSpec((bt, d), lambda i, p: (seq, 0)), fixed(heads, n, bt), *specs, fixed(8, d)],
            out_specs=[fixed(bt, d), fixed(bt, d), fixed(8, d)],
        ),
        out_shape=[
            jax.ShapeDtypeStruct((bt, d), F32),
            jax.ShapeDtypeStruct((bt, d), BF),
            jax.ShapeDtypeStruct((8, d), F32),
        ],
        compiler_params=params(),
        cost_estimate=cost(2 * bt * d * heads * n, 7e6),
        name="middle",
    )(place, x, at, *arrays, gains)


def feed_kernel(*refs, first, steps, parts):
    place_ref, n0_ref, n1_ref, c_ref = refs[:4]
    count = 2 * steps if parts else 2
    weights, refs = refs[4 : 4 + count], refs[4 + count :]
    if not first:
        fb_in, dn_in = refs[:2]
        refs = refs[2:]
    fb_ref, dn_ref, gm_ref, go_ref, nm, nmt, wscr, wsscr, hid, dgu, gsscr = refs
    f = pl.program_id(0)
    core, z = place_ref[0], place_ref[1]
    _, chips, _, per, d = wscr.shape
    rows = gm_ref.shape[2]
    unit = rows - per
    tokens, H = hid.shape
    bt = tokens // 2

    @pl.when(f == 0)
    def _():
        if first:
            fb_ref[...] = jnp.zeros_like(fb_ref)
            dn_ref[...] = jnp.zeros_like(dn_ref)
        else:
            fb_ref[...] = fb_in[...]
            dn_ref[...] = dn_in[...]
        for s, ref in enumerate((n0_ref, n1_ref)):
            for n, at in enumerate(order(core, chips)):
                nm[s * bt : (s + 1) * bt, n * 128 : (n + 1) * 128] = ref[:, lanes(at)]
        nmt[...] = nm[...].T

    for r, c in ((0, core), (1, 1 - core)):
        if parts:
            for s in range(steps):
                at = (z - s + steps) % steps
                ref = weights[r * steps + s]
                wscr[r, :, at] = ref[:, 0:per, :]
                wsscr[c, :, at] = ref[:, per:rows, :]
        else:
            wscr[r] = weights[r][:, :, 0:per, :]
            wsscr[c] = weights[r][:, :, per:rows, :]
    w, ws = flat(wscr[...]), flat(wsscr[...])
    half = tokens // 2
    for t in range(2):
        ts = slice(t * half, (t + 1) * half)
        gate_up = dot(nm[ts, :], w)
        gate, up = gate_up[:, :H], gate_up[:, H:]
        dh = dot(c_ref[ts, :], ws, NT)
        sig = 0.5 * jnp.tanh(0.5 * gate) + 0.5
        silu = gate * sig
        hidden = (silu * up).astype(BF)
        hid[ts, :] = hidden
        dgu[ts, :H] = (dh * up * sig * (1.0 + gate * (1.0 - sig))).astype(BF)
        dgu[ts, H:] = (dh * silu).astype(BF)
        fb_ref[ts, :] += dot(hidden, ws)
        dn_ref[ts, :] += dot(dgu[ts, :], w, NT)
    gsscr[...] = dot(hid[...], c_ref[...], TN).astype(BF).reshape(gsscr.shape)
    for q in (0, 1):
        ge = dot(nmt[...], dgu[:, q * H : (q + 1) * H]).astype(BF).reshape(2, chips, steps, per, H)
        for n, ref in ((0, gm_ref), (1, go_ref)):
            ref[:, :, 0:per, q * H : (q + 1) * H] = ge[n]
    for n, ref in ((core, gm_ref), (1 - core, go_ref)):
        ref[:, :, per:rows, :] = gsscr[n]


def feed(place, nm, c, w, steps, units, carry, extra):
    tokens, d = c.shape
    parts = isinstance(w, tuple) and isinstance(w[0], list)
    if parts:
        arrays = w[0] + w[1]
        chips = arrays[0].shape[0]
        per = d // (chips * 2 * steps)
        specs = [pl.BlockSpec((chips, per + UNIT, d), lambda f, p: (0, f, 0))] * len(arrays)
    else:
        chips = (w[0] if isinstance(w, tuple) else w).shape[0]
        per = d // (chips * 2 * steps)
        arrays, specs = halves(w, per + UNIT, lambda f: f)
    block = pl.BlockSpec((chips, steps, per + UNIT, d), lambda f, p: (0, 0, f, 0))
    whole = fixed(tokens, d)
    first = carry is None
    hidden = chips * 2 * steps * UNIT
    at = 4 + len(arrays)
    grad = jax.ShapeDtypeStruct((chips, steps, (per + UNIT) * units + extra, d), BF)
    return pl.pallas_call(
        functools.partial(feed_kernel, first=first, steps=steps, parts=parts),
        grid_spec=pltpu.PrefetchScalarGridSpec(
            num_scalar_prefetch=1,
            grid=(units,),
            in_specs=[fixed(*nm[0].shape), fixed(*nm[1].shape), whole, *specs] + ([] if first else [whole, whole]),
            out_specs=[whole, whole, block, block],
            scratch_shapes=[
                pltpu.VMEM((tokens, d), BF),
                pltpu.VMEM((d, tokens), BF),
                pltpu.VMEM((2, chips, steps, per, d), BF),
                pltpu.VMEM((2, chips, steps, UNIT, d), BF),
                pltpu.VMEM((tokens, hidden), BF),
                pltpu.VMEM((tokens, 2 * hidden), BF),
                pltpu.VMEM((2, chips, steps, UNIT, d), BF),
            ],
        ),
        out_shape=[jax.ShapeDtypeStruct((tokens, d), F32)] * 2 + [grad, grad],
        input_output_aliases={} if first else {at: 0, at + 1: 1},
        compiler_params=params(),
        cost_estimate=cost(18 * tokens * d * hidden * units, 8e6 * units + 20e6),
        name="feed",
    )(place, *nm, c, *arrays, *(() if first else carry))


def turn_kernel(*refs, last):
    place_ref, mid_ref, fb_ref, dn_ref, c_ref, at_ref, wm_ref, wo_ref, gains_ref = refs[:9]
    refs = refs[9:]
    if last:
        at0_ref, low0_ref = refs[:2]
        res_ref, dmid_ref, da_ref, sums_ref, gm_ref, go_ref, dn_scr, acc = refs[5:]
    else:
        res_ref, dmid_ref, da_ref, sums_ref, low_ref, dn_scr = refs
    heads, n, bt = at_ref.shape
    core = place_ref[0]
    chips, steps, per, d = wm_ref.shape
    for m, at in enumerate(order(core, chips)):
        dn_scr[:, lanes(at)] = dn_ref[:, m * 128 : (m + 1) * 128]
    mid, fb, dn = mid_ref[...], fb_ref[...], dn_scr[...]
    out = mid + fb
    res_ref[...] = out.astype(BF)
    r = lax.rsqrt(jnp.mean(mid * mid, axis=-1, keepdims=True) + epsilon)
    unit = mid * r
    g = dn * gains_ref[1:2]
    dmid = c_ref[...].astype(F32) + r * (g - unit * jnp.mean(g * unit, axis=-1, keepdims=True))
    dmid_ref[...] = dmid
    low = dmid.astype(BF)
    da = dot(both(wm_ref[...], wo_ref[...]), low, NT).astype(BF).reshape(heads, n, bt)
    for m, at in enumerate(order(core, chips)):
        da_ref[at] = da[m]
    sums_ref[...] = jnp.zeros_like(sums_ref)
    sums_ref[0:1, :] = jnp.sum(dn * unit, axis=0, keepdims=True)
    sums_ref[1:2, :] = jnp.sum(fb * fb, axis=0, keepdims=True)
    sums_ref[2:3, :] = jnp.sum(out * out, axis=0, keepdims=True)
    if last:
        a = jnp.concatenate([flat(at0_ref[...]), flat(at_ref[...])], axis=1)
        lows = jnp.concatenate([low0_ref[...], low], axis=0)
        acc[...] = dot(a, lows).astype(BF).reshape(acc.shape)
        for m, ref in ((core, gm_ref), (1 - core, go_ref)):
            ref[...] = jnp.stack([acc[a * 2 + m] for a in range(chips)])
    else:
        low_ref[...] = low


def turn(place, mid, fb, dn, c, at, w, gains, seq, before):
    d = c.shape[1]
    heads, n, bt = at.shape
    chips, _, steps = w.shape[:3]
    per = d // (chips * 2 * steps)
    rows = pl.BlockSpec((bt, d), lambda i, p: (seq, 0), pipeline_mode=pl.Buffered(1))
    here = fixed(bt, d)
    arrays, specs = output_rows(w)
    last = before is not None
    shape = jax.ShapeDtypeStruct
    if last:
        grad = before[2].shape
        behind = pl.BlockSpec(
            (chips, steps, per, d), lambda i, p: (0, 0, grad[2] // per - 1, 0), pipeline_mode=pl.Buffered(1)
        )
        anywhere = pl.BlockSpec(memory_space=pl.ANY)
    return pl.pallas_call(
        functools.partial(turn_kernel, last=last),
        grid_spec=pltpu.PrefetchScalarGridSpec(
            num_scalar_prefetch=1,
            grid=(1,),
            in_specs=[here, rows, rows, rows, fixed(heads, n, bt), *specs, fixed(8, d)]
            + ([fixed(heads, n, bt), here, anywhere, anywhere, anywhere] if last else []),
            out_specs=[rows, here, fixed(heads, n, bt), fixed(8, d)] + ([behind] * 2 if last else [here]),
            scratch_shapes=[pltpu.VMEM((bt, d), F32)]
            + ([pltpu.VMEM((chips * 2, steps, per, d), BF)] if last else []),
        ),
        out_shape=[shape(c.shape, BF), shape((bt, d), F32), shape((heads, n, bt), BF), shape((8, d), F32)]
        + ([shape(grad, BF), shape(grad, BF)] if last else [shape((bt, d), BF)]),
        input_output_aliases={11: 4, 12: 5, 13: 0} if last else {},
        compiler_params=params(),
        cost_estimate=cost((6 if last else 2) * bt * d * heads * n, 15e6),
        name="turn",
    )(place, mid, fb, dn, c, at, *arrays, gains, *(before if last else ()))


def project_back_kernel(*refs, last):
    place_ref, dqkv_ref, raw_ref, cos_ref, sin_ref, hg_ref, x_ref, dmid_ref, wm_ref, wo_ref, gains_ref = refs[:11]
    refs = refs[11:]
    if last:
        nx_ref, nx0_ref, dproj0_ref, sums0_ref, rows0_ref, head0_ref = refs[:6]
        dx_ref, gm_ref, go_ref, dproj, dn_scr, acc, extra = refs[7:]
    else:
        dx_ref, dproj, rows_ref, head_ref, dn_scr = refs
    bt, d = x_ref.shape
    core = place_ref[0]
    chips, steps, per, cols = wm_ref.shape
    wide = cols - 128
    hd, half = HEAD_DIMENSION, HEAD_DIMENSION // 2
    cos, sin = cos_ref[...], sin_ref[...]
    gains = [jnp.broadcast_to(hg_ref[:, j : j + 1], (hd, bt)) for j in (0, 1)]
    head_sums = [jnp.zeros((hd, bt), F32), jnp.zeros((hd, bt), F32)]
    for h in range(KEY_VALUE_HEADS):
        parts = []
        for slot in range(3):
            kind = 0 if slot < 2 else 1
            g = dqkv_ref[h, slot * hd : (slot + 1) * hd, :].astype(F32)
            v = raw_ref[h, slot * hd : (slot + 1) * hd, :].astype(F32)
            a, b = g[:half], g[half:]
            pre = jnp.concatenate([a * cos + b * sin, b * cos - a * sin], axis=0)
            factor = lax.rsqrt(jnp.mean(v * v, axis=0, keepdims=True) + epsilon)
            unit = v * factor
            head_sums[kind] += pre * unit
            pre = pre * gains[kind]
            back = factor * (pre - unit * jnp.mean(pre * unit, axis=0, keepdims=True))
            parts.append(back)
        parts.append(dqkv_ref[h, 3 * hd :, :].astype(F32))
        dproj[:, h * 256 : (h + 1) * 256] = jnp.concatenate(parts, axis=0).T.astype(BF)
    heads = [jnp.broadcast_to(jnp.sum(s, axis=1, keepdims=True), (hd, 128)) for s in head_sums]
    dp = dproj[...]
    dn = dot(dp, both(wm_ref[:, :, :, 0:wide], wo_ref[:, :, :, 0:wide]), NT)
    for n, at in enumerate(order(core, chips)):
        dn_scr[:, lanes(at)] = dn[:, n * 128 : (n + 1) * 128]
    dn = dn_scr[...]
    x = x_ref[...].astype(F32)
    r = lax.rsqrt(jnp.mean(x * x, axis=-1, keepdims=True) + epsilon)
    unit = x * r
    gain_sums = jnp.sum(dn * unit, axis=0, keepdims=True)
    g = dn * gains_ref[0:1]
    dx = dmid_ref[...] + r * (g - unit * jnp.mean(g * unit, axis=-1, keepdims=True))
    dx_ref[...] = dx.astype(BF)
    if not last:
        rows_ref[...] = jnp.broadcast_to(gain_sums, rows_ref.shape)
        for kind in (0, 1):
            head_ref[kind] = heads[kind]
        return
    acc[...] = (dot(nx0_ref[...], dproj0_ref[...], TN) + dot(nx_ref[...], dp, TN)).astype(BF).reshape(acc.shape)
    heads = [heads[kind] + head0_ref[kind] for kind in (0, 1)]
    lane = lax.broadcasted_iota(jnp.int32, (per, 128), 1)
    row = lax.broadcasted_iota(jnp.int32, (per, 128), 0)
    same = jnp.zeros((per, 128), F32)
    for n in range(4):
        same = jnp.where(lane == 2 + n, heads[n // 2][(n % 2) * per : (n % 2 + 1) * per, :], same)
    for n in range(3):
        same = jnp.where((lane == 6) & (row == n), jnp.sum(sums0_ref[n + 1 : n + 2, :], axis=1, keepdims=True), same)
    own = jnp.concatenate([gain_sums + rows0_ref[0:1], sums0_ref[0:1, :], jnp.zeros((126, d), F32)], axis=0)
    own = own.T.reshape(-1, per, 128)
    extra[...] = jnp.where((lane < 2)[None], own, same[None]).astype(BF).reshape(extra.shape)
    for n, ref in ((core, gm_ref), (1 - core, go_ref)):
        for a in range(chips):
            ref[a, :, :, 0:wide] = acc[a * 2 + n]
            ref[a, :, :, wide:] = extra[a * 2 + n]


def project_back(place, dqkv, raw, cos, sin, hg, x, dmid, mine, other, gains, seq, before):
    d = x.shape[1]
    kv, _, bt = raw.shape
    chips, steps, per, cols = mine.shape
    wide = cols - 128
    rows = pl.BlockSpec((bt, d), lambda i: (seq, 0), pipeline_mode=pl.Buffered(1))
    turns = pl.BlockSpec((32, bt), lambda i: (0, seq))
    last = before is not None
    shape = jax.ShapeDtypeStruct
    here = fixed(bt, d)
    grad = fixed(*mine.shape)
    proj = pltpu.VMEM((bt, wide), BF)
    return pl.pallas_call(
        functools.partial(project_back_kernel, last=last),
        grid=(1,),
        in_specs=[
            SMALL, fixed(kv, 256, bt), fixed(kv, 256, bt), turns, turns, fixed(64, 2), rows, here,
            fixed(*mine.shape), fixed(*mine.shape), fixed(8, d),
        ]
        + (
            [here, here, fixed(bt, wide), fixed(8, d), fixed(8, d), fixed(2, 64, 128), pl.BlockSpec(memory_space=pl.ANY)]
            if last
            else []
        ),
        out_specs=[rows] + ([grad, grad] if last else [fixed(bt, wide), fixed(8, d), fixed(2, 64, 128)]),
        input_output_aliases={17: 0} if last else {},
        out_shape=[shape(x.shape, BF)]
        + (
            [shape(mine.shape, BF)] * 2
            if last
            else [shape((bt, wide), BF), shape((8, d), F32), shape((2, 64, 128), F32)]
        ),
        scratch_shapes=(
            [
                proj,
                pltpu.VMEM((bt, d), F32),
                pltpu.VMEM((chips * 2, steps, per, wide), BF),
                pltpu.VMEM((chips * 2, steps, per, 128), BF),
            ]
            if last
            else [pltpu.VMEM((bt, d), F32)]
        ),
        compiler_params=params(),
        cost_estimate=cost((6 if last else 2) * bt * d * kv * 256, 20e6),
        name="project_back",
    )(place, dqkv, raw, cos, sin, hg, x, dmid, mine, other, gains, *(before if last else ()))


def heads_together(w):
    rows = w.shape[0]
    kv, hd = KEY_VALUE_HEADS, HEAD_DIMENSION
    q = w[:, : 2 * kv * hd].reshape(rows, kv, 2 * hd)
    k = w[:, 2 * kv * hd : 3 * kv * hd].reshape(rows, kv, hd)
    v = w[:, 3 * kv * hd :].reshape(rows, kv, hd)
    return jnp.concatenate([q, k, v], axis=2).reshape(rows, 4 * kv * hd)


def heads_apart(w):
    rows = w.shape[0]
    kv, hd = KEY_VALUE_HEADS, HEAD_DIMENSION
    w = w.reshape(rows, kv, 4 * hd)
    return jnp.concatenate(
        [
            w[:, :, : 2 * hd].reshape(rows, -1),
            w[:, :, 2 * hd : 3 * hd].reshape(rows, -1),
            w[:, :, 3 * hd :].reshape(rows, -1),
        ],
        axis=1,
    )


UNIT = 16
PARTS = (4, 3, 2)


def units_of(expand_weight, shrink_weight):
    per, width = expand_weight.shape
    owned, d = shrink_weight.shape
    units = owned // UNIT
    owners = width // (2 * owned)
    e = expand_weight.reshape(per, 2, owners // 8, 2, 4, units, UNIT).transpose(5, 0, 1, 3, 2, 4, 6)
    s = shrink_weight.reshape(units, UNIT, d)
    return jnp.concatenate([e.reshape(units, per, d), s], axis=1).reshape(units * (per + UNIT), d)


def units_apart(g, per):
    d = g.shape[1]
    g = g.reshape(-1, per + UNIT, d)
    units = g.shape[0]
    owners = d // (2 * UNIT)
    e = g[:, :per].reshape(units, per, 2, 2, owners // 8, 4, UNIT).transpose(1, 2, 4, 3, 5, 0, 6)
    return e.reshape(per, -1), g[:, per:].reshape(units * UNIT, d)


def after(x, *others):
    return lax.optimization_barrier((x, *others))[0]


def together(*xs):
    return lax.optimization_barrier(xs)


def heads_per_device(
    tokens, document_ids, mixer_weight, output_weight, mixer_gain, expand_weight, shrink_weight,
    feed_gain, head_gains, cotangent,
):
    seqs, rows, d = tokens.shape
    count = seqs * rows
    ring = ("chip", "core")
    steps = lax.axis_size("fsdp")
    core, z = lax.axis_index("core"), lax.axis_index("fsdp")
    place = jnp.stack([core, z]).astype(jnp.int32)
    device_count = lax.axis_size(ring) * steps
    per = mixer_gain.shape[0]
    swap = lambda a: lax.all_to_all(a, ring, 0, 0)
    across = lambda a: lax.ppermute(a, "core", [(0, 1), (1, 0)])

    def along_z(a):
        parts = [a] + [
            lax.ppermute(a, "fsdp", [(i, (i + s) % steps) for i in range(steps)]) for s in range(1, steps)
        ]
        return parts

    def in_order(parts):
        parts = [parts[-s % steps] for s in range(steps)]
        return lax.dynamic_slice_in_dim(jnp.stack(parts + parts), (steps - z) % steps, steps, 0)

    over_chips = lambda a: lax.all_gather(a, "chip", axis=0)
    reduce_chips = lambda a: lax.psum_scatter(a, "chip", scatter_dimension=0)
    add = lambda a, b: (a.astype(F32) + b.astype(F32)).astype(BF)

    def reduce_z(a):
        block = lambda s: lax.dynamic_index_in_dim(a, (z + s) % steps, 0, keepdims=False)
        out = block(0).astype(F32)
        for s in range(1, steps):
            out += lax.ppermute(block(s), "fsdp", [(i, (i + s) % steps) for i in range(steps)]).astype(F32)
        return out


    gains = jnp.pad(jnp.stack([mixer_gain, feed_gain], axis=1), ((0, 0), (0, 126)))
    mixer_parts = along_z(jnp.concatenate([heads_together(mixer_weight), gains], axis=1))

    below = jnp.sum(document_ids[:, None, :] < jnp.arange(4, dtype=jnp.int32)[None, :, None], axis=2)
    starts = jnp.sum(lax.all_gather(below.astype(jnp.int32), ring, axis=0), axis=0)
    mixer_parts, starts = lax.optimization_barrier((mixer_parts, starts))
    mixer_row = in_order(mixer_parts)
    mixer_mine = over_chips(mixer_row)

    owned = units_of(expand_weight, shrink_weight)
    owned = after(owned, mixer_row)
    pieces, at = [], 0
    for units in PARTS:
        pieces.append(owned[at : at + units * (per + UNIT)])
        at += units * (per + UNIT)
    first_row = in_order(along_z(jnp.concatenate([pieces[0], output_weight], axis=0)))
    first_part = lax.all_gather(first_row, ring, axis=0).reshape(-1, 2, *first_row.shape)
    mixer_other = across(mixer_mine)
    second = over_chips(after(pieces[1], first_row))
    third_z = along_z(after(pieces[2], first_row))

    earlier = jnp.zeros_like(document_ids)
    for n in range(1, 4):
        earlier = jnp.where(document_ids == n, starts[:, n][:, None], earlier)
    first = lax.axis_index(ring) * rows
    positions = first + jnp.arange(rows, dtype=jnp.int32)[None, :] - earlier
    half = HEAD_DIMENSION // 2
    inverse = rope_base ** (-(jnp.arange(half, dtype=F32) * 2.0 / HEAD_DIMENSION))
    angles = inverse[:, None] * positions.reshape(1, count).astype(F32)
    cos, sin = jnp.cos(angles), jnp.sin(angles)
    hg_forward = jnp.stack([head_gains[0] * QUERY_SCALE, head_gains[1]], axis=1)

    x = tokens.reshape(count, d)
    c = cotangent.reshape(count, d)
    projected = [project(place, x, mixer_mine, mixer_other, cos, sin, hg_forward, 0, rows)]
    projected.append(project(place, after(x, projected[0][0]), mixer_mine, mixer_other, cos, sin, hg_forward, 1, rows))
    qkv_heads = [swap(p[0]) for p in projected]
    gains_all = projected[0][3]

    qkv_heads[0], second = together(after(qkv_heads[0], projected[1][0]), second)
    onward = lambda a: lax.ppermute(a, "fsdp", [(i, (i + 1) % steps) for i in range(steps)])
    second_z = [second, onward(second)]
    out0 = attend(starts[0], qkv_heads[0])
    q1, second_z[1] = together(after(qkv_heads[1], out0[0]), second_z[1])
    second_z.append(onward(second_z[1]))
    out1 = attend(starts[1], q1)
    outs = [out0, out1]
    third = over_chips(in_order(after(third_z, out0[0])))
    attended = [swap(o[0]) for o in outs]
    attended[0], second_z[2] = together(after(attended[0], out1[0]), second_z[2])
    second_z.append(onward(second_z[2]))
    mids = [middle(place, x, attended[s], first_part, gains_all, s) for s in range(seqs)]
    nm = [m[1] for m in mids]
    second_other = [across(t) for t in second_z[:3]]
    nm[1], second_z[3], *second_other = together(nm[1], second_z[3], *second_other)

    units = PARTS
    fb, dn, gm, go = feed(place, nm, c, first_part, steps, units[0], None, 0)
    exchanged = (gm, across(go))
    fb, third, last_other = together(fb, third, across(second_z[3]))
    part = (second_z, second_other + [last_other])
    fb, dn, gm, go = feed(place, nm, c, part, steps, units[1], (fb, dn), 0)
    second_exchanged = (gm, across(go))
    fb, third_other, summed = together(fb, across(third), add(*after(exchanged, fb)))
    chip_sums = [reduce_chips(summed)]
    fb, dn, gm, go = feed(place, nm, c, (third, third_other), steps, units[2], (fb, dn), per)
    carry = (fb, dn)

    turned = [turn(place, mids[0][0], *carry, c, attended[0], first_part, gains_all, 0, None)]
    before = (attended[0], turned[0][4], gm, go, turned[0][0])
    d_out_heads = [swap(turned[0][2])]
    turned.append(turn(place, mids[1][0], *carry, c, attended[1], first_part, gains_all, 1, before))
    gm, go = turned[1][4:6]
    d_out_heads.append(swap(turned[1][2]))
    d_out_heads[0], chip_sums[0], summed = together(
        d_out_heads[0], chip_sums[0], add(*after(second_exchanged, gm))
    )
    chip_sums.append(reduce_chips(summed))
    sums = turned[0][3] + turned[1][3]
    small = jnp.concatenate([sums[0:1], (mids[0][2] + mids[1][2])[0:1], sums[1:3], jnp.zeros((4, d), F32)], axis=0)

    back0 = attend_back(starts[0], qkv_heads[0], d_out_heads[0], out0[0], out0[1])
    z0 = reduce_z(after(chip_sums[0], gm))
    d_out1, summed = together(after(d_out_heads[1], back0), add(*after((gm, across(go)), back0)))
    chip_sums.append(reduce_chips(summed))
    back1 = attend_back(starts[1], qkv_heads[1], d_out1, out1[0], out1[1])
    dqkv = [swap(back0), swap(back1)]
    dqkv[0], chip_sums[1] = together(after(dqkv[0], back1), chip_sums[1])
    z1 = reduce_z(chip_sums[1])

    hg = head_gains.T
    step0 = project_back(
        place, dqkv[0], projected[0][1], cos, sin, hg, x, turned[0][1], mixer_mine, mixer_other, gains_all, 0, None
    )
    before = (projected[1][2], projected[0][2], step0[1], small, step0[2], step0[3], step0[0])
    dqkv[1], chip_sums[2], z0 = together(after(dqkv[1], step0[0]), chip_sums[2], z0)
    gradients = [z0, z1, reduce_z(chip_sums[2])]
    dx1, gm, go = project_back(
        place, dqkv[1], projected[1][1], cos, sin, hg, x, turned[1][1], mixer_mine, mixer_other, gains_all, 1, before
    )
    output_gradient = gradients[2][-per:]
    gradients[2] = gradients[2][:-per]
    last = reduce_chips(add(gm, across(go)))
    expand_gradient, shrink_gradient = units_apart(jnp.concatenate(gradients, axis=0), per)
    last, expand_gradient, shrink_gradient = together(last, expand_gradient, shrink_gradient)
    last = reduce_z(last)
    wide = mixer_weight.shape[1]
    small = last[:, wide:]
    return (
        turned[1][0].reshape(tokens.shape),
        dx1.reshape(tokens.shape),
        heads_apart(last[:, :wide]),
        output_gradient,
        small[:, 0],
        expand_gradient,
        shrink_gradient,
        small[:, 1],
        small[:, 2:6].T.reshape(2, 2 * per),
        jnp.sqrt(small[:3, 6] / (device_count * count * d)),
    )


def passed_along(block, axis, distance):
    devices = range(lax.axis_size(axis))
    route = [((i - distance) % len(devices), i) for i in devices]
    return lax.ppermute(block, axis, route)


def normalize_rows(values):
    factor = lax.rsqrt(jnp.mean(values * values, axis=-1, keepdims=True) + epsilon)
    return (values * factor, factor)


def normalize_back(values, factor, upstream):
    inner_mean = jnp.mean(upstream * values, axis=-1, keepdims=True)
    return factor * upstream - values * (factor * factor * factor) * inner_mean


def rotary_tables(positions, head_size):
    halfway = head_size // 2
    inverse = rope_base ** (-(jnp.arange(halfway, dtype=jnp.float32) * 2.0 / head_size))
    angles = positions.astype(jnp.float32)[..., None] * inverse
    angles = jnp.concatenate([angles, angles], axis=-1)
    return (jnp.cos(angles), jnp.sin(angles))


def rotate(values, cosine_table, sine_table):
    halfway = values.shape[-1] // 2
    turned = jnp.concatenate([-values[..., halfway:], values[..., :halfway]], axis=-1)
    return values * cosine_table + turned * sine_table


def rotate_back(upstream, cosine_table, sine_table):
    halfway = upstream.shape[-1] // 2
    scaled = upstream * sine_table
    turned = jnp.concatenate([scaled[..., halfway:], -scaled[..., :halfway]], axis=-1)
    return upstream * cosine_table + turned


def document_positions(own_documents, all_documents, offset_rows):
    earlier = jnp.sum(
        (all_documents[:, None, :] < own_documents[:, :, None]).astype(jnp.int32), axis=2
    )
    index_rows = offset_rows + jnp.arange(own_documents.shape[1], dtype=jnp.int32)
    return index_rows[None, :] - earlier


def allowed_pairs(query_docs, key_docs, query_index, key_index):
    same_document = query_docs[:, :, None] == key_docs[:, None, :]
    causal = query_index[:, None] >= key_index[None, :]
    return jnp.logical_and(same_document, causal[None, :, :])[:, None, None, :, :]


def column_product(left, right):
    return jnp.einsum("nd,nf->df", left, right, preferred_element_type=jnp.float32)


def per_device(
    tokens,
    document_ids,
    mixer_weight,
    output_weight,
    mixer_gain,
    expand_weight,
    shrink_weight,
    feed_gain,
    head_gains,
    cotangent,
):
    sequence_count, sequence_rows, model_width = tokens.shape
    count_of_tokens = sequence_count * sequence_rows
    query_groups = QUERY_HEADS // KEY_VALUE_HEADS
    query_feature_width = QUERY_HEADS * HEAD_DIMENSION
    key_feature_width = KEY_VALUE_HEADS * HEAD_DIMENSION
    cycle_size = lax.axis_size("ctx")
    cycle_index = lax.axis_index("ctx")
    device_count = lax.axis_size("ctx") * lax.axis_size("fsdp")
    owner_slot = lax.axis_index(("ctx", "fsdp"))
    gain_rows = mixer_gain.shape[0]
    offset_rows = cycle_index * sequence_rows
    all_documents = lax.all_gather(document_ids, "ctx", axis=1, tiled=True)
    positions = document_positions(document_ids, all_documents, offset_rows)
    cosine_table, sine_table = rotary_tables(positions.reshape(count_of_tokens), HEAD_DIMENSION)
    cosine_table = cosine_table[:, None, :]
    sine_table = sine_table[:, None, :]
    query_index = offset_rows + jnp.arange(sequence_rows, dtype=jnp.int32)
    mixer_all, output_all, mixer_gain_all = (
        lax.all_gather(mixer_weight, ("ctx", "fsdp"), axis=0, tiled=True),
        lax.all_gather(output_weight, ("ctx", "fsdp"), axis=0, tiled=True),
        lax.all_gather(mixer_gain, ("ctx", "fsdp"), axis=0, tiled=True),
    )
    stream = tokens.reshape(count_of_tokens, model_width).astype(jnp.float32)
    unit_in, factor_in = normalize_rows(stream)
    normed_in = (unit_in * mixer_gain_all.astype(jnp.float32)).astype(jnp.bfloat16)
    projected_heads = jnp.dot(normed_in, mixer_all, preferred_element_type=jnp.float32)
    query_raw = projected_heads[:, :query_feature_width].reshape(
        count_of_tokens, QUERY_HEADS, HEAD_DIMENSION
    )
    unrotated_key = projected_heads[
        :, query_feature_width : query_feature_width + key_feature_width
    ].reshape(count_of_tokens, KEY_VALUE_HEADS, HEAD_DIMENSION)
    value_rows = projected_heads[:, query_feature_width + key_feature_width :].astype(jnp.bfloat16)
    query_unit, query_factor = normalize_rows(query_raw)
    key_unit, key_factor = normalize_rows(unrotated_key)
    query_row_block = rotate(query_unit * head_gains[0], cosine_table, sine_table).astype(
        jnp.bfloat16
    )
    key_rows = rotate(key_unit * head_gains[1], cosine_table, sine_table).astype(jnp.bfloat16)
    query_head_rows = query_row_block.reshape(
        sequence_count, sequence_rows, KEY_VALUE_HEADS, query_groups, HEAD_DIMENSION
    ).transpose(0, 2, 3, 1, 4)
    key_send = key_rows.reshape(sequence_count, sequence_rows, key_feature_width)
    value_send = value_rows.reshape(sequence_count, sequence_rows, key_feature_width)
    statistics_shape = (sequence_count, KEY_VALUE_HEADS, query_groups, sequence_rows)
    initial = (
        jnp.full(statistics_shape, masked_score, jnp.float32),
        jnp.zeros(statistics_shape, jnp.float32),
        jnp.zeros(statistics_shape + (HEAD_DIMENSION,), jnp.float32),
    )
    carried = initial
    key_portion = lax.all_gather(key_send, "ctx", axis=1, tiled=True)
    value_portion = lax.all_gather(value_send, "ctx", axis=1, tiled=True)
    piece_rows = key_portion.shape[1]
    block_extent = math.gcd(piece_rows, 512)
    count_of_blocks = piece_rows // block_extent
    split_key_blocks = jnp.moveaxis(
        key_portion.reshape(
            sequence_count, count_of_blocks, block_extent, KEY_VALUE_HEADS, HEAD_DIMENSION
        ),
        1,
        0,
    )
    value_blocks = jnp.moveaxis(
        value_portion.reshape(
            sequence_count, count_of_blocks, block_extent, KEY_VALUE_HEADS, HEAD_DIMENSION
        ),
        1,
        0,
    )
    block_starts = jnp.arange(count_of_blocks, dtype=jnp.int32) * block_extent

    def one_block(running, block_items):
        current_key_block, current_value_block, block_start = block_items
        row_max, total_weight, weighted_sum = running
        key_docs = lax.dynamic_slice_in_dim(all_documents, block_start, block_extent, 1)
        key_index = block_start + jnp.arange(block_extent, dtype=jnp.int32)
        allowed = allowed_pairs(document_ids, key_docs, query_index, key_index)
        scores = (
            jnp.einsum(
                "skgrd,sjkd->skgrj",
                query_head_rows,
                current_key_block,
                preferred_element_type=jnp.float32,
            )
            * 0.125
        )
        masked = jnp.where(allowed, scores, masked_score)
        new_max = jnp.maximum(row_max, jnp.max(masked, axis=-1))
        rescale = jnp.exp(row_max - new_max)
        softmax_terms = jnp.where(allowed, jnp.exp(masked - new_max[..., None]), 0.0)
        total_weight = total_weight * rescale + jnp.sum(softmax_terms, axis=-1)
        weighted_sum = weighted_sum * rescale[..., None] + jnp.einsum(
            "skgrj,sjkd->skgrd",
            softmax_terms.astype(jnp.bfloat16),
            current_value_block,
            preferred_element_type=jnp.float32,
        )
        return ((new_max, total_weight, weighted_sum), None)

    carried, _ = lax.scan(one_block, carried, (split_key_blocks, value_blocks, block_starts))
    row_max, total_weight, weighted_sum = carried
    attn_heads = weighted_sum / total_weight[..., None]
    log_total = row_max + jnp.log(total_weight)
    attended = attn_heads.transpose(0, 3, 1, 2, 4).reshape(count_of_tokens, query_feature_width)
    attended_low = attended.astype(jnp.bfloat16)
    attn_branch = jnp.dot(attended_low, output_all, preferred_element_type=jnp.float32)
    middle = stream + attn_branch
    expand_all, shrink_all, feed_gain_all = (
        lax.all_gather(expand_weight, ("ctx", "fsdp"), axis=0, tiled=True),
        lax.all_gather(shrink_weight, ("ctx", "fsdp"), axis=0, tiled=True),
        lax.all_gather(feed_gain, ("ctx", "fsdp"), axis=0, tiled=True),
    )
    unit_mid, factor_mid = normalize_rows(middle)
    normed_mid = (unit_mid * feed_gain_all.astype(jnp.float32)).astype(jnp.bfloat16)
    gate_up = jnp.dot(normed_mid, expand_all, preferred_element_type=jnp.float32)
    gate_rows = gate_up[:, :FF]
    up_rows = gate_up[:, FF:]
    gate_sigmoid = jax.nn.sigmoid(gate_rows)
    gate_silu = gate_rows * gate_sigmoid
    hidden = (gate_silu * up_rows).astype(jnp.bfloat16)
    feed_branch = jnp.dot(hidden, shrink_all, preferred_element_type=jnp.float32)
    layer_out = middle + feed_branch
    squares = jnp.stack(
        [
            jnp.sum(attn_branch * attn_branch),
            jnp.sum(feed_branch * feed_branch),
            jnp.sum(layer_out * layer_out),
        ]
    )
    stat_totals = lax.psum(squares, ("ctx", "fsdp"))
    grad_branch = cotangent.reshape(count_of_tokens, model_width)
    grad_result = grad_branch.astype(jnp.float32)
    shrink_gradient = lax.psum_scatter(
        column_product(hidden, grad_branch), ("ctx", "fsdp"), scatter_dimension=0, tiled=True
    )
    grad_hidden = jnp.einsum(
        "nd,fd->nf", grad_branch, shrink_all, preferred_element_type=jnp.float32
    )
    grad_gate = grad_hidden * up_rows * gate_sigmoid * (1.0 + gate_rows * (1.0 - gate_sigmoid))
    grad_up = grad_hidden * gate_silu
    grad_gate_up = jnp.concatenate([grad_gate, grad_up], axis=1).astype(jnp.bfloat16)
    expand_gradient = lax.psum_scatter(
        column_product(normed_mid, grad_gate_up), ("ctx", "fsdp"), scatter_dimension=0, tiled=True
    )
    grad_normed_mid = jnp.einsum(
        "nf,df->nd", grad_gate_up, expand_all, preferred_element_type=jnp.float32
    )
    feed_gain_term = jnp.sum(grad_normed_mid * unit_mid, axis=0)
    grad_middle = grad_result + normalize_back(
        middle, factor_mid, grad_normed_mid * feed_gain_all.astype(jnp.float32)
    )
    grad_attn_low = grad_middle.astype(jnp.bfloat16)
    output_gradient = lax.psum_scatter(
        column_product(attended_low, grad_attn_low),
        ("ctx", "fsdp"),
        scatter_dimension=0,
        tiled=True,
    )
    attended_gradient = jnp.einsum(
        "nd,qd->nq", grad_attn_low, output_all, preferred_element_type=jnp.float32
    ).astype(jnp.bfloat16)
    heads_gradient = attended_gradient.reshape(
        sequence_count, sequence_rows, KEY_VALUE_HEADS, query_groups, HEAD_DIMENSION
    ).transpose(0, 2, 3, 1, 4)
    delta_rows = jnp.sum(heads_gradient.astype(jnp.float32) * attn_heads, axis=-1)
    zero_query = jnp.zeros(query_head_rows.shape, jnp.float32)

    def pair_terms(current_key_block, current_value_block, block_start):
        rows_per_block = current_key_block.shape[1]
        key_reshaped = current_key_block.reshape(
            sequence_count, rows_per_block, KEY_VALUE_HEADS, HEAD_DIMENSION
        )
        value_reshaped = current_value_block.reshape(
            sequence_count, rows_per_block, KEY_VALUE_HEADS, HEAD_DIMENSION
        )
        key_docs = lax.dynamic_slice_in_dim(all_documents, block_start, rows_per_block, 1)
        key_index = block_start + jnp.arange(rows_per_block, dtype=jnp.int32)
        allowed = allowed_pairs(document_ids, key_docs, query_index, key_index)
        scores = (
            jnp.einsum(
                "skgrd,sjkd->skgrj",
                query_head_rows,
                key_reshaped,
                preferred_element_type=jnp.float32,
            )
            * 0.125
        )
        probability = jnp.where(
            allowed, jnp.exp(jnp.where(allowed, scores, 0.0) - log_total[..., None]), 0.0
        )
        value_term = jnp.einsum(
            "skgrj,skgrd->sjkd",
            probability.astype(jnp.bfloat16),
            heads_gradient,
            preferred_element_type=jnp.float32,
        )
        grad_probability = jnp.einsum(
            "skgrd,sjkd->skgrj", heads_gradient, value_reshaped, preferred_element_type=jnp.float32
        )
        grad_scores = (probability * (grad_probability - delta_rows[..., None])).astype(
            jnp.bfloat16
        )
        query_term = (
            jnp.einsum(
                "skgrj,sjkd->skgrd", grad_scores, key_reshaped, preferred_element_type=jnp.float32
            )
            * 0.125
        )
        key_term = (
            jnp.einsum(
                "skgrj,skgrd->sjkd",
                grad_scores,
                query_head_rows,
                preferred_element_type=jnp.float32,
            )
            * 0.125
        )
        return (
            query_term,
            key_term.reshape(sequence_count, rows_per_block, key_feature_width),
            value_term.reshape(sequence_count, rows_per_block, key_feature_width),
        )

    zero_keys = jnp.zeros((sequence_count, sequence_rows, key_feature_width), jnp.float32)

    def cycle_step(cycle_turn, running):
        (
            current_key_block,
            current_value_block,
            key_gradient_accumulator,
            value_accum,
            query_accum,
        ) = running
        owner_index = (cycle_index - cycle_turn) % cycle_size
        query_term, key_term, value_term = pair_terms(
            current_key_block.astype(jnp.bfloat16),
            current_value_block.astype(jnp.bfloat16),
            owner_index * sequence_rows,
        )
        query_accum = query_accum + query_term
        key_gradient_accumulator = key_gradient_accumulator + key_term
        value_accum = value_accum + value_term
        current_key_block, current_value_block, key_gradient_accumulator, value_accum = (
            passed_along(current_key_block.astype(jnp.bfloat16), "ctx", 1).astype(
                current_key_block.dtype
            ),
            passed_along(current_value_block.astype(jnp.bfloat16), "ctx", 1).astype(
                current_value_block.dtype
            ),
            passed_along(key_gradient_accumulator.astype(jnp.bfloat16), "ctx", 1).astype(
                key_gradient_accumulator.dtype
            ),
            passed_along(value_accum.astype(jnp.bfloat16), "ctx", 1).astype(value_accum.dtype),
        )
        return (
            current_key_block,
            current_value_block,
            key_gradient_accumulator,
            value_accum,
            query_accum,
        )

    carried = lax.fori_loop(
        0,
        cycle_size,
        cycle_step,
        (
            key_send.astype(jnp.float32),
            value_send.astype(jnp.float32),
            zero_keys,
            zero_keys,
            zero_query,
        ),
    )
    key_gradient_accumulator, value_accum, query_accum = (carried[2], carried[3], carried[4])
    grad_query = query_accum.transpose(0, 3, 1, 2, 4).reshape(
        count_of_tokens, QUERY_HEADS, HEAD_DIMENSION
    )
    key_grad_total = key_gradient_accumulator.reshape(
        count_of_tokens, KEY_VALUE_HEADS, HEAD_DIMENSION
    )
    grad_value = value_accum.reshape(count_of_tokens, key_feature_width)
    grad_query_pre = rotate_back(grad_query, cosine_table, sine_table)
    grad_key_pre = rotate_back(key_grad_total, cosine_table, sine_table)
    head_terms = jnp.stack(
        [
            jnp.sum(grad_query_pre * query_unit, axis=(0, 1)),
            jnp.sum(grad_key_pre * key_unit, axis=(0, 1)),
        ]
    )
    grad_query_raw = normalize_back(query_raw, query_factor, grad_query_pre * head_gains[0])
    grad_key_raw = normalize_back(unrotated_key, key_factor, grad_key_pre * head_gains[1])
    grad_projected = jnp.concatenate(
        [
            grad_query_raw.reshape(count_of_tokens, query_feature_width),
            grad_key_raw.reshape(count_of_tokens, key_feature_width),
            grad_value,
        ],
        axis=1,
    ).astype(jnp.bfloat16)
    mixer_gradient = lax.psum_scatter(
        column_product(normed_in, grad_projected), ("ctx", "fsdp"), scatter_dimension=0, tiled=True
    )
    grad_normed_in = jnp.einsum(
        "nq,dq->nd", grad_projected, mixer_all, preferred_element_type=jnp.float32
    )
    mixer_gain_term = jnp.sum(grad_normed_in * unit_in, axis=0)
    grad_stream = grad_middle + normalize_back(
        stream, factor_in, grad_normed_in * mixer_gain_all.astype(jnp.float32)
    )
    feed_gain_total, mixer_gain_total, head_total = lax.psum(
        (feed_gain_term, mixer_gain_term, head_terms), ("ctx", "fsdp")
    )
    feed_gain_gradient = lax.dynamic_slice_in_dim(
        feed_gain_total, owner_slot * gain_rows, gain_rows, 0
    )
    mixer_gain_gradient = lax.dynamic_slice_in_dim(
        mixer_gain_total, owner_slot * gain_rows, gain_rows, 0
    )
    statistics = jnp.sqrt(stat_totals / (device_count * count_of_tokens * model_width))
    result = layer_out.astype(jnp.bfloat16).reshape(sequence_count, sequence_rows, model_width)
    tokens_gradient = grad_stream.astype(jnp.bfloat16).reshape(
        sequence_count, sequence_rows, model_width
    )
    return (
        result,
        tokens_gradient,
        mixer_gradient,
        output_gradient,
        mixer_gain_gradient,
        expand_gradient,
        shrink_gradient,
        feed_gain_gradient,
        head_total,
        statistics,
    )


def solution(mesh):
    function, ring = per_device, "ctx"
    if mesh.shape["ctx"] == KEY_VALUE_HEADS:
        shape = (KEY_VALUE_HEADS // 2, 2, mesh.shape["fsdp"])
        mesh = jax.sharding.Mesh(mesh.devices.reshape(shape), ("chip", "core", "fsdp"))
        function, ring = heads_per_device, ("chip", "core")
    every = (ring, "fsdp") if isinstance(ring, str) else ring + ("fsdp",)
    tokens, rows, vector = P("fsdp", ring, None), P(every, None), P(every)
    return jax.shard_map(
        function,
        mesh=mesh,
        in_specs=(
            tokens,
            P("fsdp", ring),
            rows,
            rows,
            vector,
            rows,
            rows,
            vector,
            P(),
            tokens,
        ),
        out_specs=(tokens, tokens, rows, rows, vector, rows, rows, vector, P(), P()),
        check_vma=False,
    )
```

```python
import functools
import math

import jax
import jax.numpy as jnp
from jax import lax
from jax.experimental import pallas as pl
from jax.experimental.pallas import tpu as pltpu
from jax.sharding import PartitionSpec as P

QUERY_HEADS = 16
KEY_VALUE_HEADS = 8
HEAD_DIMENSION = 64
FF = 4608

epsilon = 1e-05
rope_base = 1000000.0
masked_score = -1e30
LOG2E = math.log2(math.e)
QUERY_SCALE = 0.125 * LOG2E
MASK = 256.0
VMEM = 60 * 2**20
BF, F32 = jnp.bfloat16, jnp.float32

NN = (((1,), (0,)), ((), ()))
NT = (((1,), (1,)), ((), ()))
TN = (((0,), (0,)), ((), ()))


def dot(a, b, dims=NN):
    return lax.dot_general(a, b, dims, preferred_element_type=F32)


def params(**kw):
    return pltpu.CompilerParams(vmem_limit_bytes=VMEM, **kw)


def cost(flops, nbytes):
    return pl.CostEstimate(flops=int(0.001 * flops), bytes_accessed=int(0.001 * nbytes), transcendentals=0)


def flat(x):
    return x.reshape(-1, x.shape[-1])


def both(mine, other):
    return jnp.concatenate([flat(mine), flat(other)], axis=0)


def order(core, chips):
    return [a * 2 + core for a in range(chips)] + [a * 2 + 1 - core for a in range(chips)]


def lanes(n, width=128):
    return pl.ds(pl.multiple_of(n * width, width), width)


SMALL = pl.BlockSpec(memory_space=pltpu.SMEM)


def fixed(*shape):
    return pl.BlockSpec(shape, lambda *i: (0,) * len(shape), pipeline_mode=pl.Buffered(1))


def halves(w, rows, index, **kw):
    if isinstance(w, tuple):
        block = (*w[0].shape[:2], rows, w[0].shape[-1])
        spec = pl.BlockSpec(block, lambda i, place: (0, 0, index(i), 0), **kw)
        return list(w), [spec, spec]
    block = (w.shape[0], None, w.shape[2], rows, w.shape[-1])
    return [w, w], [
        pl.BlockSpec(block, lambda i, place: (0, place[0], 0, index(i), 0), **kw),
        pl.BlockSpec(block, lambda i, place: (0, 1 - place[0], 0, index(i), 0), **kw),
    ]


def project_kernel(
    place_ref, x_ref, wm_ref, wo_ref, cos_ref, sin_ref, hg_ref, qkv_ref, raw_ref, nx_ref, gains_ref, nxt, grow
):
    core = place_ref[0]
    chips = wm_ref.shape[0]
    kv = KEY_VALUE_HEADS
    wide = kv * 256
    g = both(wm_ref[:, :, :, wide:], wo_ref[:, :, :, wide:]).astype(F32).T[0:8]
    for n, at in enumerate(order(core, chips)):
        grow[:, lanes(at)] = g[:, n * 128 : (n + 1) * 128]
    gains_ref[...] = grow[...]
    x = x_ref[...].astype(F32)
    r = lax.rsqrt(jnp.mean(x * x, axis=-1, keepdims=True) + epsilon)
    nx = (x * r * grow[0:1]).astype(BF)
    nx_ref[...] = nx
    bt = x.shape[0]
    nxt[...] = nx.T.reshape(nxt.shape)
    xt = jnp.concatenate([nxt[at] for at in order(core, chips)], axis=0)
    cos, sin = cos_ref[...], sin_ref[...]
    hd, half = HEAD_DIMENSION, HEAD_DIMENSION // 2
    gains = [jnp.broadcast_to(hg_ref[:, j : j + 1], (hd, bt)) for j in (0, 1)]
    for h in range(kv):
        cols = slice(h * 256, (h + 1) * 256)
        p = dot(both(wm_ref[:, :, :, cols], wo_ref[:, :, :, cols]), xt, TN)
        raw_ref[h] = p.astype(BF)
        for slot in range(3):
            v = p[slot * hd : (slot + 1) * hd]
            factor = lax.rsqrt(jnp.mean(v * v, axis=0, keepdims=True) + epsilon)
            u = v * factor * gains[0 if slot < 2 else 1]
            a, b = u[:half], u[half:]
            qkv_ref[h, slot * hd : slot * hd + half, :] = (a * cos - b * sin).astype(BF)
            qkv_ref[h, slot * hd + half : (slot + 1) * hd, :] = (b * cos + a * sin).astype(BF)
        qkv_ref[h, 3 * hd :, :] = p[3 * hd :].astype(BF)


def project(place, x, mine, other, cos, sin, hg, seq, bt):
    d = x.shape[1]
    kv = KEY_VALUE_HEADS
    turns = pl.BlockSpec((32, bt), lambda i: (0, seq))
    return pl.pallas_call(
        project_kernel,
        grid=(1,),
        in_specs=[
            SMALL,
            pl.BlockSpec((bt, d), lambda i: (seq, 0)),
            fixed(*mine.shape),
            fixed(*mine.shape),
            turns,
            turns,
            fixed(64, 2),
        ],
        out_specs=[fixed(kv, 256, bt), fixed(kv, 256, bt), fixed(bt, d), fixed(8, d)],
        out_shape=[
            jax.ShapeDtypeStruct((kv, 256, bt), BF),
            jax.ShapeDtypeStruct((kv, 256, bt), BF),
            jax.ShapeDtypeStruct((bt, d), BF),
            jax.ShapeDtypeStruct((8, d), F32),
        ],
        scratch_shapes=[pltpu.VMEM((d // 128, 128, bt), BF), pltpu.VMEM((8, d), F32)],
        compiler_params=params(),
        cost_estimate=cost(2 * bt * d * kv * 256, 14e6),
        name="project",
    )(place, x, mine, other, cos, sin, hg)


def first_start(starts_ref, s, t):
    out = jnp.int32(0)
    for d in range(1, 4):
        b = starts_ref[s * 4 + d]
        out = jnp.where(t >= b, b, out)
    return out


def next_start(starts_ref, s, t, total):
    out = jnp.int32(total)
    for d in range(3, 0, -1):
        b = starts_ref[s * 4 + d]
        out = jnp.where(t < b, b, out)
    return out


def member(starts_ref, s, base, rows, width, total):
    pos = base + lax.broadcasted_iota(jnp.int32, (rows, width), 1)
    row = lax.broadcasted_iota(jnp.int32, (rows, width), 0)
    out = jnp.zeros((rows, width), F32)
    for d in range(4):
        lo = starts_ref[s * 4 + d]
        hi = starts_ref[s * 4 + d + 1] if d < 3 else jnp.int32(total)
        out = jnp.where((row == d) & (pos >= lo) & (pos < hi), 1.0, out)
    return out


def attend_kernel(starts_ref, q_ref, seq_ref, out_ref, lse_ref, kx, vt, acc):
    s, i = pl.program_id(0), pl.program_id(1)
    blocks, _, width = seq_ref.shape
    total = blocks * width

    @pl.when(i == 0)
    def _():
        for j in range(blocks):
            aux = member(starts_ref, s, j * width, 64, width, total)
            kk = jnp.concatenate([seq_ref[j, 128:192, :].astype(F32), aux], axis=0)
            kx[j] = kk.T.astype(BF)
            vt[j, 0:64, :] = seq_ref[j, 192:256, :]
            ones = (lax.broadcasted_iota(jnp.int32, (16, width), 0) == 0).astype(F32)
            vt[j, 64:80, :] = ones.astype(BF)

    aux = ((member(starts_ref, s, i * width, 64, width, total) - 1.0) * MASK).astype(BF)
    row = lax.broadcasted_iota(jnp.int32, (64, width), 0)
    aux = jnp.where(row < 4, aux.astype(F32), 0.0).astype(BF)
    q = [jnp.concatenate([q_ref[0, g * 64 : g * 64 + 64, :], aux], axis=0) for g in (0, 1)]
    acc[...] = jnp.zeros_like(acc)

    def block(j, diagonal):
        k, v = kx[j], vt[j]
        sc = [dot(k, q[g]) for g in (0, 1)]
        if diagonal:
            keep = lax.broadcasted_iota(jnp.int32, (width, width), 0) <= lax.broadcasted_iota(
                jnp.int32, (width, width), 1
            )
            sc = [jnp.where(keep, x, -MASK) for x in sc]
        p = [jnp.exp2(x).astype(BF) for x in sc]
        for g in (0, 1):
            acc[g] += dot(v, p[g])

    lo = first_start(starts_ref, s, i * width) // width
    lax.fori_loop(lo, i, lambda j, c: (block(j, False), c)[1], 0)
    block(i, True)
    for g in (0, 1):
        a = acc[g]
        total_weight = a[64:65]
        out_ref[0, g * 64 : g * 64 + 64, :] = (a[0:64] / total_weight).astype(BF)
        lse_ref[0, g : g + 1, :] = jnp.log2(total_weight)
    lse_ref[0, 2:8, :] = jnp.zeros((6, width), F32)


def attend(starts, qkv, seqs=1):
    blocks, _, rows = qkv.shape
    width = rows // seqs
    return pl.pallas_call(
        attend_kernel,
        grid_spec=pltpu.PrefetchScalarGridSpec(
            num_scalar_prefetch=1,
            grid=(seqs, blocks),
            in_specs=[
                pl.BlockSpec((1, 256, width), lambda s, i, st: (i, 0, s)),
                pl.BlockSpec((blocks, 256, width), lambda s, i, st: (0, 0, s)),
            ],
            out_specs=[
                pl.BlockSpec((1, 128, width), lambda s, i, st: (i, 0, s)),
                pl.BlockSpec((1, 8, width), lambda s, i, st: (i, 0, s)),
            ],
            scratch_shapes=[
                pltpu.VMEM((blocks, width, 128), BF),
                pltpu.VMEM((blocks, 80, width), BF),
                pltpu.VMEM((2, 80, width), F32),
            ],
        ),
        out_shape=[
            jax.ShapeDtypeStruct((blocks, 128, rows), BF),
            jax.ShapeDtypeStruct((blocks, 8, rows), F32),
        ],
        compiler_params=params(),
        cost_estimate=cost(30e9, 4e6),
        name="attend",
    )(starts, qkv, qkv)


def split3(x):
    hi = x.astype(BF).astype(F32)
    mid = (x - hi).astype(BF).astype(F32)
    return hi, mid, x - hi - mid


def attend_back_kernel(
    starts_ref, seq_ref, do_ref, o_ref, lse_ref, out_ref, kx, vx, qx, dox, dq, dk, dv
):
    s, j = pl.program_id(0), pl.program_id(1)
    blocks, _, width = seq_ref.shape
    total = blocks * width

    @pl.when(j == 0)
    def _():
        row = lax.broadcasted_iota(jnp.int32, (64, width), 0)
        minus = jnp.where((row >= 4) & (row < 7), -1.0, 0.0)
        for b in range(blocks):
            mem = member(starts_ref, s, b * width, 64, width, total)
            aux = mem + minus
            kk = jnp.concatenate([seq_ref[b, 128:192, :].astype(F32), aux], axis=0)
            kx[b] = kk.T.astype(BF)
            vv = jnp.concatenate([seq_ref[b, 192:256, :].astype(F32), minus], axis=0)
            vx[b] = vv.T.astype(BF)
            qmask = jnp.where(row < 4, (mem - 1.0) * MASK, 0.0)
            for g in (0, 1):
                h1, h2, h3 = split3(lse_ref[b, g : g + 1, :])
                ax = jnp.where(row == 4, h1, jnp.where(row == 5, h2, jnp.where(row == 6, h3, qmask)))
                qx[b, g, 0:64, :] = seq_ref[b, g * 64 : g * 64 + 64, :]
                qx[b, g, 64:128, :] = ax.astype(BF)
                d_out = do_ref[b, g * 64 : g * 64 + 64, :]
                out = o_ref[b, g * 64 : g * 64 + 64, :]
                delta = jnp.sum(d_out.astype(F32) * out.astype(F32), axis=0, keepdims=True)
                h1, h2, h3 = split3(delta)
                ax = jnp.where(row == 4, h1, jnp.where(row == 5, h2, jnp.where(row == 6, h3, 0.0)))
                dox[b, g, 0:64, :] = d_out
                dox[b, g, 64:128, :] = ax.astype(BF)
        dq[...] = jnp.zeros_like(dq)

    dk[...] = jnp.zeros_like(dk)
    dv[...] = jnp.zeros_like(dv)
    k, v, ktr = kx[j], vx[j], seq_ref[j, 128:192, :]

    def block(i, diagonal):
        sc = [dot(k, qx[i, g]) for g in (0, 1)]
        dp = [dot(v, dox[i, g]) for g in (0, 1)]
        if diagonal:
            keep = lax.broadcasted_iota(jnp.int32, (width, width), 0) <= lax.broadcasted_iota(
                jnp.int32, (width, width), 1
            )
            sc = [jnp.where(keep, x, -MASK) for x in sc]
        p = [jnp.exp2(x) for x in sc]
        ds = [(p[g] * dp[g]).astype(BF) for g in (0, 1)]
        pb = [x.astype(BF) for x in p]
        for g in (0, 1):
            dv[...] += dot(dox[i, g, 0:64, :], pb[g], NT)
            dk[...] += dot(qx[i, g, 0:64, :], ds[g], NT)
            dq[i, g] += dot(ktr, ds[g])

    block(j, True)
    hi = (next_start(starts_ref, s, j * width + width - 1, total) - 1) // width
    lax.fori_loop(j + 1, hi + 1, lambda i, c: (block(i, False), c)[1], 0)
    out_ref[j, 128:192, :] = (dk[...] * (0.125 / QUERY_SCALE)).astype(BF)
    out_ref[j, 192:256, :] = dv[...].astype(BF)

    @pl.when(j == blocks - 1)
    def _():
        for b in range(blocks):
            for g in (0, 1):
                out_ref[b, g * 64 : g * 64 + 64, :] = (dq[b, g] * 0.125).astype(BF)


def attend_back(starts, qkv, d_out, out, lse, seqs=1):
    blocks, _, rows = qkv.shape
    width = rows // seqs
    whole = lambda n: pl.BlockSpec((blocks, n, width), lambda s, j, st: (0, 0, s))
    return pl.pallas_call(
        attend_back_kernel,
        grid_spec=pltpu.PrefetchScalarGridSpec(
            num_scalar_prefetch=1,
            grid=(seqs, blocks),
            in_specs=[whole(256), whole(128), whole(128), whole(8)],
            out_specs=whole(256),
            scratch_shapes=[
                pltpu.VMEM((blocks, width, 128), BF),
                pltpu.VMEM((blocks, width, 128), BF),
                pltpu.VMEM((blocks, 2, 128, width), BF),
                pltpu.VMEM((blocks, 2, 128, width), BF),
                pltpu.VMEM((blocks, 2, 64, width), F32),
                pltpu.VMEM((64, width), F32),
                pltpu.VMEM((64, width), F32),
            ],
        ),
        out_shape=jax.ShapeDtypeStruct((blocks, 256, rows), BF),
        compiler_params=params(),
        cost_estimate=cost(60e9, 6e6),
        name="attend_back",
    )(starts, qkv, d_out, out, lse)


def middle_kernel(place_ref, x_ref, at_ref, wm_ref, wo_ref, gains_ref, mid_ref, nm_ref, sq_ref):
    core = place_ref[0]
    a = jnp.concatenate([at_ref[at] for at in order(core, wm_ref.shape[0])], axis=0)
    branch = dot(a, both(wm_ref[...], wo_ref[...]), TN)
    mid = x_ref[...].astype(F32) + branch
    mid_ref[...] = mid
    r = lax.rsqrt(jnp.mean(mid * mid, axis=-1, keepdims=True) + epsilon)
    nm_ref[...] = (mid * r * gains_ref[1:2]).astype(BF)
    sq_ref[...] = jnp.zeros_like(sq_ref)
    sq_ref[0:1, :] = jnp.sum(branch * branch, axis=0, keepdims=True)


def output_rows(w):
    rows = w.shape[3]
    return halves(w, 32, lambda i: rows // 32 - 1, pipeline_mode=pl.Buffered(1))


def middle(place, x, at, w, gains, seq):
    d = x.shape[1]
    heads, n, bt = at.shape
    arrays, specs = output_rows(w)
    return pl.pallas_call(
        middle_kernel,
        grid_spec=pltpu.PrefetchScalarGridSpec(
            num_scalar_prefetch=1,
            grid=(1,),
            in_specs=[pl.BlockSpec((bt, d), lambda i, p: (seq, 0)), fixed(heads, n, bt), *specs, fixed(8, d)],
            out_specs=[fixed(bt, d), fixed(bt, d), fixed(8, d)],
        ),
        out_shape=[
            jax.ShapeDtypeStruct((bt, d), F32),
            jax.ShapeDtypeStruct((bt, d), BF),
            jax.ShapeDtypeStruct((8, d), F32),
        ],
        compiler_params=params(),
        cost_estimate=cost(2 * bt * d * heads * n, 7e6),
        name="middle",
    )(place, x, at, *arrays, gains)


def feed_kernel(*refs, first, steps, parts):
    place_ref, n0_ref, n1_ref, c_ref = refs[:4]
    count = 2 * steps if parts else 2
    weights, refs = refs[4 : 4 + count], refs[4 + count :]
    if not first:
        fb_in, dn_in = refs[:2]
        refs = refs[2:]
    fb_ref, dn_ref, gm_ref, go_ref, nm, nmt, wscr, wsscr, hid, dgu, gsscr = refs
    f = pl.program_id(0)
    core, z = place_ref[0], place_ref[1]
    _, chips, _, per, d = wscr.shape
    rows = gm_ref.shape[2]
    unit = rows - per
    tokens, H = hid.shape
    bt = tokens // 2

    @pl.when(f == 0)
    def _():
        if first:
            fb_ref[...] = jnp.zeros_like(fb_ref)
            dn_ref[...] = jnp.zeros_like(dn_ref)
        else:
            fb_ref[...] = fb_in[...]
            dn_ref[...] = dn_in[...]
        for s, ref in enumerate((n0_ref, n1_ref)):
            for n, at in enumerate(order(core, chips)):
                nm[s * bt : (s + 1) * bt, n * 128 : (n + 1) * 128] = ref[:, lanes(at)]
        nmt[...] = nm[...].T

    for r, c in ((0, core), (1, 1 - core)):
        if parts:
            for s in range(steps):
                at = (z - s + steps) % steps
                ref = weights[r * steps + s]
                wscr[r, :, at] = ref[:, 0:per, :]
                wsscr[c, :, at] = ref[:, per:rows, :]
        else:
            wscr[r] = weights[r][:, :, 0:per, :]
            wsscr[c] = weights[r][:, :, per:rows, :]
    w, ws = flat(wscr[...]), flat(wsscr[...])
    half = tokens // 2
    for t in range(2):
        ts = slice(t * half, (t + 1) * half)
        gate_up = dot(nm[ts, :], w)
        gate, up = gate_up[:, :H], gate_up[:, H:]
        dh = dot(c_ref[ts, :], ws, NT)
        sig = 0.5 * jnp.tanh(0.5 * gate) + 0.5
        silu = gate * sig
        hidden = (silu * up).astype(BF)
        hid[ts, :] = hidden
        dgu[ts, :H] = (dh * up * sig * (1.0 + gate * (1.0 - sig))).astype(BF)
        dgu[ts, H:] = (dh * silu).astype(BF)
        fb_ref[ts, :] += dot(hidden, ws)
        dn_ref[ts, :] += dot(dgu[ts, :], w, NT)
    gsscr[...] = dot(hid[...], c_ref[...], TN).astype(BF).reshape(gsscr.shape)
    for q in (0, 1):
        ge = dot(nmt[...], dgu[:, q * H : (q + 1) * H]).astype(BF).reshape(2, chips, steps, per, H)
        for n, ref in ((0, gm_ref), (1, go_ref)):
            ref[:, :, 0:per, q * H : (q + 1) * H] = ge[n]
    for n, ref in ((core, gm_ref), (1 - core, go_ref)):
        ref[:, :, per:rows, :] = gsscr[n]


def feed(place, nm, c, w, steps, units, carry, extra):
    tokens, d = c.shape
    parts = isinstance(w, tuple) and isinstance(w[0], list)
    if parts:
        arrays = w[0] + w[1]
        chips = arrays[0].shape[0]
        per = d // (chips * 2 * steps)
        specs = [pl.BlockSpec((chips, per + UNIT, d), lambda f, p: (0, f, 0))] * len(arrays)
    else:
        chips = (w[0] if isinstance(w, tuple) else w).shape[0]
        per = d // (chips * 2 * steps)
        arrays, specs = halves(w, per + UNIT, lambda f: f)
    block = pl.BlockSpec((chips, steps, per + UNIT, d), lambda f, p: (0, 0, f, 0))
    whole = fixed(tokens, d)
    first = carry is None
    hidden = chips * 2 * steps * UNIT
    at = 4 + len(arrays)
    grad = jax.ShapeDtypeStruct((chips, steps, (per + UNIT) * units + extra, d), BF)
    return pl.pallas_call(
        functools.partial(feed_kernel, first=first, steps=steps, parts=parts),
        grid_spec=pltpu.PrefetchScalarGridSpec(
            num_scalar_prefetch=1,
            grid=(units,),
            in_specs=[fixed(*nm[0].shape), fixed(*nm[1].shape), whole, *specs] + ([] if first else [whole, whole]),
            out_specs=[whole, whole, block, block],
            scratch_shapes=[
                pltpu.VMEM((tokens, d), BF),
                pltpu.VMEM((d, tokens), BF),
                pltpu.VMEM((2, chips, steps, per, d), BF),
                pltpu.VMEM((2, chips, steps, UNIT, d), BF),
                pltpu.VMEM((tokens, hidden), BF),
                pltpu.VMEM((tokens, 2 * hidden), BF),
                pltpu.VMEM((2, chips, steps, UNIT, d), BF),
            ],
        ),
        out_shape=[jax.ShapeDtypeStruct((tokens, d), F32)] * 2 + [grad, grad],
        input_output_aliases={} if first else {at: 0, at + 1: 1},
        compiler_params=params(),
        cost_estimate=cost(18 * tokens * d * hidden * units, 8e6 * units + 20e6),
        name="feed",
    )(place, *nm, c, *arrays, *(() if first else carry))


def turn_kernel(*refs, last):
    place_ref, mid_ref, fb_ref, dn_ref, c_ref, at_ref, wm_ref, wo_ref, gains_ref = refs[:9]
    refs = refs[9:]
    if last:
        at0_ref, low0_ref = refs[:2]
        res_ref, dmid_ref, da_ref, sums_ref, gm_ref, go_ref, dn_scr, acc = refs[5:]
    else:
        res_ref, dmid_ref, da_ref, sums_ref, low_ref, dn_scr = refs
    heads, n, bt = at_ref.shape
    core = place_ref[0]
    chips, steps, per, d = wm_ref.shape
    for m, at in enumerate(order(core, chips)):
        dn_scr[:, lanes(at)] = dn_ref[:, m * 128 : (m + 1) * 128]
    mid, fb, dn = mid_ref[...], fb_ref[...], dn_scr[...]
    out = mid + fb
    res_ref[...] = out.astype(BF)
    r = lax.rsqrt(jnp.mean(mid * mid, axis=-1, keepdims=True) + epsilon)
    unit = mid * r
    g = dn * gains_ref[1:2]
    dmid = c_ref[...].astype(F32) + r * (g - unit * jnp.mean(g * unit, axis=-1, keepdims=True))
    dmid_ref[...] = dmid
    low = dmid.astype(BF)
    da = dot(both(wm_ref[...], wo_ref[...]), low, NT).astype(BF).reshape(heads, n, bt)
    for m, at in enumerate(order(core, chips)):
        da_ref[at] = da[m]
    sums_ref[...] = jnp.zeros_like(sums_ref)
    sums_ref[0:1, :] = jnp.sum(dn * unit, axis=0, keepdims=True)
    sums_ref[1:2, :] = jnp.sum(fb * fb, axis=0, keepdims=True)
    sums_ref[2:3, :] = jnp.sum(out * out, axis=0, keepdims=True)
    if last:
        a = jnp.concatenate([flat(at0_ref[...]), flat(at_ref[...])], axis=1)
        lows = jnp.concatenate([low0_ref[...], low], axis=0)
        acc[...] = dot(a, lows).astype(BF).reshape(acc.shape)
        for m, ref in ((core, gm_ref), (1 - core, go_ref)):
            ref[...] = jnp.stack([acc[a * 2 + m] for a in range(chips)])
    else:
        low_ref[...] = low


def turn(place, mid, fb, dn, c, at, w, gains, seq, before):
    d = c.shape[1]
    heads, n, bt = at.shape
    chips, _, steps = w.shape[:3]
    per = d // (chips * 2 * steps)
    rows = pl.BlockSpec((bt, d), lambda i, p: (seq, 0), pipeline_mode=pl.Buffered(1))
    here = fixed(bt, d)
    arrays, specs = output_rows(w)
    last = before is not None
    shape = jax.ShapeDtypeStruct
    if last:
        grad = before[2].shape
        behind = pl.BlockSpec(
            (chips, steps, per, d), lambda i, p: (0, 0, grad[2] // per - 1, 0), pipeline_mode=pl.Buffered(1)
        )
        anywhere = pl.BlockSpec(memory_space=pl.ANY)
    return pl.pallas_call(
        functools.partial(turn_kernel, last=last),
        grid_spec=pltpu.PrefetchScalarGridSpec(
            num_scalar_prefetch=1,
            grid=(1,),
            in_specs=[here, rows, rows, rows, fixed(heads, n, bt), *specs, fixed(8, d)]
            + ([fixed(heads, n, bt), here, anywhere, anywhere, anywhere] if last else []),
            out_specs=[rows, here, fixed(heads, n, bt), fixed(8, d)] + ([behind] * 2 if last else [here]),
            scratch_shapes=[pltpu.VMEM((bt, d), F32)]
            + ([pltpu.VMEM((chips * 2, steps, per, d), BF)] if last else []),
        ),
        out_shape=[shape(c.shape, BF), shape((bt, d), F32), shape((heads, n, bt), BF), shape((8, d), F32)]
        + ([shape(grad, BF), shape(grad, BF)] if last else [shape((bt, d), BF)]),
        input_output_aliases={11: 4, 12: 5, 13: 0} if last else {},
        compiler_params=params(),
        cost_estimate=cost((6 if last else 2) * bt * d * heads * n, 15e6),
        name="turn",
    )(place, mid, fb, dn, c, at, *arrays, gains, *(before if last else ()))


def project_back_kernel(*refs, last):
    place_ref, dqkv_ref, raw_ref, cos_ref, sin_ref, hg_ref, x_ref, dmid_ref, wm_ref, wo_ref, gains_ref = refs[:11]
    refs = refs[11:]
    if last:
        nx_ref, nx0_ref, dproj0_ref, sums0_ref, rows0_ref, head0_ref = refs[:6]
        dx_ref, gm_ref, go_ref, dproj, dn_scr, acc, extra = refs[7:]
    else:
        dx_ref, dproj, rows_ref, head_ref, dn_scr = refs
    bt, d = x_ref.shape
    core = place_ref[0]
    chips, steps, per, cols = wm_ref.shape
    wide = cols - 128
    hd, half = HEAD_DIMENSION, HEAD_DIMENSION // 2
    cos, sin = cos_ref[...], sin_ref[...]
    gains = [jnp.broadcast_to(hg_ref[:, j : j + 1], (hd, bt)) for j in (0, 1)]
    head_sums = [jnp.zeros((hd, bt), F32), jnp.zeros((hd, bt), F32)]
    for h in range(KEY_VALUE_HEADS):
        parts = []
        for slot in range(3):
            kind = 0 if slot < 2 else 1
            g = dqkv_ref[h, slot * hd : (slot + 1) * hd, :].astype(F32)
            v = raw_ref[h, slot * hd : (slot + 1) * hd, :].astype(F32)
            a, b = g[:half], g[half:]
            pre = jnp.concatenate([a * cos + b * sin, b * cos - a * sin], axis=0)
            factor = lax.rsqrt(jnp.mean(v * v, axis=0, keepdims=True) + epsilon)
            unit = v * factor
            head_sums[kind] += pre * unit
            pre = pre * gains[kind]
            back = factor * (pre - unit * jnp.mean(pre * unit, axis=0, keepdims=True))
            parts.append(back)
        parts.append(dqkv_ref[h, 3 * hd :, :].astype(F32))
        dproj[:, h * 256 : (h + 1) * 256] = jnp.concatenate(parts, axis=0).T.astype(BF)
    heads = [jnp.broadcast_to(jnp.sum(s, axis=1, keepdims=True), (hd, 128)) for s in head_sums]
    dp = dproj[...]
    dn = dot(dp, both(wm_ref[:, :, :, 0:wide], wo_ref[:, :, :, 0:wide]), NT)
    for n, at in enumerate(order(core, chips)):
        dn_scr[:, lanes(at)] = dn[:, n * 128 : (n + 1) * 128]
    dn = dn_scr[...]
    x = x_ref[...].astype(F32)
    r = lax.rsqrt(jnp.mean(x * x, axis=-1, keepdims=True) + epsilon)
    unit = x * r
    gain_sums = jnp.sum(dn * unit, axis=0, keepdims=True)
    g = dn * gains_ref[0:1]
    dx = dmid_ref[...] + r * (g - unit * jnp.mean(g * unit, axis=-1, keepdims=True))
    dx_ref[...] = dx.astype(BF)
    if not last:
        rows_ref[...] = jnp.broadcast_to(gain_sums, rows_ref.shape)
        for kind in (0, 1):
            head_ref[kind] = heads[kind]
        return
    acc[...] = (dot(nx0_ref[...], dproj0_ref[...], TN) + dot(nx_ref[...], dp, TN)).astype(BF).reshape(acc.shape)
    heads = [heads[kind] + head0_ref[kind] for kind in (0, 1)]
    lane = lax.broadcasted_iota(jnp.int32, (per, 128), 1)
    row = lax.broadcasted_iota(jnp.int32, (per, 128), 0)
    same = jnp.zeros((per, 128), F32)
    for n in range(4):
        same = jnp.where(lane == 2 + n, heads[n // 2][(n % 2) * per : (n % 2 + 1) * per, :], same)
    for n in range(3):
        same = jnp.where((lane == 6) & (row == n), jnp.sum(sums0_ref[n + 1 : n + 2, :], axis=1, keepdims=True), same)
    own = jnp.concatenate([gain_sums + rows0_ref[0:1], sums0_ref[0:1, :], jnp.zeros((126, d), F32)], axis=0)
    own = own.T.reshape(-1, per, 128)
    extra[...] = jnp.where((lane < 2)[None], own, same[None]).astype(BF).reshape(extra.shape)
    for n, ref in ((core, gm_ref), (1 - core, go_ref)):
        for a in range(chips):
            ref[a, :, :, 0:wide] = acc[a * 2 + n]
            ref[a, :, :, wide:] = extra[a * 2 + n]


def project_back(place, dqkv, raw, cos, sin, hg, x, dmid, mine, other, gains, seq, before):
    d = x.shape[1]
    kv, _, bt = raw.shape
    chips, steps, per, cols = mine.shape
    wide = cols - 128
    rows = pl.BlockSpec((bt, d), lambda i: (seq, 0), pipeline_mode=pl.Buffered(1))
    turns = pl.BlockSpec((32, bt), lambda i: (0, seq))
    last = before is not None
    shape = jax.ShapeDtypeStruct
    here = fixed(bt, d)
    grad = fixed(*mine.shape)
    proj = pltpu.VMEM((bt, wide), BF)
    return pl.pallas_call(
        functools.partial(project_back_kernel, last=last),
        grid=(1,),
        in_specs=[
            SMALL, fixed(kv, 256, bt), fixed(kv, 256, bt), turns, turns, fixed(64, 2), rows, here,
            fixed(*mine.shape), fixed(*mine.shape), fixed(8, d),
        ]
        + (
            [here, here, fixed(bt, wide), fixed(8, d), fixed(8, d), fixed(2, 64, 128), pl.BlockSpec(memory_space=pl.ANY)]
            if last
            else []
        ),
        out_specs=[rows] + ([grad, grad] if last else [fixed(bt, wide), fixed(8, d), fixed(2, 64, 128)]),
        input_output_aliases={17: 0} if last else {},
        out_shape=[shape(x.shape, BF)]
        + (
            [shape(mine.shape, BF)] * 2
            if last
            else [shape((bt, wide), BF), shape((8, d), F32), shape((2, 64, 128), F32)]
        ),
        scratch_shapes=(
            [
                proj,
                pltpu.VMEM((bt, d), F32),
                pltpu.VMEM((chips * 2, steps, per, wide), BF),
                pltpu.VMEM((chips * 2, steps, per, 128), BF),
            ]
            if last
            else [pltpu.VMEM((bt, d), F32)]
        ),
        compiler_params=params(),
        cost_estimate=cost((6 if last else 2) * bt * d * kv * 256, 20e6),
        name="project_back",
    )(place, dqkv, raw, cos, sin, hg, x, dmid, mine, other, gains, *(before if last else ()))


def add_kernel(a_ref, b_ref, out_ref):
    out_ref[...] = (a_ref[...].astype(F32) + b_ref[...].astype(F32)).astype(BF)


def add_up(a, b):
    n, rows, columns = a.shape[0] * a.shape[1], a.shape[2], a.shape[3]
    if rows < 128:
        return (a.astype(F32) + b.astype(F32)).astype(BF)
    block = pl.BlockSpec((n // 8, rows, columns), lambda i: (i, 0, 0))
    flat3 = (n, rows, columns)
    out = pl.pallas_call(
        add_kernel,
        grid=(8,),
        in_specs=[block, block],
        out_specs=block,
        out_shape=jax.ShapeDtypeStruct(flat3, BF),
        compiler_params=params(),
        cost_estimate=cost(n * rows * columns, 6 * n * rows * columns),
        name="add_up",
    )(a.reshape(flat3), b.reshape(flat3))
    return out.reshape(a.shape)


def heads_together(w):
    rows = w.shape[0]
    kv, hd = KEY_VALUE_HEADS, HEAD_DIMENSION
    q = w[:, : 2 * kv * hd].reshape(rows, kv, 2 * hd)
    k = w[:, 2 * kv * hd : 3 * kv * hd].reshape(rows, kv, hd)
    v = w[:, 3 * kv * hd :].reshape(rows, kv, hd)
    return jnp.concatenate([q, k, v], axis=2).reshape(rows, 4 * kv * hd)


def heads_apart(w):
    rows = w.shape[0]
    kv, hd = KEY_VALUE_HEADS, HEAD_DIMENSION
    w = w.reshape(rows, kv, 4 * hd)
    return jnp.concatenate(
        [
            w[:, :, : 2 * hd].reshape(rows, -1),
            w[:, :, 2 * hd : 3 * hd].reshape(rows, -1),
            w[:, :, 3 * hd :].reshape(rows, -1),
        ],
        axis=1,
    )


UNIT = 16
PARTS = (2, 3, 4)


def units_of(expand_weight, shrink_weight):
    per, width = expand_weight.shape
    owned, d = shrink_weight.shape
    units = owned // UNIT
    owners = width // (2 * owned)
    e = expand_weight.reshape(per, 2, owners // 8, 2, 4, units, UNIT).transpose(5, 0, 1, 3, 2, 4, 6)
    s = shrink_weight.reshape(units, UNIT, d)
    return jnp.concatenate([e.reshape(units, per, d), s], axis=1).reshape(units * (per + UNIT), d)


def units_apart(g, per):
    d = g.shape[1]
    g = g.reshape(-1, per + UNIT, d)
    units = g.shape[0]
    owners = d // (2 * UNIT)
    e = g[:, :per].reshape(units, per, 2, 2, owners // 8, 4, UNIT).transpose(1, 2, 4, 3, 5, 0, 6)
    return e.reshape(per, -1), g[:, per:].reshape(units * UNIT, d)


def after(x, *others):
    return lax.optimization_barrier((x, *others))[0]


def together(*xs):
    return lax.optimization_barrier(xs)


def heads_per_device(
    tokens, document_ids, mixer_weight, output_weight, mixer_gain, expand_weight, shrink_weight,
    feed_gain, head_gains, cotangent,
):
    seqs, rows, d = tokens.shape
    count = seqs * rows
    ring = ("chip", "core")
    steps = lax.axis_size("fsdp")
    core, z = lax.axis_index("core"), lax.axis_index("fsdp")
    place = jnp.stack([core, z]).astype(jnp.int32)
    device_count = lax.axis_size(ring) * steps
    per = mixer_gain.shape[0]
    swap = lambda a: lax.all_to_all(a, ring, 0, 0)
    across = lambda a: lax.ppermute(a, "core", [(0, 1), (1, 0)])

    def along_z(a):
        parts = [a] + [
            lax.ppermute(a, "fsdp", [(i, (i + s) % steps) for i in range(steps)]) for s in range(1, steps)
        ]
        return parts

    def in_order(parts):
        parts = [parts[-s % steps] for s in range(steps)]
        return lax.dynamic_slice_in_dim(jnp.stack(parts + parts), (steps - z) % steps, steps, 0)

    over_chips = lambda a: lax.all_gather(a, "chip", axis=0)
    reduce_chips = lambda a: lax.psum_scatter(a, "chip", scatter_dimension=0)

    def reduce_z(a):
        block = lambda s: lax.dynamic_index_in_dim(a, (z + s) % steps, 0, keepdims=False)
        out = block(0).astype(F32)
        for s in range(1, steps):
            out += lax.ppermute(block(s), "fsdp", [(i, (i + s) % steps) for i in range(steps)]).astype(F32)
        return out


    gains = jnp.pad(jnp.stack([mixer_gain, feed_gain], axis=1), ((0, 0), (0, 126)))
    mixer_parts = along_z(jnp.concatenate([heads_together(mixer_weight), gains], axis=1))

    below = jnp.sum(document_ids[:, None, :] < jnp.arange(4, dtype=jnp.int32)[None, :, None], axis=2)
    starts = jnp.sum(lax.all_gather(below.astype(jnp.int32), ring, axis=0), axis=0)
    mixer_parts, starts = lax.optimization_barrier((mixer_parts, starts))
    mixer_row = in_order(mixer_parts)
    mixer_mine = over_chips(mixer_row)

    owned = units_of(expand_weight, shrink_weight)
    owned = after(owned, mixer_row)
    pieces, at = [], 0
    for units in PARTS:
        pieces.append(owned[at : at + units * (per + UNIT)])
        at += units * (per + UNIT)
    first_row = in_order(along_z(jnp.concatenate([pieces[0], output_weight], axis=0)))
    first_part = lax.all_gather(first_row, ring, axis=0).reshape(-1, 2, *first_row.shape)
    mixer_other = across(mixer_mine)
    second = over_chips(after(pieces[1], first_row))
    third_z = along_z(after(pieces[2], first_row))

    earlier = jnp.zeros_like(document_ids)
    for n in range(1, 4):
        earlier = jnp.where(document_ids == n, starts[:, n][:, None], earlier)
    first = lax.axis_index(ring) * rows
    positions = first + jnp.arange(rows, dtype=jnp.int32)[None, :] - earlier
    half = HEAD_DIMENSION // 2
    inverse = rope_base ** (-(jnp.arange(half, dtype=F32) * 2.0 / HEAD_DIMENSION))
    angles = inverse[:, None] * positions.reshape(1, count).astype(F32)
    cos, sin = jnp.cos(angles), jnp.sin(angles)
    hg_forward = jnp.stack([head_gains[0] * QUERY_SCALE, head_gains[1]], axis=1)

    x = tokens.reshape(count, d)
    c = cotangent.reshape(count, d)
    projected = [project(place, x, mixer_mine, mixer_other, cos, sin, hg_forward, 0, rows)]
    projected.append(project(place, after(x, projected[0][0]), mixer_mine, mixer_other, cos, sin, hg_forward, 1, rows))
    qkv_heads = [swap(p[0]) for p in projected]
    gains_all = projected[0][3]

    qkv_heads[0], second = together(after(qkv_heads[0], projected[1][0]), second)
    onward = lambda a: lax.ppermute(a, "fsdp", [(i, (i + 1) % steps) for i in range(steps)])
    second_z = [second, onward(second)]
    out0 = attend(starts[0], qkv_heads[0])
    q1, second_z[1] = together(after(qkv_heads[1], out0[0]), second_z[1])
    second_z.append(onward(second_z[1]))
    out1 = attend(starts[1], q1)
    outs = [out0, out1]
    third = over_chips(in_order(after(third_z, out0[0])))
    attended = [swap(o[0]) for o in outs]
    attended[0], second_z[2] = together(after(attended[0], out1[0]), second_z[2])
    second_z.append(onward(second_z[2]))
    mids = [middle(place, x, attended[s], first_part, gains_all, s) for s in range(seqs)]
    nm = [m[1] for m in mids]
    second_other = [across(t) for t in second_z[:3]]
    nm[1], second_z[3], *second_other = together(nm[1], second_z[3], *second_other)

    units = PARTS
    fb, dn, gm, go = feed(place, nm, c, first_part, steps, units[0], None, 0)
    exchanged = (gm, across(go))
    fb, third, last_other = together(fb, third, across(second_z[3]))
    part = (second_z, second_other + [last_other])
    fb, dn, gm, go = feed(place, nm, c, part, steps, units[1], (fb, dn), 0)
    second_exchanged = (gm, across(go))
    fb, third_other, summed = together(fb, across(third), add_up(*after(exchanged, fb)))
    chip_sums = [reduce_chips(summed)]
    fb, dn, gm, go = feed(place, nm, c, (third, third_other), steps, units[2], (fb, dn), per)
    carry = (fb, dn)

    turned = [turn(place, mids[0][0], *carry, c, attended[0], first_part, gains_all, 0, None)]
    before = (attended[0], turned[0][4], gm, go, turned[0][0])
    d_out_heads = [swap(turned[0][2])]
    turned.append(turn(place, mids[1][0], *carry, c, attended[1], first_part, gains_all, 1, before))
    gm, go = turned[1][4:6]
    d_out_heads.append(swap(turned[1][2]))
    d_out_heads[0], chip_sums[0], summed = together(
        d_out_heads[0], chip_sums[0], add_up(*after(second_exchanged, gm))
    )
    chip_sums.append(reduce_chips(summed))
    sums = turned[0][3] + turned[1][3]
    small = jnp.concatenate([sums[0:1], (mids[0][2] + mids[1][2])[0:1], sums[1:3], jnp.zeros((4, d), F32)], axis=0)

    back0 = attend_back(starts[0], qkv_heads[0], d_out_heads[0], out0[0], out0[1])
    d_out1, summed = together(after(d_out_heads[1], back0), add_up(*after((gm, across(go)), back0)))
    chip_sums.append(reduce_chips(summed))
    back1 = attend_back(starts[1], qkv_heads[1], d_out1, out1[0], out1[1])
    dqkv = [swap(back0), swap(back1)]
    dqkv[0], chip_sums[0], chip_sums[1] = together(after(dqkv[0], back1), chip_sums[0], chip_sums[1])
    z0 = reduce_z(chip_sums[0])
    z1 = reduce_z(chip_sums[1])

    hg = head_gains.T
    step0 = project_back(
        place, dqkv[0], projected[0][1], cos, sin, hg, x, turned[0][1], mixer_mine, mixer_other, gains_all, 0, None
    )
    before = (projected[1][2], projected[0][2], step0[1], small, step0[2], step0[3], step0[0])
    dqkv[1], z0, z1 = together(after(dqkv[1], step0[0]), z0, z1)
    dx1, gm, go = project_back(
        place, dqkv[1], projected[1][1], cos, sin, hg, x, turned[1][1], mixer_mine, mixer_other, gains_all, 1, before
    )
    gm, chip_sums[2] = together(gm, chip_sums[2])
    gradients = [z0, z1, reduce_z(chip_sums[2])]
    output_gradient = gradients[2][-per:]
    gradients[2] = gradients[2][:-per]
    last = reduce_chips(add_up(gm, across(go)))
    expand_gradient, shrink_gradient = units_apart(jnp.concatenate(gradients, axis=0), per)
    last = after(last, dx1)
    last = reduce_z(last)
    wide = mixer_weight.shape[1]
    small = last[:, wide:]
    return (
        turned[1][0].reshape(tokens.shape),
        dx1.reshape(tokens.shape),
        heads_apart(last[:, :wide]),
        output_gradient,
        small[:, 0],
        expand_gradient,
        shrink_gradient,
        small[:, 1],
        small[:, 2:6].T.reshape(2, 2 * per),
        jnp.sqrt(small[:3, 6] / (device_count * count * d)),
    )


def passed_along(block, axis, distance):
    devices = range(lax.axis_size(axis))
    route = [((i - distance) % len(devices), i) for i in devices]
    return lax.ppermute(block, axis, route)


def normalize_rows(values):
    factor = lax.rsqrt(jnp.mean(values * values, axis=-1, keepdims=True) + epsilon)
    return (values * factor, factor)


def normalize_back(values, factor, upstream):
    inner_mean = jnp.mean(upstream * values, axis=-1, keepdims=True)
    return factor * upstream - values * (factor * factor * factor) * inner_mean


def rotary_tables(positions, head_size):
    halfway = head_size // 2
    inverse = rope_base ** (-(jnp.arange(halfway, dtype=jnp.float32) * 2.0 / head_size))
    angles = positions.astype(jnp.float32)[..., None] * inverse
    angles = jnp.concatenate([angles, angles], axis=-1)
    return (jnp.cos(angles), jnp.sin(angles))


def rotate(values, cosine_table, sine_table):
    halfway = values.shape[-1] // 2
    turned = jnp.concatenate([-values[..., halfway:], values[..., :halfway]], axis=-1)
    return values * cosine_table + turned * sine_table


def rotate_back(upstream, cosine_table, sine_table):
    halfway = upstream.shape[-1] // 2
    scaled = upstream * sine_table
    turned = jnp.concatenate([scaled[..., halfway:], -scaled[..., :halfway]], axis=-1)
    return upstream * cosine_table + turned


def document_positions(own_documents, all_documents, offset_rows):
    earlier = jnp.sum(
        (all_documents[:, None, :] < own_documents[:, :, None]).astype(jnp.int32), axis=2
    )
    index_rows = offset_rows + jnp.arange(own_documents.shape[1], dtype=jnp.int32)
    return index_rows[None, :] - earlier


def allowed_pairs(query_docs, key_docs, query_index, key_index):
    same_document = query_docs[:, :, None] == key_docs[:, None, :]
    causal = query_index[:, None] >= key_index[None, :]
    return jnp.logical_and(same_document, causal[None, :, :])[:, None, None, :, :]


def column_product(left, right):
    return jnp.einsum("nd,nf->df", left, right, preferred_element_type=jnp.float32)


def per_device(
    tokens,
    document_ids,
    mixer_weight,
    output_weight,
    mixer_gain,
    expand_weight,
    shrink_weight,
    feed_gain,
    head_gains,
    cotangent,
):
    sequence_count, sequence_rows, model_width = tokens.shape
    count_of_tokens = sequence_count * sequence_rows
    query_groups = QUERY_HEADS // KEY_VALUE_HEADS
    query_feature_width = QUERY_HEADS * HEAD_DIMENSION
    key_feature_width = KEY_VALUE_HEADS * HEAD_DIMENSION
    cycle_size = lax.axis_size("ctx")
    cycle_index = lax.axis_index("ctx")
    device_count = lax.axis_size("ctx") * lax.axis_size("fsdp")
    owner_slot = lax.axis_index(("ctx", "fsdp"))
    gain_rows = mixer_gain.shape[0]
    offset_rows = cycle_index * sequence_rows
    all_documents = lax.all_gather(document_ids, "ctx", axis=1, tiled=True)
    positions = document_positions(document_ids, all_documents, offset_rows)
    cosine_table, sine_table = rotary_tables(positions.reshape(count_of_tokens), HEAD_DIMENSION)
    cosine_table = cosine_table[:, None, :]
    sine_table = sine_table[:, None, :]
    query_index = offset_rows + jnp.arange(sequence_rows, dtype=jnp.int32)
    mixer_all, output_all, mixer_gain_all = (
        lax.all_gather(mixer_weight, ("ctx", "fsdp"), axis=0, tiled=True),
        lax.all_gather(output_weight, ("ctx", "fsdp"), axis=0, tiled=True),
        lax.all_gather(mixer_gain, ("ctx", "fsdp"), axis=0, tiled=True),
    )
    stream = tokens.reshape(count_of_tokens, model_width).astype(jnp.float32)
    unit_in, factor_in = normalize_rows(stream)
    normed_in = (unit_in * mixer_gain_all.astype(jnp.float32)).astype(jnp.bfloat16)
    projected_heads = jnp.dot(normed_in, mixer_all, preferred_element_type=jnp.float32)
    query_raw = projected_heads[:, :query_feature_width].reshape(
        count_of_tokens, QUERY_HEADS, HEAD_DIMENSION
    )
    unrotated_key = projected_heads[
        :, query_feature_width : query_feature_width + key_feature_width
    ].reshape(count_of_tokens, KEY_VALUE_HEADS, HEAD_DIMENSION)
    value_rows = projected_heads[:, query_feature_width + key_feature_width :].astype(jnp.bfloat16)
    query_unit, query_factor = normalize_rows(query_raw)
    key_unit, key_factor = normalize_rows(unrotated_key)
    query_row_block = rotate(query_unit * head_gains[0], cosine_table, sine_table).astype(
        jnp.bfloat16
    )
    key_rows = rotate(key_unit * head_gains[1], cosine_table, sine_table).astype(jnp.bfloat16)
    query_head_rows = query_row_block.reshape(
        sequence_count, sequence_rows, KEY_VALUE_HEADS, query_groups, HEAD_DIMENSION
    ).transpose(0, 2, 3, 1, 4)
    key_send = key_rows.reshape(sequence_count, sequence_rows, key_feature_width)
    value_send = value_rows.reshape(sequence_count, sequence_rows, key_feature_width)
    statistics_shape = (sequence_count, KEY_VALUE_HEADS, query_groups, sequence_rows)
    initial = (
        jnp.full(statistics_shape, masked_score, jnp.float32),
        jnp.zeros(statistics_shape, jnp.float32),
        jnp.zeros(statistics_shape + (HEAD_DIMENSION,), jnp.float32),
    )
    carried = initial
    key_portion = lax.all_gather(key_send, "ctx", axis=1, tiled=True)
    value_portion = lax.all_gather(value_send, "ctx", axis=1, tiled=True)
    piece_rows = key_portion.shape[1]
    block_extent = math.gcd(piece_rows, 512)
    count_of_blocks = piece_rows // block_extent
    split_key_blocks = jnp.moveaxis(
        key_portion.reshape(
            sequence_count, count_of_blocks, block_extent, KEY_VALUE_HEADS, HEAD_DIMENSION
        ),
        1,
        0,
    )
    value_blocks = jnp.moveaxis(
        value_portion.reshape(
            sequence_count, count_of_blocks, block_extent, KEY_VALUE_HEADS, HEAD_DIMENSION
        ),
        1,
        0,
    )
    block_starts = jnp.arange(count_of_blocks, dtype=jnp.int32) * block_extent

    def one_block(running, block_items):
        current_key_block, current_value_block, block_start = block_items
        row_max, total_weight, weighted_sum = running
        key_docs = lax.dynamic_slice_in_dim(all_documents, block_start, block_extent, 1)
        key_index = block_start + jnp.arange(block_extent, dtype=jnp.int32)
        allowed = allowed_pairs(document_ids, key_docs, query_index, key_index)
        scores = (
            jnp.einsum(
                "skgrd,sjkd->skgrj",
                query_head_rows,
                current_key_block,
                preferred_element_type=jnp.float32,
            )
            * 0.125
        )
        masked = jnp.where(allowed, scores, masked_score)
        new_max = jnp.maximum(row_max, jnp.max(masked, axis=-1))
        rescale = jnp.exp(row_max - new_max)
        softmax_terms = jnp.where(allowed, jnp.exp(masked - new_max[..., None]), 0.0)
        total_weight = total_weight * rescale + jnp.sum(softmax_terms, axis=-1)
        weighted_sum = weighted_sum * rescale[..., None] + jnp.einsum(
            "skgrj,sjkd->skgrd",
            softmax_terms.astype(jnp.bfloat16),
            current_value_block,
            preferred_element_type=jnp.float32,
        )
        return ((new_max, total_weight, weighted_sum), None)

    carried, _ = lax.scan(one_block, carried, (split_key_blocks, value_blocks, block_starts))
    row_max, total_weight, weighted_sum = carried
    attn_heads = weighted_sum / total_weight[..., None]
    log_total = row_max + jnp.log(total_weight)
    attended = attn_heads.transpose(0, 3, 1, 2, 4).reshape(count_of_tokens, query_feature_width)
    attended_low = attended.astype(jnp.bfloat16)
    attn_branch = jnp.dot(attended_low, output_all, preferred_element_type=jnp.float32)
    middle = stream + attn_branch
    expand_all, shrink_all, feed_gain_all = (
        lax.all_gather(expand_weight, ("ctx", "fsdp"), axis=0, tiled=True),
        lax.all_gather(shrink_weight, ("ctx", "fsdp"), axis=0, tiled=True),
        lax.all_gather(feed_gain, ("ctx", "fsdp"), axis=0, tiled=True),
    )
    unit_mid, factor_mid = normalize_rows(middle)
    normed_mid = (unit_mid * feed_gain_all.astype(jnp.float32)).astype(jnp.bfloat16)
    gate_up = jnp.dot(normed_mid, expand_all, preferred_element_type=jnp.float32)
    gate_rows = gate_up[:, :FF]
    up_rows = gate_up[:, FF:]
    gate_sigmoid = jax.nn.sigmoid(gate_rows)
    gate_silu = gate_rows * gate_sigmoid
    hidden = (gate_silu * up_rows).astype(jnp.bfloat16)
    feed_branch = jnp.dot(hidden, shrink_all, preferred_element_type=jnp.float32)
    layer_out = middle + feed_branch
    squares = jnp.stack(
        [
            jnp.sum(attn_branch * attn_branch),
            jnp.sum(feed_branch * feed_branch),
            jnp.sum(layer_out * layer_out),
        ]
    )
    stat_totals = lax.psum(squares, ("ctx", "fsdp"))
    grad_branch = cotangent.reshape(count_of_tokens, model_width)
    grad_result = grad_branch.astype(jnp.float32)
    shrink_gradient = lax.psum_scatter(
        column_product(hidden, grad_branch), ("ctx", "fsdp"), scatter_dimension=0, tiled=True
    )
    grad_hidden = jnp.einsum(
        "nd,fd->nf", grad_branch, shrink_all, preferred_element_type=jnp.float32
    )
    grad_gate = grad_hidden * up_rows * gate_sigmoid * (1.0 + gate_rows * (1.0 - gate_sigmoid))
    grad_up = grad_hidden * gate_silu
    grad_gate_up = jnp.concatenate([grad_gate, grad_up], axis=1).astype(jnp.bfloat16)
    expand_gradient = lax.psum_scatter(
        column_product(normed_mid, grad_gate_up), ("ctx", "fsdp"), scatter_dimension=0, tiled=True
    )
    grad_normed_mid = jnp.einsum(
        "nf,df->nd", grad_gate_up, expand_all, preferred_element_type=jnp.float32
    )
    feed_gain_term = jnp.sum(grad_normed_mid * unit_mid, axis=0)
    grad_middle = grad_result + normalize_back(
        middle, factor_mid, grad_normed_mid * feed_gain_all.astype(jnp.float32)
    )
    grad_attn_low = grad_middle.astype(jnp.bfloat16)
    output_gradient = lax.psum_scatter(
        column_product(attended_low, grad_attn_low),
        ("ctx", "fsdp"),
        scatter_dimension=0,
        tiled=True,
    )
    attended_gradient = jnp.einsum(
        "nd,qd->nq", grad_attn_low, output_all, preferred_element_type=jnp.float32
    ).astype(jnp.bfloat16)
    heads_gradient = attended_gradient.reshape(
        sequence_count, sequence_rows, KEY_VALUE_HEADS, query_groups, HEAD_DIMENSION
    ).transpose(0, 2, 3, 1, 4)
    delta_rows = jnp.sum(heads_gradient.astype(jnp.float32) * attn_heads, axis=-1)
    zero_query = jnp.zeros(query_head_rows.shape, jnp.float32)

    def pair_terms(current_key_block, current_value_block, block_start):
        rows_per_block = current_key_block.shape[1]
        key_reshaped = current_key_block.reshape(
            sequence_count, rows_per_block, KEY_VALUE_HEADS, HEAD_DIMENSION
        )
        value_reshaped = current_value_block.reshape(
            sequence_count, rows_per_block, KEY_VALUE_HEADS, HEAD_DIMENSION
        )
        key_docs = lax.dynamic_slice_in_dim(all_documents, block_start, rows_per_block, 1)
        key_index = block_start + jnp.arange(rows_per_block, dtype=jnp.int32)
        allowed = allowed_pairs(document_ids, key_docs, query_index, key_index)
        scores = (
            jnp.einsum(
                "skgrd,sjkd->skgrj",
                query_head_rows,
                key_reshaped,
                preferred_element_type=jnp.float32,
            )
            * 0.125
        )
        probability = jnp.where(
            allowed, jnp.exp(jnp.where(allowed, scores, 0.0) - log_total[..., None]), 0.0
        )
        value_term = jnp.einsum(
            "skgrj,skgrd->sjkd",
            probability.astype(jnp.bfloat16),
            heads_gradient,
            preferred_element_type=jnp.float32,
        )
        grad_probability = jnp.einsum(
            "skgrd,sjkd->skgrj", heads_gradient, value_reshaped, preferred_element_type=jnp.float32
        )
        grad_scores = (probability * (grad_probability - delta_rows[..., None])).astype(
            jnp.bfloat16
        )
        query_term = (
            jnp.einsum(
                "skgrj,sjkd->skgrd", grad_scores, key_reshaped, preferred_element_type=jnp.float32
            )
            * 0.125
        )
        key_term = (
            jnp.einsum(
                "skgrj,skgrd->sjkd",
                grad_scores,
                query_head_rows,
                preferred_element_type=jnp.float32,
            )
            * 0.125
        )
        return (
            query_term,
            key_term.reshape(sequence_count, rows_per_block, key_feature_width),
            value_term.reshape(sequence_count, rows_per_block, key_feature_width),
        )

    zero_keys = jnp.zeros((sequence_count, sequence_rows, key_feature_width), jnp.float32)

    def cycle_step(cycle_turn, running):
        (
            current_key_block,
            current_value_block,
            key_gradient_accumulator,
            value_accum,
            query_accum,
        ) = running
        owner_index = (cycle_index - cycle_turn) % cycle_size
        query_term, key_term, value_term = pair_terms(
            current_key_block.astype(jnp.bfloat16),
            current_value_block.astype(jnp.bfloat16),
            owner_index * sequence_rows,
        )
        query_accum = query_accum + query_term
        key_gradient_accumulator = key_gradient_accumulator + key_term
        value_accum = value_accum + value_term
        current_key_block, current_value_block, key_gradient_accumulator, value_accum = (
            passed_along(current_key_block.astype(jnp.bfloat16), "ctx", 1).astype(
                current_key_block.dtype
            ),
            passed_along(current_value_block.astype(jnp.bfloat16), "ctx", 1).astype(
                current_value_block.dtype
            ),
            passed_along(key_gradient_accumulator.astype(jnp.bfloat16), "ctx", 1).astype(
                key_gradient_accumulator.dtype
            ),
            passed_along(value_accum.astype(jnp.bfloat16), "ctx", 1).astype(value_accum.dtype),
        )
        return (
            current_key_block,
            current_value_block,
            key_gradient_accumulator,
            value_accum,
            query_accum,
        )

    carried = lax.fori_loop(
        0,
        cycle_size,
        cycle_step,
        (
            key_send.astype(jnp.float32),
            value_send.astype(jnp.float32),
            zero_keys,
            zero_keys,
            zero_query,
        ),
    )
    key_gradient_accumulator, value_accum, query_accum = (carried[2], carried[3], carried[4])
    grad_query = query_accum.transpose(0, 3, 1, 2, 4).reshape(
        count_of_tokens, QUERY_HEADS, HEAD_DIMENSION
    )
    key_grad_total = key_gradient_accumulator.reshape(
        count_of_tokens, KEY_VALUE_HEADS, HEAD_DIMENSION
    )
    grad_value = value_accum.reshape(count_of_tokens, key_feature_width)
    grad_query_pre = rotate_back(grad_query, cosine_table, sine_table)
    grad_key_pre = rotate_back(key_grad_total, cosine_table, sine_table)
    head_terms = jnp.stack(
        [
            jnp.sum(grad_query_pre * query_unit, axis=(0, 1)),
            jnp.sum(grad_key_pre * key_unit, axis=(0, 1)),
        ]
    )
    grad_query_raw = normalize_back(query_raw, query_factor, grad_query_pre * head_gains[0])
    grad_key_raw = normalize_back(unrotated_key, key_factor, grad_key_pre * head_gains[1])
    grad_projected = jnp.concatenate(
        [
            grad_query_raw.reshape(count_of_tokens, query_feature_width),
            grad_key_raw.reshape(count_of_tokens, key_feature_width),
            grad_value,
        ],
        axis=1,
    ).astype(jnp.bfloat16)
    mixer_gradient = lax.psum_scatter(
        column_product(normed_in, grad_projected), ("ctx", "fsdp"), scatter_dimension=0, tiled=True
    )
    grad_normed_in = jnp.einsum(
        "nq,dq->nd", grad_projected, mixer_all, preferred_element_type=jnp.float32
    )
    mixer_gain_term = jnp.sum(grad_normed_in * unit_in, axis=0)
    grad_stream = grad_middle + normalize_back(
        stream, factor_in, grad_normed_in * mixer_gain_all.astype(jnp.float32)
    )
    feed_gain_total, mixer_gain_total, head_total = lax.psum(
        (feed_gain_term, mixer_gain_term, head_terms), ("ctx", "fsdp")
    )
    feed_gain_gradient = lax.dynamic_slice_in_dim(
        feed_gain_total, owner_slot * gain_rows, gain_rows, 0
    )
    mixer_gain_gradient = lax.dynamic_slice_in_dim(
        mixer_gain_total, owner_slot * gain_rows, gain_rows, 0
    )
    statistics = jnp.sqrt(stat_totals / (device_count * count_of_tokens * model_width))
    result = layer_out.astype(jnp.bfloat16).reshape(sequence_count, sequence_rows, model_width)
    tokens_gradient = grad_stream.astype(jnp.bfloat16).reshape(
        sequence_count, sequence_rows, model_width
    )
    return (
        result,
        tokens_gradient,
        mixer_gradient,
        output_gradient,
        mixer_gain_gradient,
        expand_gradient,
        shrink_gradient,
        feed_gain_gradient,
        head_total,
        statistics,
    )


def solution(mesh):
    function, ring = per_device, "ctx"
    if mesh.shape["ctx"] == KEY_VALUE_HEADS:
        shape = (KEY_VALUE_HEADS // 2, 2, mesh.shape["fsdp"])
        mesh = jax.sharding.Mesh(mesh.devices.reshape(shape), ("chip", "core", "fsdp"))
        function, ring = heads_per_device, ("chip", "core")
    every = (ring, "fsdp") if isinstance(ring, str) else ring + ("fsdp",)
    tokens, rows, vector = P("fsdp", ring, None), P(every, None), P(every)
    return jax.shard_map(
        function,
        mesh=mesh,
        in_specs=(
            tokens,
            P("fsdp", ring),
            rows,
            rows,
            vector,
            rows,
            rows,
            vector,
            P(),
            tokens,
        ),
        out_specs=(tokens, tokens, rows, rows, vector, rows, rows, vector, P(), P()),
        check_vma=False,
    )
```

```python
import functools
import math

import jax
import jax.numpy as jnp
from jax import lax
from jax.experimental import pallas as pl
from jax.experimental.pallas import tpu as pltpu
from jax.sharding import PartitionSpec as P

QUERY_HEADS = 16
KEY_VALUE_HEADS = 8
HEAD_DIMENSION = 64
FF = 4608

epsilon = 1e-05
rope_base = 1000000.0
masked_score = -1e30
LOG2E = math.log2(math.e)
QUERY_SCALE = 0.125 * LOG2E
MASK = 256.0
VMEM = 60 * 2**20
BF, F32 = jnp.bfloat16, jnp.float32

NN = (((1,), (0,)), ((), ()))
NT = (((1,), (1,)), ((), ()))
TN = (((0,), (0,)), ((), ()))


def dot(a, b, dims=NN):
    return lax.dot_general(a, b, dims, preferred_element_type=F32)


def params(**kw):
    return pltpu.CompilerParams(vmem_limit_bytes=VMEM, **kw)


def cost(flops, nbytes):
    return pl.CostEstimate(flops=int(0.001 * flops), bytes_accessed=int(0.001 * nbytes), transcendentals=0)


def flat(x):
    return x.reshape(-1, x.shape[-1])


def both(mine, other):
    return jnp.concatenate([flat(mine), flat(other)], axis=0)


def order(core, chips):
    return [a * 2 + core for a in range(chips)] + [a * 2 + 1 - core for a in range(chips)]


def lanes(n, width=128):
    return pl.ds(pl.multiple_of(n * width, width), width)


SMALL = pl.BlockSpec(memory_space=pltpu.SMEM)


def fixed(*shape):
    return pl.BlockSpec(shape, lambda *i: (0,) * len(shape), pipeline_mode=pl.Buffered(1))


def halves(w, rows, index, **kw):
    if isinstance(w, tuple):
        block = (*w[0].shape[:2], rows, w[0].shape[-1])
        spec = pl.BlockSpec(block, lambda i, place: (0, 0, index(i), 0), **kw)
        return list(w), [spec, spec]
    block = (w.shape[0], None, w.shape[2], rows, w.shape[-1])
    return [w, w], [
        pl.BlockSpec(block, lambda i, place: (0, place[0], 0, index(i), 0), **kw),
        pl.BlockSpec(block, lambda i, place: (0, 1 - place[0], 0, index(i), 0), **kw),
    ]


def project_kernel(
    place_ref, x_ref, wm_ref, wo_ref, cos_ref, sin_ref, hg_ref, qkv_ref, raw_ref, nx_ref, gains_ref, nxt, grow
):
    core = place_ref[0]
    chips = wm_ref.shape[0]
    kv = KEY_VALUE_HEADS
    wide = kv * 256
    g = both(wm_ref[:, :, :, wide:], wo_ref[:, :, :, wide:]).astype(F32).T[0:8]
    for n, at in enumerate(order(core, chips)):
        grow[:, lanes(at)] = g[:, n * 128 : (n + 1) * 128]
    gains_ref[...] = grow[...]
    x = x_ref[...].astype(F32)
    r = lax.rsqrt(jnp.mean(x * x, axis=-1, keepdims=True) + epsilon)
    nx = (x * r * grow[0:1]).astype(BF)
    nx_ref[...] = nx
    bt = x.shape[0]
    nxt[...] = nx.T.reshape(nxt.shape)
    xt = jnp.concatenate([nxt[at] for at in order(core, chips)], axis=0)
    cos, sin = cos_ref[...], sin_ref[...]
    hd, half = HEAD_DIMENSION, HEAD_DIMENSION // 2
    gains = [jnp.broadcast_to(hg_ref[:, j : j + 1], (hd, bt)) for j in (0, 1)]
    for h in range(kv):
        cols = slice(h * 256, (h + 1) * 256)
        p = dot(both(wm_ref[:, :, :, cols], wo_ref[:, :, :, cols]), xt, TN)
        raw_ref[h] = p.astype(BF)
        for slot in range(3):
            v = p[slot * hd : (slot + 1) * hd]
            factor = lax.rsqrt(jnp.mean(v * v, axis=0, keepdims=True) + epsilon)
            u = v * factor * gains[0 if slot < 2 else 1]
            a, b = u[:half], u[half:]
            qkv_ref[h, slot * hd : slot * hd + half, :] = (a * cos - b * sin).astype(BF)
            qkv_ref[h, slot * hd + half : (slot + 1) * hd, :] = (b * cos + a * sin).astype(BF)
        qkv_ref[h, 3 * hd :, :] = p[3 * hd :].astype(BF)


def project(place, x, mine, other, cos, sin, hg, seq, bt):
    d = x.shape[1]
    kv = KEY_VALUE_HEADS
    turns = pl.BlockSpec((32, bt), lambda i: (0, seq))
    return pl.pallas_call(
        project_kernel,
        grid=(1,),
        in_specs=[
            SMALL,
            pl.BlockSpec((bt, d), lambda i: (seq, 0)),
            fixed(*mine.shape),
            fixed(*mine.shape),
            turns,
            turns,
            fixed(64, 2),
        ],
        out_specs=[fixed(kv, 256, bt), fixed(kv, 256, bt), fixed(bt, d), fixed(8, d)],
        out_shape=[
            jax.ShapeDtypeStruct((kv, 256, bt), BF),
            jax.ShapeDtypeStruct((kv, 256, bt), BF),
            jax.ShapeDtypeStruct((bt, d), BF),
            jax.ShapeDtypeStruct((8, d), F32),
        ],
        scratch_shapes=[pltpu.VMEM((d // 128, 128, bt), BF), pltpu.VMEM((8, d), F32)],
        compiler_params=params(),
        cost_estimate=cost(2 * bt * d * kv * 256, 14e6),
        name="project",
    )(place, x, mine, other, cos, sin, hg)


def first_start(starts_ref, s, t):
    out = jnp.int32(0)
    for d in range(1, 4):
        b = starts_ref[s * 4 + d]
        out = jnp.where(t >= b, b, out)
    return out


def next_start(starts_ref, s, t, total):
    out = jnp.int32(total)
    for d in range(3, 0, -1):
        b = starts_ref[s * 4 + d]
        out = jnp.where(t < b, b, out)
    return out


def member(starts_ref, s, base, rows, width, total):
    pos = base + lax.broadcasted_iota(jnp.int32, (rows, width), 1)
    row = lax.broadcasted_iota(jnp.int32, (rows, width), 0)
    out = jnp.zeros((rows, width), F32)
    for d in range(4):
        lo = starts_ref[s * 4 + d]
        hi = starts_ref[s * 4 + d + 1] if d < 3 else jnp.int32(total)
        out = jnp.where((row == d) & (pos >= lo) & (pos < hi), 1.0, out)
    return out


def attend_kernel(starts_ref, q_ref, seq_ref, out_ref, lse_ref, kx, vt, acc):
    s, i = pl.program_id(0), pl.program_id(1)
    blocks, _, width = seq_ref.shape
    total = blocks * width

    @pl.when(i == 0)
    def _():
        for j in range(blocks):
            aux = member(starts_ref, s, j * width, 64, width, total)
            kk = jnp.concatenate([seq_ref[j, 128:192, :].astype(F32), aux], axis=0)
            kx[j] = kk.T.astype(BF)
            vt[j, 0:64, :] = seq_ref[j, 192:256, :]
            ones = (lax.broadcasted_iota(jnp.int32, (16, width), 0) == 0).astype(F32)
            vt[j, 64:80, :] = ones.astype(BF)

    aux = ((member(starts_ref, s, i * width, 64, width, total) - 1.0) * MASK).astype(BF)
    row = lax.broadcasted_iota(jnp.int32, (64, width), 0)
    aux = jnp.where(row < 4, aux.astype(F32), 0.0).astype(BF)
    q = [jnp.concatenate([q_ref[0, g * 64 : g * 64 + 64, :], aux], axis=0) for g in (0, 1)]
    acc[...] = jnp.zeros_like(acc)

    def block(j, diagonal):
        k, v = kx[j], vt[j]
        sc = [dot(k, q[g]) for g in (0, 1)]
        if diagonal:
            keep = lax.broadcasted_iota(jnp.int32, (width, width), 0) <= lax.broadcasted_iota(
                jnp.int32, (width, width), 1
            )
            sc = [jnp.where(keep, x, -MASK) for x in sc]
        p = [jnp.exp2(x).astype(BF) for x in sc]
        for g in (0, 1):
            acc[g] += dot(v, p[g])

    lo = first_start(starts_ref, s, i * width) // width
    lax.fori_loop(lo, i, lambda j, c: (block(j, False), c)[1], 0)
    block(i, True)
    for g in (0, 1):
        a = acc[g]
        total_weight = a[64:65]
        out_ref[0, g * 64 : g * 64 + 64, :] = (a[0:64] / total_weight).astype(BF)
        lse_ref[0, g : g + 1, :] = jnp.log2(total_weight)
    lse_ref[0, 2:8, :] = jnp.zeros((6, width), F32)


def attend(starts, qkv, seqs=1):
    blocks, _, rows = qkv.shape
    width = rows // seqs
    return pl.pallas_call(
        attend_kernel,
        grid_spec=pltpu.PrefetchScalarGridSpec(
            num_scalar_prefetch=1,
            grid=(seqs, blocks),
            in_specs=[
                pl.BlockSpec((1, 256, width), lambda s, i, st: (i, 0, s)),
                pl.BlockSpec((blocks, 256, width), lambda s, i, st: (0, 0, s)),
            ],
            out_specs=[
                pl.BlockSpec((1, 128, width), lambda s, i, st: (i, 0, s)),
                pl.BlockSpec((1, 8, width), lambda s, i, st: (i, 0, s)),
            ],
            scratch_shapes=[
                pltpu.VMEM((blocks, width, 128), BF),
                pltpu.VMEM((blocks, 80, width), BF),
                pltpu.VMEM((2, 80, width), F32),
            ],
        ),
        out_shape=[
            jax.ShapeDtypeStruct((blocks, 128, rows), BF),
            jax.ShapeDtypeStruct((blocks, 8, rows), F32),
        ],
        compiler_params=params(),
        cost_estimate=cost(30e9, 4e6),
        name="attend",
    )(starts, qkv, qkv)


def split3(x):
    hi = x.astype(BF).astype(F32)
    mid = (x - hi).astype(BF).astype(F32)
    return hi, mid, x - hi - mid


def attend_back_kernel(
    starts_ref, seq_ref, do_ref, o_ref, lse_ref, out_ref, kx, vx, qx, dox, dq, dk, dv
):
    s, j = pl.program_id(0), pl.program_id(1)
    blocks, _, width = seq_ref.shape
    total = blocks * width

    @pl.when(j == 0)
    def _():
        row = lax.broadcasted_iota(jnp.int32, (64, width), 0)
        minus = jnp.where((row >= 4) & (row < 7), -1.0, 0.0)
        for b in range(blocks):
            mem = member(starts_ref, s, b * width, 64, width, total)
            aux = mem + minus
            kk = jnp.concatenate([seq_ref[b, 128:192, :].astype(F32), aux], axis=0)
            kx[b] = kk.T.astype(BF)
            vv = jnp.concatenate([seq_ref[b, 192:256, :].astype(F32), minus], axis=0)
            vx[b] = vv.T.astype(BF)
            qmask = jnp.where(row < 4, (mem - 1.0) * MASK, 0.0)
            for g in (0, 1):
                h1, h2, h3 = split3(lse_ref[b, g : g + 1, :])
                ax = jnp.where(row == 4, h1, jnp.where(row == 5, h2, jnp.where(row == 6, h3, qmask)))
                qx[b, g, 0:64, :] = seq_ref[b, g * 64 : g * 64 + 64, :]
                qx[b, g, 64:128, :] = ax.astype(BF)
                d_out = do_ref[b, g * 64 : g * 64 + 64, :]
                out = o_ref[b, g * 64 : g * 64 + 64, :]
                delta = jnp.sum(d_out.astype(F32) * out.astype(F32), axis=0, keepdims=True)
                h1, h2, h3 = split3(delta)
                ax = jnp.where(row == 4, h1, jnp.where(row == 5, h2, jnp.where(row == 6, h3, 0.0)))
                dox[b, g, 0:64, :] = d_out
                dox[b, g, 64:128, :] = ax.astype(BF)
        dq[...] = jnp.zeros_like(dq)

    dk[...] = jnp.zeros_like(dk)
    dv[...] = jnp.zeros_like(dv)
    k, v, ktr = kx[j], vx[j], seq_ref[j, 128:192, :]

    def block(i, diagonal):
        sc = [dot(k, qx[i, g]) for g in (0, 1)]
        dp = [dot(v, dox[i, g]) for g in (0, 1)]
        if diagonal:
            keep = lax.broadcasted_iota(jnp.int32, (width, width), 0) <= lax.broadcasted_iota(
                jnp.int32, (width, width), 1
            )
            sc = [jnp.where(keep, x, -MASK) for x in sc]
        p = [jnp.exp2(x) for x in sc]
        ds = [(p[g] * dp[g]).astype(BF) for g in (0, 1)]
        pb = [x.astype(BF) for x in p]
        for g in (0, 1):
            dv[...] += dot(dox[i, g, 0:64, :], pb[g], NT)
            dk[...] += dot(qx[i, g, 0:64, :], ds[g], NT)
            dq[i, g] += dot(ktr, ds[g])

    block(j, True)
    hi = (next_start(starts_ref, s, j * width + width - 1, total) - 1) // width
    lax.fori_loop(j + 1, hi + 1, lambda i, c: (block(i, False), c)[1], 0)
    out_ref[j, 128:192, :] = (dk[...] * (0.125 / QUERY_SCALE)).astype(BF)
    out_ref[j, 192:256, :] = dv[...].astype(BF)

    @pl.when(j == blocks - 1)
    def _():
        for b in range(blocks):
            for g in (0, 1):
                out_ref[b, g * 64 : g * 64 + 64, :] = (dq[b, g] * 0.125).astype(BF)


def attend_back(starts, qkv, d_out, out, lse, seqs=1):
    blocks, _, rows = qkv.shape
    width = rows // seqs
    whole = lambda n: pl.BlockSpec((blocks, n, width), lambda s, j, st: (0, 0, s))
    return pl.pallas_call(
        attend_back_kernel,
        grid_spec=pltpu.PrefetchScalarGridSpec(
            num_scalar_prefetch=1,
            grid=(seqs, blocks),
            in_specs=[whole(256), whole(128), whole(128), whole(8)],
            out_specs=whole(256),
            scratch_shapes=[
                pltpu.VMEM((blocks, width, 128), BF),
                pltpu.VMEM((blocks, width, 128), BF),
                pltpu.VMEM((blocks, 2, 128, width), BF),
                pltpu.VMEM((blocks, 2, 128, width), BF),
                pltpu.VMEM((blocks, 2, 64, width), F32),
                pltpu.VMEM((64, width), F32),
                pltpu.VMEM((64, width), F32),
            ],
        ),
        out_shape=jax.ShapeDtypeStruct((blocks, 256, rows), BF),
        compiler_params=params(),
        cost_estimate=cost(60e9, 6e6),
        name="attend_back",
    )(starts, qkv, d_out, out, lse)


def middle_kernel(place_ref, x_ref, at_ref, wm_ref, wo_ref, gains_ref, mid_ref, nm_ref, sq_ref):
    core = place_ref[0]
    a = jnp.concatenate([at_ref[at] for at in order(core, wm_ref.shape[0])], axis=0)
    branch = dot(a, both(wm_ref[...], wo_ref[...]), TN)
    mid = x_ref[...].astype(F32) + branch
    mid_ref[...] = mid
    r = lax.rsqrt(jnp.mean(mid * mid, axis=-1, keepdims=True) + epsilon)
    nm_ref[...] = (mid * r * gains_ref[1:2]).astype(BF)
    sq_ref[...] = jnp.zeros_like(sq_ref)
    sq_ref[0:1, :] = jnp.sum(branch * branch, axis=0, keepdims=True)


def output_rows(w):
    rows = w.shape[3]
    return halves(w, 32, lambda i: rows // 32 - 1, pipeline_mode=pl.Buffered(1))


def middle(place, x, at, w, gains, seq):
    d = x.shape[1]
    heads, n, bt = at.shape
    arrays, specs = output_rows(w)
    return pl.pallas_call(
        middle_kernel,
        grid_spec=pltpu.PrefetchScalarGridSpec(
            num_scalar_prefetch=1,
            grid=(1,),
            in_specs=[pl.BlockSpec((bt, d), lambda i, p: (seq, 0)), fixed(heads, n, bt), *specs, fixed(8, d)],
            out_specs=[fixed(bt, d), fixed(bt, d), fixed(8, d)],
        ),
        out_shape=[
            jax.ShapeDtypeStruct((bt, d), F32),
            jax.ShapeDtypeStruct((bt, d), BF),
            jax.ShapeDtypeStruct((8, d), F32),
        ],
        compiler_params=params(),
        cost_estimate=cost(2 * bt * d * heads * n, 7e6),
        name="middle",
    )(place, x, at, *arrays, gains)


def feed_kernel(*refs, first, steps, parts):
    place_ref, n0_ref, n1_ref, c_ref = refs[:4]
    count = 2 * steps if parts else 2
    weights, refs = refs[4 : 4 + count], refs[4 + count :]
    if not first:
        fb_in, dn_in = refs[:2]
        refs = refs[2:]
    fb_ref, dn_ref, gm_ref, go_ref, nm, nmt, wscr, wsscr, hid, dgu, gsscr = refs
    f = pl.program_id(0)
    core, z = place_ref[0], place_ref[1]
    _, chips, _, per, d = wscr.shape
    rows = gm_ref.shape[2]
    unit = rows - per
    tokens, H = hid.shape
    bt = tokens // 2

    @pl.when(f == 0)
    def _():
        if first:
            fb_ref[...] = jnp.zeros_like(fb_ref)
            dn_ref[...] = jnp.zeros_like(dn_ref)
        else:
            fb_ref[...] = fb_in[...]
            dn_ref[...] = dn_in[...]
        for s, ref in enumerate((n0_ref, n1_ref)):
            for n, at in enumerate(order(core, chips)):
                nm[s * bt : (s + 1) * bt, n * 128 : (n + 1) * 128] = ref[:, lanes(at)]
        nmt[...] = nm[...].T

    for r, c in ((0, core), (1, 1 - core)):
        if parts:
            for s in range(steps):
                at = (z - s + steps) % steps
                ref = weights[r * steps + s]
                wscr[r, :, at] = ref[:, 0:per, :]
                wsscr[c, :, at] = ref[:, per:rows, :]
        else:
            wscr[r] = weights[r][:, :, 0:per, :]
            wsscr[c] = weights[r][:, :, per:rows, :]
    w, ws = flat(wscr[...]), flat(wsscr[...])
    half = tokens // 2
    for t in range(2):
        ts = slice(t * half, (t + 1) * half)
        gate_up = dot(nm[ts, :], w)
        gate, up = gate_up[:, :H], gate_up[:, H:]
        dh = dot(c_ref[ts, :], ws, NT)
        sig = 0.5 * jnp.tanh(0.5 * gate) + 0.5
        silu = gate * sig
        hidden = (silu * up).astype(BF)
        hid[ts, :] = hidden
        dgu[ts, :H] = (dh * up * sig * (1.0 + gate * (1.0 - sig))).astype(BF)
        dgu[ts, H:] = (dh * silu).astype(BF)
        fb_ref[ts, :] += dot(hidden, ws)
        dn_ref[ts, :] += dot(dgu[ts, :], w, NT)
    gsscr[...] = dot(hid[...], c_ref[...], TN).astype(BF).reshape(gsscr.shape)
    for q in (0, 1):
        ge = dot(nmt[...], dgu[:, q * H : (q + 1) * H]).astype(BF).reshape(2, chips, steps, per, H)
        for n, ref in ((0, gm_ref), (1, go_ref)):
            ref[:, :, 0:per, q * H : (q + 1) * H] = ge[n]
    for n, ref in ((core, gm_ref), (1 - core, go_ref)):
        ref[:, :, per:rows, :] = gsscr[n]


def feed(place, nm, c, w, steps, units, carry, extra):
    tokens, d = c.shape
    parts = isinstance(w, tuple) and isinstance(w[0], list)
    if parts:
        arrays = w[0] + w[1]
        chips = arrays[0].shape[0]
        per = d // (chips * 2 * steps)
        specs = [pl.BlockSpec((chips, per + UNIT, d), lambda f, p: (0, f, 0))] * len(arrays)
    else:
        chips = (w[0] if isinstance(w, tuple) else w).shape[0]
        per = d // (chips * 2 * steps)
        arrays, specs = halves(w, per + UNIT, lambda f: f)
    block = pl.BlockSpec((chips, steps, per + UNIT, d), lambda f, p: (0, 0, f, 0))
    whole = fixed(tokens, d)
    first = carry is None
    hidden = chips * 2 * steps * UNIT
    at = 4 + len(arrays)
    grad = jax.ShapeDtypeStruct((chips, steps, (per + UNIT) * units + extra, d), BF)
    return pl.pallas_call(
        functools.partial(feed_kernel, first=first, steps=steps, parts=parts),
        grid_spec=pltpu.PrefetchScalarGridSpec(
            num_scalar_prefetch=1,
            grid=(units,),
            in_specs=[fixed(*nm[0].shape), fixed(*nm[1].shape), whole, *specs] + ([] if first else [whole, whole]),
            out_specs=[whole, whole, block, block],
            scratch_shapes=[
                pltpu.VMEM((tokens, d), BF),
                pltpu.VMEM((d, tokens), BF),
                pltpu.VMEM((2, chips, steps, per, d), BF),
                pltpu.VMEM((2, chips, steps, UNIT, d), BF),
                pltpu.VMEM((tokens, hidden), BF),
                pltpu.VMEM((tokens, 2 * hidden), BF),
                pltpu.VMEM((2, chips, steps, UNIT, d), BF),
            ],
        ),
        out_shape=[jax.ShapeDtypeStruct((tokens, d), F32)] * 2 + [grad, grad],
        input_output_aliases={} if first else {at: 0, at + 1: 1},
        compiler_params=params(),
        cost_estimate=cost(18 * tokens * d * hidden * units, 8e6 * units + 20e6),
        name="feed",
    )(place, *nm, c, *arrays, *(() if first else carry))


def turn_kernel(*refs, last):
    place_ref, mid_ref, fb_ref, dn_ref, c_ref, at_ref, wm_ref, wo_ref, gains_ref = refs[:9]
    refs = refs[9:]
    if last:
        at0_ref, low0_ref = refs[:2]
        res_ref, dmid_ref, da_ref, sums_ref, gm_ref, go_ref, dn_scr, acc = refs[5:]
    else:
        res_ref, dmid_ref, da_ref, sums_ref, low_ref, dn_scr = refs
    heads, n, bt = at_ref.shape
    core = place_ref[0]
    chips, steps, per, d = wm_ref.shape
    for m, at in enumerate(order(core, chips)):
        dn_scr[:, lanes(at)] = dn_ref[:, m * 128 : (m + 1) * 128]
    mid, fb, dn = mid_ref[...], fb_ref[...], dn_scr[...]
    out = mid + fb
    res_ref[...] = out.astype(BF)
    r = lax.rsqrt(jnp.mean(mid * mid, axis=-1, keepdims=True) + epsilon)
    unit = mid * r
    g = dn * gains_ref[1:2]
    dmid = c_ref[...].astype(F32) + r * (g - unit * jnp.mean(g * unit, axis=-1, keepdims=True))
    dmid_ref[...] = dmid
    low = dmid.astype(BF)
    da = dot(both(wm_ref[...], wo_ref[...]), low, NT).astype(BF).reshape(heads, n, bt)
    for m, at in enumerate(order(core, chips)):
        da_ref[at] = da[m]
    sums_ref[...] = jnp.zeros_like(sums_ref)
    sums_ref[0:1, :] = jnp.sum(dn * unit, axis=0, keepdims=True)
    sums_ref[1:2, :] = jnp.sum(fb * fb, axis=0, keepdims=True)
    sums_ref[2:3, :] = jnp.sum(out * out, axis=0, keepdims=True)
    if last:
        a = jnp.concatenate([flat(at0_ref[...]), flat(at_ref[...])], axis=1)
        lows = jnp.concatenate([low0_ref[...], low], axis=0)
        acc[...] = dot(a, lows).astype(BF).reshape(acc.shape)
        for m, ref in ((core, gm_ref), (1 - core, go_ref)):
            ref[...] = jnp.stack([acc[a * 2 + m] for a in range(chips)])
    else:
        low_ref[...] = low


def turn(place, mid, fb, dn, c, at, w, gains, seq, before):
    d = c.shape[1]
    heads, n, bt = at.shape
    chips, _, steps = w.shape[:3]
    per = d // (chips * 2 * steps)
    rows = pl.BlockSpec((bt, d), lambda i, p: (seq, 0), pipeline_mode=pl.Buffered(1))
    here = fixed(bt, d)
    arrays, specs = output_rows(w)
    last = before is not None
    shape = jax.ShapeDtypeStruct
    if last:
        grad = before[2].shape
        behind = pl.BlockSpec(
            (chips, steps, per, d), lambda i, p: (0, 0, grad[2] // per - 1, 0), pipeline_mode=pl.Buffered(1)
        )
        anywhere = pl.BlockSpec(memory_space=pl.ANY)
    return pl.pallas_call(
        functools.partial(turn_kernel, last=last),
        grid_spec=pltpu.PrefetchScalarGridSpec(
            num_scalar_prefetch=1,
            grid=(1,),
            in_specs=[here, rows, rows, rows, fixed(heads, n, bt), *specs, fixed(8, d)]
            + ([fixed(heads, n, bt), here, anywhere, anywhere, anywhere] if last else []),
            out_specs=[rows, here, fixed(heads, n, bt), fixed(8, d)] + ([behind] * 2 if last else [here]),
            scratch_shapes=[pltpu.VMEM((bt, d), F32)]
            + ([pltpu.VMEM((chips * 2, steps, per, d), BF)] if last else []),
        ),
        out_shape=[shape(c.shape, BF), shape((bt, d), F32), shape((heads, n, bt), BF), shape((8, d), F32)]
        + ([shape(grad, BF), shape(grad, BF)] if last else [shape((bt, d), BF)]),
        input_output_aliases={11: 4, 12: 5, 13: 0} if last else {},
        compiler_params=params(),
        cost_estimate=cost((6 if last else 2) * bt * d * heads * n, 15e6),
        name="turn",
    )(place, mid, fb, dn, c, at, *arrays, gains, *(before if last else ()))


def project_back_kernel(*refs, last):
    place_ref, dqkv_ref, raw_ref, cos_ref, sin_ref, hg_ref, x_ref, dmid_ref, wm_ref, wo_ref, gains_ref = refs[:11]
    refs = refs[11:]
    if last:
        nx_ref, nx0_ref, dproj0_ref, sums0_ref, rows0_ref, head0_ref = refs[:6]
        dx_ref, gm_ref, go_ref, dproj, dn_scr, acc, extra = refs[7:]
    else:
        dx_ref, dproj, rows_ref, head_ref, dn_scr = refs
    bt, d = x_ref.shape
    core = place_ref[0]
    chips, steps, per, cols = wm_ref.shape
    wide = cols - 128
    hd, half = HEAD_DIMENSION, HEAD_DIMENSION // 2
    cos, sin = cos_ref[...], sin_ref[...]
    gains = [jnp.broadcast_to(hg_ref[:, j : j + 1], (hd, bt)) for j in (0, 1)]
    head_sums = [jnp.zeros((hd, bt), F32), jnp.zeros((hd, bt), F32)]
    for h in range(KEY_VALUE_HEADS):
        parts = []
        for slot in range(3):
            kind = 0 if slot < 2 else 1
            g = dqkv_ref[h, slot * hd : (slot + 1) * hd, :].astype(F32)
            v = raw_ref[h, slot * hd : (slot + 1) * hd, :].astype(F32)
            a, b = g[:half], g[half:]
            pre = jnp.concatenate([a * cos + b * sin, b * cos - a * sin], axis=0)
            factor = lax.rsqrt(jnp.mean(v * v, axis=0, keepdims=True) + epsilon)
            unit = v * factor
            head_sums[kind] += pre * unit
            pre = pre * gains[kind]
            back = factor * (pre - unit * jnp.mean(pre * unit, axis=0, keepdims=True))
            parts.append(back)
        parts.append(dqkv_ref[h, 3 * hd :, :].astype(F32))
        dproj[:, h * 256 : (h + 1) * 256] = jnp.concatenate(parts, axis=0).T.astype(BF)
    heads = [jnp.broadcast_to(jnp.sum(s, axis=1, keepdims=True), (hd, 128)) for s in head_sums]
    dp = dproj[...]
    dn = dot(dp, both(wm_ref[:, :, :, 0:wide], wo_ref[:, :, :, 0:wide]), NT)
    for n, at in enumerate(order(core, chips)):
        dn_scr[:, lanes(at)] = dn[:, n * 128 : (n + 1) * 128]
    dn = dn_scr[...]
    x = x_ref[...].astype(F32)
    r = lax.rsqrt(jnp.mean(x * x, axis=-1, keepdims=True) + epsilon)
    unit = x * r
    gain_sums = jnp.sum(dn * unit, axis=0, keepdims=True)
    g = dn * gains_ref[0:1]
    dx = dmid_ref[...] + r * (g - unit * jnp.mean(g * unit, axis=-1, keepdims=True))
    dx_ref[...] = dx.astype(BF)
    if not last:
        rows_ref[...] = jnp.broadcast_to(gain_sums, rows_ref.shape)
        for kind in (0, 1):
            head_ref[kind] = heads[kind]
        return
    acc[...] = (dot(nx0_ref[...], dproj0_ref[...], TN) + dot(nx_ref[...], dp, TN)).astype(BF).reshape(acc.shape)
    heads = [heads[kind] + head0_ref[kind] for kind in (0, 1)]
    lane = lax.broadcasted_iota(jnp.int32, (per, 128), 1)
    row = lax.broadcasted_iota(jnp.int32, (per, 128), 0)
    same = jnp.zeros((per, 128), F32)
    for n in range(4):
        same = jnp.where(lane == 2 + n, heads[n // 2][(n % 2) * per : (n % 2 + 1) * per, :], same)
    for n in range(3):
        same = jnp.where((lane == 6) & (row == n), jnp.sum(sums0_ref[n + 1 : n + 2, :], axis=1, keepdims=True), same)
    own = jnp.concatenate([gain_sums + rows0_ref[0:1], sums0_ref[0:1, :], jnp.zeros((126, d), F32)], axis=0)
    own = own.T.reshape(-1, per, 128)
    extra[...] = jnp.where((lane < 2)[None], own, same[None]).astype(BF).reshape(extra.shape)
    for n, ref in ((core, gm_ref), (1 - core, go_ref)):
        for a in range(chips):
            ref[a, :, :, 0:wide] = acc[a * 2 + n]
            ref[a, :, :, wide:] = extra[a * 2 + n]


def project_back(place, dqkv, raw, cos, sin, hg, x, dmid, mine, other, gains, seq, before):
    d = x.shape[1]
    kv, _, bt = raw.shape
    chips, steps, per, cols = mine.shape
    wide = cols - 128
    rows = pl.BlockSpec((bt, d), lambda i: (seq, 0), pipeline_mode=pl.Buffered(1))
    turns = pl.BlockSpec((32, bt), lambda i: (0, seq))
    last = before is not None
    shape = jax.ShapeDtypeStruct
    here = fixed(bt, d)
    grad = fixed(*mine.shape)
    proj = pltpu.VMEM((bt, wide), BF)
    return pl.pallas_call(
        functools.partial(project_back_kernel, last=last),
        grid=(1,),
        in_specs=[
            SMALL, fixed(kv, 256, bt), fixed(kv, 256, bt), turns, turns, fixed(64, 2), rows, here,
            fixed(*mine.shape), fixed(*mine.shape), fixed(8, d),
        ]
        + (
            [here, here, fixed(bt, wide), fixed(8, d), fixed(8, d), fixed(2, 64, 128), pl.BlockSpec(memory_space=pl.ANY)]
            if last
            else []
        ),
        out_specs=[rows] + ([grad, grad] if last else [fixed(bt, wide), fixed(8, d), fixed(2, 64, 128)]),
        input_output_aliases={17: 0} if last else {},
        out_shape=[shape(x.shape, BF)]
        + (
            [shape(mine.shape, BF)] * 2
            if last
            else [shape((bt, wide), BF), shape((8, d), F32), shape((2, 64, 128), F32)]
        ),
        scratch_shapes=(
            [
                proj,
                pltpu.VMEM((bt, d), F32),
                pltpu.VMEM((chips * 2, steps, per, wide), BF),
                pltpu.VMEM((chips * 2, steps, per, 128), BF),
            ]
            if last
            else [pltpu.VMEM((bt, d), F32)]
        ),
        compiler_params=params(),
        cost_estimate=cost((6 if last else 2) * bt * d * kv * 256, 20e6),
        name="project_back",
    )(place, dqkv, raw, cos, sin, hg, x, dmid, mine, other, gains, *(before if last else ()))


def add_kernel(a_ref, b_ref, out_ref):
    out_ref[...] = (a_ref[...].astype(F32) + b_ref[...].astype(F32)).astype(BF)


def add_up(a, b):
    n, rows, columns = a.shape[0] * a.shape[1], a.shape[2], a.shape[3]
    if rows < 128:
        return (a.astype(F32) + b.astype(F32)).astype(BF)
    block = pl.BlockSpec((n // 8, rows, columns), lambda i: (i, 0, 0))
    flat3 = (n, rows, columns)
    out = pl.pallas_call(
        add_kernel,
        grid=(8,),
        in_specs=[block, block],
        out_specs=block,
        out_shape=jax.ShapeDtypeStruct(flat3, BF),
        compiler_params=params(),
        cost_estimate=cost(n * rows * columns, 6 * n * rows * columns),
        name="add_up",
    )(a.reshape(flat3), b.reshape(flat3))
    return out.reshape(a.shape)


def heads_together(w):
    rows = w.shape[0]
    kv, hd = KEY_VALUE_HEADS, HEAD_DIMENSION
    q = w[:, : 2 * kv * hd].reshape(rows, kv, 2 * hd)
    k = w[:, 2 * kv * hd : 3 * kv * hd].reshape(rows, kv, hd)
    v = w[:, 3 * kv * hd :].reshape(rows, kv, hd)
    return jnp.concatenate([q, k, v], axis=2).reshape(rows, 4 * kv * hd)


def heads_apart(w):
    rows = w.shape[0]
    kv, hd = KEY_VALUE_HEADS, HEAD_DIMENSION
    w = w.reshape(rows, kv, 4 * hd)
    return jnp.concatenate(
        [
            w[:, :, : 2 * hd].reshape(rows, -1),
            w[:, :, 2 * hd : 3 * hd].reshape(rows, -1),
            w[:, :, 3 * hd :].reshape(rows, -1),
        ],
        axis=1,
    )


UNIT = 16
PARTS = (2, 3, 4)


def units_of(expand_weight, shrink_weight):
    per, width = expand_weight.shape
    owned, d = shrink_weight.shape
    units = owned // UNIT
    owners = width // (2 * owned)
    e = expand_weight.reshape(per, 2, owners // 8, 2, 4, units, UNIT).transpose(5, 0, 1, 3, 2, 4, 6)
    s = shrink_weight.reshape(units, UNIT, d)
    return jnp.concatenate([e.reshape(units, per, d), s], axis=1).reshape(units * (per + UNIT), d)


def units_apart(g, per):
    d = g.shape[1]
    g = g.reshape(-1, per + UNIT, d)
    units = g.shape[0]
    owners = d // (2 * UNIT)
    e = g[:, :per].reshape(units, per, 2, 2, owners // 8, 4, UNIT).transpose(1, 2, 4, 3, 5, 0, 6)
    return e.reshape(per, -1), g[:, per:].reshape(units * UNIT, d)


def after(x, *others):
    return lax.optimization_barrier((x, *others))[0]


def together(*xs):
    return lax.optimization_barrier(xs)


def heads_per_device(
    tokens, document_ids, mixer_weight, output_weight, mixer_gain, expand_weight, shrink_weight,
    feed_gain, head_gains, cotangent,
):
    seqs, rows, d = tokens.shape
    count = seqs * rows
    ring = ("chip", "core")
    steps = lax.axis_size("fsdp")
    core, z = lax.axis_index("core"), lax.axis_index("fsdp")
    place = jnp.stack([core, z]).astype(jnp.int32)
    device_count = lax.axis_size(ring) * steps
    per = mixer_gain.shape[0]
    swap = lambda a: lax.all_to_all(a, ring, 0, 0)
    across = lambda a: lax.ppermute(a, "core", [(0, 1), (1, 0)])

    def along_z(a):
        parts = [a] + [
            lax.ppermute(a, "fsdp", [(i, (i + s) % steps) for i in range(steps)]) for s in range(1, steps)
        ]
        return parts

    def in_order(parts):
        parts = [parts[-s % steps] for s in range(steps)]
        return lax.dynamic_slice_in_dim(jnp.stack(parts + parts), (steps - z) % steps, steps, 0)

    over_chips = lambda a: lax.all_gather(a, "chip", axis=0)
    reduce_chips = lambda a: lax.psum_scatter(a, "chip", scatter_dimension=0)

    def reduce_z(a):
        block = lambda s: lax.dynamic_index_in_dim(a, (z + s) % steps, 0, keepdims=False)
        out = block(0).astype(F32)
        for s in range(1, steps):
            out += lax.ppermute(block(s), "fsdp", [(i, (i + s) % steps) for i in range(steps)]).astype(F32)
        return out


    gains = jnp.pad(jnp.stack([mixer_gain, feed_gain], axis=1), ((0, 0), (0, 126)))
    mixer_parts = along_z(jnp.concatenate([heads_together(mixer_weight), gains], axis=1))

    below = jnp.sum(document_ids[:, None, :] < jnp.arange(4, dtype=jnp.int32)[None, :, None], axis=2)
    starts = jnp.sum(lax.all_gather(below.astype(jnp.int32), ring, axis=0), axis=0)
    mixer_parts, starts = lax.optimization_barrier((mixer_parts, starts))
    mixer_row = in_order(mixer_parts)
    mixer_mine = over_chips(mixer_row)

    owned = units_of(expand_weight, shrink_weight)
    owned = after(owned, mixer_row)
    pieces, at = [], 0
    for units in PARTS:
        pieces.append(owned[at : at + units * (per + UNIT)])
        at += units * (per + UNIT)
    first_row = in_order(along_z(jnp.concatenate([pieces[0], output_weight], axis=0)))
    first_part = lax.all_gather(first_row, ring, axis=0).reshape(-1, 2, *first_row.shape)
    mixer_other = across(mixer_mine)
    second = over_chips(after(pieces[1], first_row))
    third_z = along_z(after(pieces[2], first_row))

    earlier = jnp.zeros_like(document_ids)
    for n in range(1, 4):
        earlier = jnp.where(document_ids == n, starts[:, n][:, None], earlier)
    first = lax.axis_index(ring) * rows
    positions = first + jnp.arange(rows, dtype=jnp.int32)[None, :] - earlier
    half = HEAD_DIMENSION // 2
    inverse = rope_base ** (-(jnp.arange(half, dtype=F32) * 2.0 / HEAD_DIMENSION))
    angles = inverse[:, None] * positions.reshape(1, count).astype(F32)
    cos, sin = jnp.cos(angles), jnp.sin(angles)
    hg_forward = jnp.stack([head_gains[0] * QUERY_SCALE, head_gains[1]], axis=1)

    x = tokens.reshape(count, d)
    c = cotangent.reshape(count, d)
    projected = [project(place, x, mixer_mine, mixer_other, cos, sin, hg_forward, 0, rows)]
    projected.append(project(place, after(x, projected[0][0]), mixer_mine, mixer_other, cos, sin, hg_forward, 1, rows))
    qkv_heads = [swap(p[0]) for p in projected]
    gains_all = projected[0][3]

    qkv_heads[0], second = together(after(qkv_heads[0], projected[1][0]), second)
    onward = lambda a: lax.ppermute(a, "fsdp", [(i, (i + 1) % steps) for i in range(steps)])
    second_z = [second, onward(second)]
    out0 = attend(starts[0], qkv_heads[0])
    q1, second_z[1] = together(after(qkv_heads[1], out0[0]), second_z[1])
    second_z.append(onward(second_z[1]))
    out1 = attend(starts[1], q1)
    outs = [out0, out1]
    third = over_chips(in_order(after(third_z, out0[0])))
    attended = [swap(o[0]) for o in outs]
    attended[0], second_z[2] = together(after(attended[0], out1[0]), second_z[2])
    second_z.append(onward(second_z[2]))
    mids = [middle(place, x, attended[0], first_part, gains_all, 0)]
    attended[1] = after(attended[1], mids[0][1])
    mids.append(middle(place, x, attended[1], first_part, gains_all, 1))
    nm = [m[1] for m in mids]
    second_other = [across(t) for t in second_z[:3]]
    nm[1], second_z[3], *second_other = together(nm[1], second_z[3], *second_other)

    units = PARTS
    fb, dn, gm, go = feed(place, nm, c, first_part, steps, units[0], None, 0)
    exchanged = (gm, across(go))
    fb, third, last_other = together(fb, third, across(second_z[3]))
    part = (second_z, second_other + [last_other])
    fb, dn, gm, go = feed(place, nm, c, part, steps, units[1], (fb, dn), 0)
    second_exchanged = (gm, across(go))
    fb, third_other, summed = together(fb, across(third), add_up(*after(exchanged, fb)))
    chip_sums = [reduce_chips(summed)]
    fb, dn, gm, go = feed(place, nm, c, (third, third_other), steps, units[2], (fb, dn), per)
    carry = (fb, dn)

    turned = [turn(place, mids[0][0], *carry, c, attended[0], first_part, gains_all, 0, None)]
    before = (attended[0], turned[0][4], gm, go, turned[0][0])
    d_out_heads = [swap(turned[0][2])]
    turned.append(turn(place, mids[1][0], *carry, c, attended[1], first_part, gains_all, 1, before))
    gm, go = turned[1][4:6]
    d_out_heads.append(swap(turned[1][2]))
    d_out_heads[0], chip_sums[0], summed = together(
        d_out_heads[0], chip_sums[0], add_up(*after(second_exchanged, gm))
    )
    chip_sums.append(reduce_chips(summed))
    sums = turned[0][3] + turned[1][3]
    small = jnp.concatenate([sums[0:1], (mids[0][2] + mids[1][2])[0:1], sums[1:3], jnp.zeros((4, d), F32)], axis=0)

    back0 = attend_back(starts[0], qkv_heads[0], d_out_heads[0], out0[0], out0[1])
    d_out1, summed = together(after(d_out_heads[1], back0), add_up(*after((gm, across(go)), back0)))
    chip_sums.append(reduce_chips(summed))
    back1 = attend_back(starts[1], qkv_heads[1], d_out1, out1[0], out1[1])
    dqkv = [swap(back0), swap(back1)]
    dqkv[0], chip_sums[0], chip_sums[1] = together(after(dqkv[0], back1), chip_sums[0], chip_sums[1])
    z0 = reduce_z(chip_sums[0])
    z1 = reduce_z(chip_sums[1])

    hg = head_gains.T
    step0 = project_back(
        place, dqkv[0], projected[0][1], cos, sin, hg, x, turned[0][1], mixer_mine, mixer_other, gains_all, 0, None
    )
    before = (projected[1][2], projected[0][2], step0[1], small, step0[2], step0[3], step0[0])
    dqkv[1], z0, z1 = together(after(dqkv[1], step0[0]), z0, z1)
    dx1, gm, go = project_back(
        place, dqkv[1], projected[1][1], cos, sin, hg, x, turned[1][1], mixer_mine, mixer_other, gains_all, 1, before
    )
    gm, chip_sums[2] = together(gm, chip_sums[2])
    gradients = [z0, z1, reduce_z(chip_sums[2])]
    output_gradient = gradients[2][-per:]
    gradients[2] = gradients[2][:-per]
    last = reduce_chips(add_up(gm, across(go)))
    expand_gradient, shrink_gradient = units_apart(jnp.concatenate(gradients, axis=0), per)
    last = after(last, dx1)
    last = reduce_z(last)
    wide = mixer_weight.shape[1]
    small = last[:, wide:]
    return (
        turned[1][0].reshape(tokens.shape),
        dx1.reshape(tokens.shape),
        heads_apart(last[:, :wide]),
        output_gradient,
        small[:, 0],
        expand_gradient,
        shrink_gradient,
        small[:, 1],
        small[:, 2:6].T.reshape(2, 2 * per),
        jnp.sqrt(small[:3, 6] / (device_count * count * d)),
    )


def passed_along(block, axis, distance):
    devices = range(lax.axis_size(axis))
    route = [((i - distance) % len(devices), i) for i in devices]
    return lax.ppermute(block, axis, route)


def normalize_rows(values):
    factor = lax.rsqrt(jnp.mean(values * values, axis=-1, keepdims=True) + epsilon)
    return (values * factor, factor)


def normalize_back(values, factor, upstream):
    inner_mean = jnp.mean(upstream * values, axis=-1, keepdims=True)
    return factor * upstream - values * (factor * factor * factor) * inner_mean


def rotary_tables(positions, head_size):
    halfway = head_size // 2
    inverse = rope_base ** (-(jnp.arange(halfway, dtype=jnp.float32) * 2.0 / head_size))
    angles = positions.astype(jnp.float32)[..., None] * inverse
    angles = jnp.concatenate([angles, angles], axis=-1)
    return (jnp.cos(angles), jnp.sin(angles))


def rotate(values, cosine_table, sine_table):
    halfway = values.shape[-1] // 2
    turned = jnp.concatenate([-values[..., halfway:], values[..., :halfway]], axis=-1)
    return values * cosine_table + turned * sine_table


def rotate_back(upstream, cosine_table, sine_table):
    halfway = upstream.shape[-1] // 2
    scaled = upstream * sine_table
    turned = jnp.concatenate([scaled[..., halfway:], -scaled[..., :halfway]], axis=-1)
    return upstream * cosine_table + turned


def document_positions(own_documents, all_documents, offset_rows):
    earlier = jnp.sum(
        (all_documents[:, None, :] < own_documents[:, :, None]).astype(jnp.int32), axis=2
    )
    index_rows = offset_rows + jnp.arange(own_documents.shape[1], dtype=jnp.int32)
    return index_rows[None, :] - earlier


def allowed_pairs(query_docs, key_docs, query_index, key_index):
    same_document = query_docs[:, :, None] == key_docs[:, None, :]
    causal = query_index[:, None] >= key_index[None, :]
    return jnp.logical_and(same_document, causal[None, :, :])[:, None, None, :, :]


def column_product(left, right):
    return jnp.einsum("nd,nf->df", left, right, preferred_element_type=jnp.float32)


def per_device(
    tokens,
    document_ids,
    mixer_weight,
    output_weight,
    mixer_gain,
    expand_weight,
    shrink_weight,
    feed_gain,
    head_gains,
    cotangent,
):
    sequence_count, sequence_rows, model_width = tokens.shape
    count_of_tokens = sequence_count * sequence_rows
    query_groups = QUERY_HEADS // KEY_VALUE_HEADS
    query_feature_width = QUERY_HEADS * HEAD_DIMENSION
    key_feature_width = KEY_VALUE_HEADS * HEAD_DIMENSION
    cycle_size = lax.axis_size("ctx")
    cycle_index = lax.axis_index("ctx")
    device_count = lax.axis_size("ctx") * lax.axis_size("fsdp")
    owner_slot = lax.axis_index(("ctx", "fsdp"))
    gain_rows = mixer_gain.shape[0]
    offset_rows = cycle_index * sequence_rows
    all_documents = lax.all_gather(document_ids, "ctx", axis=1, tiled=True)
    positions = document_positions(document_ids, all_documents, offset_rows)
    cosine_table, sine_table = rotary_tables(positions.reshape(count_of_tokens), HEAD_DIMENSION)
    cosine_table = cosine_table[:, None, :]
    sine_table = sine_table[:, None, :]
    query_index = offset_rows + jnp.arange(sequence_rows, dtype=jnp.int32)
    mixer_all, output_all, mixer_gain_all = (
        lax.all_gather(mixer_weight, ("ctx", "fsdp"), axis=0, tiled=True),
        lax.all_gather(output_weight, ("ctx", "fsdp"), axis=0, tiled=True),
        lax.all_gather(mixer_gain, ("ctx", "fsdp"), axis=0, tiled=True),
    )
    stream = tokens.reshape(count_of_tokens, model_width).astype(jnp.float32)
    unit_in, factor_in = normalize_rows(stream)
    normed_in = (unit_in * mixer_gain_all.astype(jnp.float32)).astype(jnp.bfloat16)
    projected_heads = jnp.dot(normed_in, mixer_all, preferred_element_type=jnp.float32)
    query_raw = projected_heads[:, :query_feature_width].reshape(
        count_of_tokens, QUERY_HEADS, HEAD_DIMENSION
    )
    unrotated_key = projected_heads[
        :, query_feature_width : query_feature_width + key_feature_width
    ].reshape(count_of_tokens, KEY_VALUE_HEADS, HEAD_DIMENSION)
    value_rows = projected_heads[:, query_feature_width + key_feature_width :].astype(jnp.bfloat16)
    query_unit, query_factor = normalize_rows(query_raw)
    key_unit, key_factor = normalize_rows(unrotated_key)
    query_row_block = rotate(query_unit * head_gains[0], cosine_table, sine_table).astype(
        jnp.bfloat16
    )
    key_rows = rotate(key_unit * head_gains[1], cosine_table, sine_table).astype(jnp.bfloat16)
    query_head_rows = query_row_block.reshape(
        sequence_count, sequence_rows, KEY_VALUE_HEADS, query_groups, HEAD_DIMENSION
    ).transpose(0, 2, 3, 1, 4)
    key_send = key_rows.reshape(sequence_count, sequence_rows, key_feature_width)
    value_send = value_rows.reshape(sequence_count, sequence_rows, key_feature_width)
    statistics_shape = (sequence_count, KEY_VALUE_HEADS, query_groups, sequence_rows)
    initial = (
        jnp.full(statistics_shape, masked_score, jnp.float32),
        jnp.zeros(statistics_shape, jnp.float32),
        jnp.zeros(statistics_shape + (HEAD_DIMENSION,), jnp.float32),
    )
    carried = initial
    key_portion = lax.all_gather(key_send, "ctx", axis=1, tiled=True)
    value_portion = lax.all_gather(value_send, "ctx", axis=1, tiled=True)
    piece_rows = key_portion.shape[1]
    block_extent = math.gcd(piece_rows, 512)
    count_of_blocks = piece_rows // block_extent
    split_key_blocks = jnp.moveaxis(
        key_portion.reshape(
            sequence_count, count_of_blocks, block_extent, KEY_VALUE_HEADS, HEAD_DIMENSION
        ),
        1,
        0,
    )
    value_blocks = jnp.moveaxis(
        value_portion.reshape(
            sequence_count, count_of_blocks, block_extent, KEY_VALUE_HEADS, HEAD_DIMENSION
        ),
        1,
        0,
    )
    block_starts = jnp.arange(count_of_blocks, dtype=jnp.int32) * block_extent

    def one_block(running, block_items):
        current_key_block, current_value_block, block_start = block_items
        row_max, total_weight, weighted_sum = running
        key_docs = lax.dynamic_slice_in_dim(all_documents, block_start, block_extent, 1)
        key_index = block_start + jnp.arange(block_extent, dtype=jnp.int32)
        allowed = allowed_pairs(document_ids, key_docs, query_index, key_index)
        scores = (
            jnp.einsum(
                "skgrd,sjkd->skgrj",
                query_head_rows,
                current_key_block,
                preferred_element_type=jnp.float32,
            )
            * 0.125
        )
        masked = jnp.where(allowed, scores, masked_score)
        new_max = jnp.maximum(row_max, jnp.max(masked, axis=-1))
        rescale = jnp.exp(row_max - new_max)
        softmax_terms = jnp.where(allowed, jnp.exp(masked - new_max[..., None]), 0.0)
        total_weight = total_weight * rescale + jnp.sum(softmax_terms, axis=-1)
        weighted_sum = weighted_sum * rescale[..., None] + jnp.einsum(
            "skgrj,sjkd->skgrd",
            softmax_terms.astype(jnp.bfloat16),
            current_value_block,
            preferred_element_type=jnp.float32,
        )
        return ((new_max, total_weight, weighted_sum), None)

    carried, _ = lax.scan(one_block, carried, (split_key_blocks, value_blocks, block_starts))
    row_max, total_weight, weighted_sum = carried
    attn_heads = weighted_sum / total_weight[..., None]
    log_total = row_max + jnp.log(total_weight)
    attended = attn_heads.transpose(0, 3, 1, 2, 4).reshape(count_of_tokens, query_feature_width)
    attended_low = attended.astype(jnp.bfloat16)
    attn_branch = jnp.dot(attended_low, output_all, preferred_element_type=jnp.float32)
    middle = stream + attn_branch
    expand_all, shrink_all, feed_gain_all = (
        lax.all_gather(expand_weight, ("ctx", "fsdp"), axis=0, tiled=True),
        lax.all_gather(shrink_weight, ("ctx", "fsdp"), axis=0, tiled=True),
        lax.all_gather(feed_gain, ("ctx", "fsdp"), axis=0, tiled=True),
    )
    unit_mid, factor_mid = normalize_rows(middle)
    normed_mid = (unit_mid * feed_gain_all.astype(jnp.float32)).astype(jnp.bfloat16)
    gate_up = jnp.dot(normed_mid, expand_all, preferred_element_type=jnp.float32)
    gate_rows = gate_up[:, :FF]
    up_rows = gate_up[:, FF:]
    gate_sigmoid = jax.nn.sigmoid(gate_rows)
    gate_silu = gate_rows * gate_sigmoid
    hidden = (gate_silu * up_rows).astype(jnp.bfloat16)
    feed_branch = jnp.dot(hidden, shrink_all, preferred_element_type=jnp.float32)
    layer_out = middle + feed_branch
    squares = jnp.stack(
        [
            jnp.sum(attn_branch * attn_branch),
            jnp.sum(feed_branch * feed_branch),
            jnp.sum(layer_out * layer_out),
        ]
    )
    stat_totals = lax.psum(squares, ("ctx", "fsdp"))
    grad_branch = cotangent.reshape(count_of_tokens, model_width)
    grad_result = grad_branch.astype(jnp.float32)
    shrink_gradient = lax.psum_scatter(
        column_product(hidden, grad_branch), ("ctx", "fsdp"), scatter_dimension=0, tiled=True
    )
    grad_hidden = jnp.einsum(
        "nd,fd->nf", grad_branch, shrink_all, preferred_element_type=jnp.float32
    )
    grad_gate = grad_hidden * up_rows * gate_sigmoid * (1.0 + gate_rows * (1.0 - gate_sigmoid))
    grad_up = grad_hidden * gate_silu
    grad_gate_up = jnp.concatenate([grad_gate, grad_up], axis=1).astype(jnp.bfloat16)
    expand_gradient = lax.psum_scatter(
        column_product(normed_mid, grad_gate_up), ("ctx", "fsdp"), scatter_dimension=0, tiled=True
    )
    grad_normed_mid = jnp.einsum(
        "nf,df->nd", grad_gate_up, expand_all, preferred_element_type=jnp.float32
    )
    feed_gain_term = jnp.sum(grad_normed_mid * unit_mid, axis=0)
    grad_middle = grad_result + normalize_back(
        middle, factor_mid, grad_normed_mid * feed_gain_all.astype(jnp.float32)
    )
    grad_attn_low = grad_middle.astype(jnp.bfloat16)
    output_gradient = lax.psum_scatter(
        column_product(attended_low, grad_attn_low),
        ("ctx", "fsdp"),
        scatter_dimension=0,
        tiled=True,
    )
    attended_gradient = jnp.einsum(
        "nd,qd->nq", grad_attn_low, output_all, preferred_element_type=jnp.float32
    ).astype(jnp.bfloat16)
    heads_gradient = attended_gradient.reshape(
        sequence_count, sequence_rows, KEY_VALUE_HEADS, query_groups, HEAD_DIMENSION
    ).transpose(0, 2, 3, 1, 4)
    delta_rows = jnp.sum(heads_gradient.astype(jnp.float32) * attn_heads, axis=-1)
    zero_query = jnp.zeros(query_head_rows.shape, jnp.float32)

    def pair_terms(current_key_block, current_value_block, block_start):
        rows_per_block = current_key_block.shape[1]
        key_reshaped = current_key_block.reshape(
            sequence_count, rows_per_block, KEY_VALUE_HEADS, HEAD_DIMENSION
        )
        value_reshaped = current_value_block.reshape(
            sequence_count, rows_per_block, KEY_VALUE_HEADS, HEAD_DIMENSION
        )
        key_docs = lax.dynamic_slice_in_dim(all_documents, block_start, rows_per_block, 1)
        key_index = block_start + jnp.arange(rows_per_block, dtype=jnp.int32)
        allowed = allowed_pairs(document_ids, key_docs, query_index, key_index)
        scores = (
            jnp.einsum(
                "skgrd,sjkd->skgrj",
                query_head_rows,
                key_reshaped,
                preferred_element_type=jnp.float32,
            )
            * 0.125
        )
        probability = jnp.where(
            allowed, jnp.exp(jnp.where(allowed, scores, 0.0) - log_total[..., None]), 0.0
        )
        value_term = jnp.einsum(
            "skgrj,skgrd->sjkd",
            probability.astype(jnp.bfloat16),
            heads_gradient,
            preferred_element_type=jnp.float32,
        )
        grad_probability = jnp.einsum(
            "skgrd,sjkd->skgrj", heads_gradient, value_reshaped, preferred_element_type=jnp.float32
        )
        grad_scores = (probability * (grad_probability - delta_rows[..., None])).astype(
            jnp.bfloat16
        )
        query_term = (
            jnp.einsum(
                "skgrj,sjkd->skgrd", grad_scores, key_reshaped, preferred_element_type=jnp.float32
            )
            * 0.125
        )
        key_term = (
            jnp.einsum(
                "skgrj,skgrd->sjkd",
                grad_scores,
                query_head_rows,
                preferred_element_type=jnp.float32,
            )
            * 0.125
        )
        return (
            query_term,
            key_term.reshape(sequence_count, rows_per_block, key_feature_width),
            value_term.reshape(sequence_count, rows_per_block, key_feature_width),
        )

    zero_keys = jnp.zeros((sequence_count, sequence_rows, key_feature_width), jnp.float32)

    def cycle_step(cycle_turn, running):
        (
            current_key_block,
            current_value_block,
            key_gradient_accumulator,
            value_accum,
            query_accum,
        ) = running
        owner_index = (cycle_index - cycle_turn) % cycle_size
        query_term, key_term, value_term = pair_terms(
            current_key_block.astype(jnp.bfloat16),
            current_value_block.astype(jnp.bfloat16),
            owner_index * sequence_rows,
        )
        query_accum = query_accum + query_term
        key_gradient_accumulator = key_gradient_accumulator + key_term
        value_accum = value_accum + value_term
        current_key_block, current_value_block, key_gradient_accumulator, value_accum = (
            passed_along(current_key_block.astype(jnp.bfloat16), "ctx", 1).astype(
                current_key_block.dtype
            ),
            passed_along(current_value_block.astype(jnp.bfloat16), "ctx", 1).astype(
                current_value_block.dtype
            ),
            passed_along(key_gradient_accumulator.astype(jnp.bfloat16), "ctx", 1).astype(
                key_gradient_accumulator.dtype
            ),
            passed_along(value_accum.astype(jnp.bfloat16), "ctx", 1).astype(value_accum.dtype),
        )
        return (
            current_key_block,
            current_value_block,
            key_gradient_accumulator,
            value_accum,
            query_accum,
        )

    carried = lax.fori_loop(
        0,
        cycle_size,
        cycle_step,
        (
            key_send.astype(jnp.float32),
            value_send.astype(jnp.float32),
            zero_keys,
            zero_keys,
            zero_query,
        ),
    )
    key_gradient_accumulator, value_accum, query_accum = (carried[2], carried[3], carried[4])
    grad_query = query_accum.transpose(0, 3, 1, 2, 4).reshape(
        count_of_tokens, QUERY_HEADS, HEAD_DIMENSION
    )
    key_grad_total = key_gradient_accumulator.reshape(
        count_of_tokens, KEY_VALUE_HEADS, HEAD_DIMENSION
    )
    grad_value = value_accum.reshape(count_of_tokens, key_feature_width)
    grad_query_pre = rotate_back(grad_query, cosine_table, sine_table)
    grad_key_pre = rotate_back(key_grad_total, cosine_table, sine_table)
    head_terms = jnp.stack(
        [
            jnp.sum(grad_query_pre * query_unit, axis=(0, 1)),
            jnp.sum(grad_key_pre * key_unit, axis=(0, 1)),
        ]
    )
    grad_query_raw = normalize_back(query_raw, query_factor, grad_query_pre * head_gains[0])
    grad_key_raw = normalize_back(unrotated_key, key_factor, grad_key_pre * head_gains[1])
    grad_projected = jnp.concatenate(
        [
            grad_query_raw.reshape(count_of_tokens, query_feature_width),
            grad_key_raw.reshape(count_of_tokens, key_feature_width),
            grad_value,
        ],
        axis=1,
    ).astype(jnp.bfloat16)
    mixer_gradient = lax.psum_scatter(
        column_product(normed_in, grad_projected), ("ctx", "fsdp"), scatter_dimension=0, tiled=True
    )
    grad_normed_in = jnp.einsum(
        "nq,dq->nd", grad_projected, mixer_all, preferred_element_type=jnp.float32
    )
    mixer_gain_term = jnp.sum(grad_normed_in * unit_in, axis=0)
    grad_stream = grad_middle + normalize_back(
        stream, factor_in, grad_normed_in * mixer_gain_all.astype(jnp.float32)
    )
    feed_gain_total, mixer_gain_total, head_total = lax.psum(
        (feed_gain_term, mixer_gain_term, head_terms), ("ctx", "fsdp")
    )
    feed_gain_gradient = lax.dynamic_slice_in_dim(
        feed_gain_total, owner_slot * gain_rows, gain_rows, 0
    )
    mixer_gain_gradient = lax.dynamic_slice_in_dim(
        mixer_gain_total, owner_slot * gain_rows, gain_rows, 0
    )
    statistics = jnp.sqrt(stat_totals / (device_count * count_of_tokens * model_width))
    result = layer_out.astype(jnp.bfloat16).reshape(sequence_count, sequence_rows, model_width)
    tokens_gradient = grad_stream.astype(jnp.bfloat16).reshape(
        sequence_count, sequence_rows, model_width
    )
    return (
        result,
        tokens_gradient,
        mixer_gradient,
        output_gradient,
        mixer_gain_gradient,
        expand_gradient,
        shrink_gradient,
        feed_gain_gradient,
        head_total,
        statistics,
    )


def solution(mesh):
    function, ring = per_device, "ctx"
    if mesh.shape["ctx"] == KEY_VALUE_HEADS:
        shape = (KEY_VALUE_HEADS // 2, 2, mesh.shape["fsdp"])
        mesh = jax.sharding.Mesh(mesh.devices.reshape(shape), ("chip", "core", "fsdp"))
        function, ring = heads_per_device, ("chip", "core")
    every = (ring, "fsdp") if isinstance(ring, str) else ring + ("fsdp",)
    tokens, rows, vector = P("fsdp", ring, None), P(every, None), P(every)
    return jax.shard_map(
        function,
        mesh=mesh,
        in_specs=(
            tokens,
            P("fsdp", ring),
            rows,
            rows,
            vector,
            rows,
            rows,
            vector,
            P(),
            tokens,
        ),
        out_specs=(tokens, tokens, rows, rows, vector, rows, rows, vector, P(), P()),
        check_vma=False,
    )
```

```python
import functools
import math

import jax
import jax.numpy as jnp
from jax import lax
from jax.experimental import pallas as pl
from jax.experimental.pallas import tpu as pltpu
from jax.sharding import PartitionSpec as P

QUERY_HEADS = 16
KEY_VALUE_HEADS = 8
HEAD_DIMENSION = 64
FF = 4608

epsilon = 1e-05
rope_base = 1000000.0
masked_score = -1e30
LOG2E = math.log2(math.e)
QUERY_SCALE = 0.125 * LOG2E
MASK = 256.0
VMEM = 60 * 2**20
BF, F32 = jnp.bfloat16, jnp.float32

NN = (((1,), (0,)), ((), ()))
NT = (((1,), (1,)), ((), ()))
TN = (((0,), (0,)), ((), ()))


def dot(a, b, dims=NN):
    return lax.dot_general(a, b, dims, preferred_element_type=F32)


def params(**kw):
    return pltpu.CompilerParams(vmem_limit_bytes=VMEM, **kw)


def cost(flops, nbytes):
    return pl.CostEstimate(flops=int(0.001 * flops), bytes_accessed=int(0.001 * nbytes), transcendentals=0)


def flat(x):
    return x.reshape(-1, x.shape[-1])


def both(mine, other):
    return jnp.concatenate([flat(mine), flat(other)], axis=0)


def order(core, chips):
    return [a * 2 + core for a in range(chips)] + [a * 2 + 1 - core for a in range(chips)]


def lanes(n, width=128):
    return pl.ds(pl.multiple_of(n * width, width), width)


SMALL = pl.BlockSpec(memory_space=pltpu.SMEM)


def fixed(*shape):
    return pl.BlockSpec(shape, lambda *i: (0,) * len(shape), pipeline_mode=pl.Buffered(1))


def halves(w, rows, index, **kw):
    if isinstance(w, tuple):
        block = (*w[0].shape[:2], rows, w[0].shape[-1])
        spec = pl.BlockSpec(block, lambda i, place: (0, 0, index(i), 0), **kw)
        return list(w), [spec, spec]
    block = (w.shape[0], None, w.shape[2], rows, w.shape[-1])
    return [w, w], [
        pl.BlockSpec(block, lambda i, place: (0, place[0], 0, index(i), 0), **kw),
        pl.BlockSpec(block, lambda i, place: (0, 1 - place[0], 0, index(i), 0), **kw),
    ]


def project_kernel(
    place_ref, x_ref, wm_ref, wo_ref, cos_ref, sin_ref, hg_ref, qkv_ref, raw_ref, nx_ref, gains_ref, nxt, grow
):
    core = place_ref[0]
    chips = wm_ref.shape[0]
    kv = KEY_VALUE_HEADS
    wide = kv * 256
    g = both(wm_ref[:, :, :, wide:], wo_ref[:, :, :, wide:]).astype(F32).T[0:8]
    for n, at in enumerate(order(core, chips)):
        grow[:, lanes(at)] = g[:, n * 128 : (n + 1) * 128]
    gains_ref[...] = grow[...]
    x = x_ref[...].astype(F32)
    r = lax.rsqrt(jnp.mean(x * x, axis=-1, keepdims=True) + epsilon)
    nx = (x * r * grow[0:1]).astype(BF)
    nx_ref[...] = nx
    bt = x.shape[0]
    nxt[...] = nx.T.reshape(nxt.shape)
    xt = jnp.concatenate([nxt[at] for at in order(core, chips)], axis=0)
    cos, sin = cos_ref[...], sin_ref[...]
    hd, half = HEAD_DIMENSION, HEAD_DIMENSION // 2
    gains = [jnp.broadcast_to(hg_ref[:, j : j + 1], (hd, bt)) for j in (0, 1)]
    for h in range(kv):
        cols = slice(h * 256, (h + 1) * 256)
        p = dot(both(wm_ref[:, :, :, cols], wo_ref[:, :, :, cols]), xt, TN)
        raw_ref[h] = p.astype(BF)
        for slot in range(3):
            v = p[slot * hd : (slot + 1) * hd]
            factor = lax.rsqrt(jnp.mean(v * v, axis=0, keepdims=True) + epsilon)
            u = v * factor * gains[0 if slot < 2 else 1]
            a, b = u[:half], u[half:]
            qkv_ref[h, slot * hd : slot * hd + half, :] = (a * cos - b * sin).astype(BF)
            qkv_ref[h, slot * hd + half : (slot + 1) * hd, :] = (b * cos + a * sin).astype(BF)
        qkv_ref[h, 3 * hd :, :] = p[3 * hd :].astype(BF)


def project(place, x, mine, other, cos, sin, hg, seq, bt):
    d = x.shape[1]
    kv = KEY_VALUE_HEADS
    turns = pl.BlockSpec((32, bt), lambda i: (0, seq))
    return pl.pallas_call(
        project_kernel,
        grid=(1,),
        in_specs=[
            SMALL,
            pl.BlockSpec((bt, d), lambda i: (seq, 0)),
            fixed(*mine.shape),
            fixed(*mine.shape),
            turns,
            turns,
            fixed(64, 2),
        ],
        out_specs=[fixed(kv, 256, bt), fixed(kv, 256, bt), fixed(bt, d), fixed(8, d)],
        out_shape=[
            jax.ShapeDtypeStruct((kv, 256, bt), BF),
            jax.ShapeDtypeStruct((kv, 256, bt), BF),
            jax.ShapeDtypeStruct((bt, d), BF),
            jax.ShapeDtypeStruct((8, d), F32),
        ],
        scratch_shapes=[pltpu.VMEM((d // 128, 128, bt), BF), pltpu.VMEM((8, d), F32)],
        compiler_params=params(),
        cost_estimate=cost(2 * bt * d * kv * 256, 14e6),
        name="project",
    )(place, x, mine, other, cos, sin, hg)


def first_start(starts_ref, s, t):
    out = jnp.int32(0)
    for d in range(1, 4):
        b = starts_ref[s * 4 + d]
        out = jnp.where(t >= b, b, out)
    return out


def next_start(starts_ref, s, t, total):
    out = jnp.int32(total)
    for d in range(3, 0, -1):
        b = starts_ref[s * 4 + d]
        out = jnp.where(t < b, b, out)
    return out


def member(starts_ref, s, base, rows, width, total):
    pos = base + lax.broadcasted_iota(jnp.int32, (rows, width), 1)
    row = lax.broadcasted_iota(jnp.int32, (rows, width), 0)
    out = jnp.zeros((rows, width), F32)
    for d in range(4):
        lo = starts_ref[s * 4 + d]
        hi = starts_ref[s * 4 + d + 1] if d < 3 else jnp.int32(total)
        out = jnp.where((row == d) & (pos >= lo) & (pos < hi), 1.0, out)
    return out


def attend_kernel(starts_ref, q_ref, seq_ref, out_ref, lse_ref, kx, vt, acc):
    s, i = pl.program_id(0), pl.program_id(1)
    blocks, _, width = seq_ref.shape
    total = blocks * width

    @pl.when(i == 0)
    def _():
        for j in range(blocks):
            aux = member(starts_ref, s, j * width, 64, width, total)
            kk = jnp.concatenate([seq_ref[j, 128:192, :].astype(F32), aux], axis=0)
            kx[j] = kk.T.astype(BF)
            vt[j, 0:64, :] = seq_ref[j, 192:256, :]
            ones = (lax.broadcasted_iota(jnp.int32, (16, width), 0) == 0).astype(F32)
            vt[j, 64:80, :] = ones.astype(BF)

    aux = ((member(starts_ref, s, i * width, 64, width, total) - 1.0) * MASK).astype(BF)
    row = lax.broadcasted_iota(jnp.int32, (64, width), 0)
    aux = jnp.where(row < 4, aux.astype(F32), 0.0).astype(BF)
    q = [jnp.concatenate([q_ref[0, g * 64 : g * 64 + 64, :], aux], axis=0) for g in (0, 1)]
    acc[...] = jnp.zeros_like(acc)

    def block(j, diagonal):
        k, v = kx[j], vt[j]
        sc = [dot(k, q[g]) for g in (0, 1)]
        if diagonal:
            keep = lax.broadcasted_iota(jnp.int32, (width, width), 0) <= lax.broadcasted_iota(
                jnp.int32, (width, width), 1
            )
            sc = [jnp.where(keep, x, -MASK) for x in sc]
        p = [jnp.exp2(x).astype(BF) for x in sc]
        for g in (0, 1):
            acc[g] += dot(v, p[g])

    lo = first_start(starts_ref, s, i * width) // width
    lax.fori_loop(lo, i, lambda j, c: (block(j, False), c)[1], 0)
    block(i, True)
    for g in (0, 1):
        a = acc[g]
        total_weight = a[64:65]
        out_ref[0, g * 64 : g * 64 + 64, :] = (a[0:64] / total_weight).astype(BF)
        lse_ref[0, g : g + 1, :] = jnp.log2(total_weight)
    lse_ref[0, 2:8, :] = jnp.zeros((6, width), F32)


def attend(starts, qkv, seqs=1):
    blocks, _, rows = qkv.shape
    width = rows // seqs
    return pl.pallas_call(
        attend_kernel,
        grid_spec=pltpu.PrefetchScalarGridSpec(
            num_scalar_prefetch=1,
            grid=(seqs, blocks),
            in_specs=[
                pl.BlockSpec((1, 256, width), lambda s, i, st: (i, 0, s)),
                pl.BlockSpec((blocks, 256, width), lambda s, i, st: (0, 0, s)),
            ],
            out_specs=[
                pl.BlockSpec((1, 128, width), lambda s, i, st: (i, 0, s)),
                pl.BlockSpec((1, 8, width), lambda s, i, st: (i, 0, s)),
            ],
            scratch_shapes=[
                pltpu.VMEM((blocks, width, 128), BF),
                pltpu.VMEM((blocks, 80, width), BF),
                pltpu.VMEM((2, 80, width), F32),
            ],
        ),
        out_shape=[
            jax.ShapeDtypeStruct((blocks, 128, rows), BF),
            jax.ShapeDtypeStruct((blocks, 8, rows), F32),
        ],
        compiler_params=params(),
        cost_estimate=cost(30e9, 4e6),
        name="attend",
    )(starts, qkv, qkv)


def split3(x):
    hi = x.astype(BF).astype(F32)
    mid = (x - hi).astype(BF).astype(F32)
    return hi, mid, x - hi - mid


def attend_back_kernel(
    starts_ref, seq_ref, do_ref, o_ref, lse_ref, out_ref, kx, vx, qx, dox, dq, dk, dv
):
    s, j = pl.program_id(0), pl.program_id(1)
    blocks, _, width = seq_ref.shape
    total = blocks * width

    @pl.when(j == 0)
    def _():
        row = lax.broadcasted_iota(jnp.int32, (64, width), 0)
        minus = jnp.where((row >= 4) & (row < 7), -1.0, 0.0)
        for b in range(blocks):
            mem = member(starts_ref, s, b * width, 64, width, total)
            aux = mem + minus
            kk = jnp.concatenate([seq_ref[b, 128:192, :].astype(F32), aux], axis=0)
            kx[b] = kk.T.astype(BF)
            vv = jnp.concatenate([seq_ref[b, 192:256, :].astype(F32), minus], axis=0)
            vx[b] = vv.T.astype(BF)
            qmask = jnp.where(row < 4, (mem - 1.0) * MASK, 0.0)
            for g in (0, 1):
                h1, h2, h3 = split3(lse_ref[b, g : g + 1, :])
                ax = jnp.where(row == 4, h1, jnp.where(row == 5, h2, jnp.where(row == 6, h3, qmask)))
                qx[b, g, 0:64, :] = seq_ref[b, g * 64 : g * 64 + 64, :]
                qx[b, g, 64:128, :] = ax.astype(BF)
                d_out = do_ref[b, g * 64 : g * 64 + 64, :]
                out = o_ref[b, g * 64 : g * 64 + 64, :]
                delta = jnp.sum(d_out.astype(F32) * out.astype(F32), axis=0, keepdims=True)
                h1, h2, h3 = split3(delta)
                ax = jnp.where(row == 4, h1, jnp.where(row == 5, h2, jnp.where(row == 6, h3, 0.0)))
                dox[b, g, 0:64, :] = d_out
                dox[b, g, 64:128, :] = ax.astype(BF)
        dq[...] = jnp.zeros_like(dq)

    dk[...] = jnp.zeros_like(dk)
    dv[...] = jnp.zeros_like(dv)
    k, v, ktr = kx[j], vx[j], seq_ref[j, 128:192, :]

    def block(i, diagonal):
        sc = [dot(k, qx[i, g]) for g in (0, 1)]
        dp = [dot(v, dox[i, g]) for g in (0, 1)]
        if diagonal:
            keep = lax.broadcasted_iota(jnp.int32, (width, width), 0) <= lax.broadcasted_iota(
                jnp.int32, (width, width), 1
            )
            sc = [jnp.where(keep, x, -MASK) for x in sc]
        p = [jnp.exp2(x) for x in sc]
        ds = [(p[g] * dp[g]).astype(BF) for g in (0, 1)]
        pb = [x.astype(BF) for x in p]
        for g in (0, 1):
            dv[...] += dot(dox[i, g, 0:64, :], pb[g], NT)
            dk[...] += dot(qx[i, g, 0:64, :], ds[g], NT)
            dq[i, g] += dot(ktr, ds[g])

    block(j, True)
    hi = (next_start(starts_ref, s, j * width + width - 1, total) - 1) // width
    lax.fori_loop(j + 1, hi + 1, lambda i, c: (block(i, False), c)[1], 0)
    out_ref[j, 128:192, :] = (dk[...] * (0.125 / QUERY_SCALE)).astype(BF)
    out_ref[j, 192:256, :] = dv[...].astype(BF)

    @pl.when(j == blocks - 1)
    def _():
        for b in range(blocks):
            for g in (0, 1):
                out_ref[b, g * 64 : g * 64 + 64, :] = (dq[b, g] * 0.125).astype(BF)


def attend_back(starts, qkv, d_out, out, lse, seqs=1):
    blocks, _, rows = qkv.shape
    width = rows // seqs
    whole = lambda n: pl.BlockSpec((blocks, n, width), lambda s, j, st: (0, 0, s))
    return pl.pallas_call(
        attend_back_kernel,
        grid_spec=pltpu.PrefetchScalarGridSpec(
            num_scalar_prefetch=1,
            grid=(seqs, blocks),
            in_specs=[whole(256), whole(128), whole(128), whole(8)],
            out_specs=whole(256),
            scratch_shapes=[
                pltpu.VMEM((blocks, width, 128), BF),
                pltpu.VMEM((blocks, width, 128), BF),
                pltpu.VMEM((blocks, 2, 128, width), BF),
                pltpu.VMEM((blocks, 2, 128, width), BF),
                pltpu.VMEM((blocks, 2, 64, width), F32),
                pltpu.VMEM((64, width), F32),
                pltpu.VMEM((64, width), F32),
            ],
        ),
        out_shape=jax.ShapeDtypeStruct((blocks, 256, rows), BF),
        compiler_params=params(),
        cost_estimate=cost(60e9, 6e6),
        name="attend_back",
    )(starts, qkv, d_out, out, lse)


def middle_kernel(place_ref, x_ref, at_ref, wm_ref, wo_ref, gains_ref, mid_ref, nm_ref, sq_ref):
    core = place_ref[0]
    a = jnp.concatenate([at_ref[at] for at in order(core, wm_ref.shape[0])], axis=0)
    branch = dot(a, both(wm_ref[...], wo_ref[...]), TN)
    mid = x_ref[...].astype(F32) + branch
    mid_ref[...] = mid
    r = lax.rsqrt(jnp.mean(mid * mid, axis=-1, keepdims=True) + epsilon)
    nm_ref[...] = (mid * r * gains_ref[1:2]).astype(BF)
    sq_ref[...] = jnp.zeros_like(sq_ref)
    sq_ref[0:1, :] = jnp.sum(branch * branch, axis=0, keepdims=True)


def output_rows(w):
    rows = w.shape[3]
    return halves(w, 32, lambda i: rows // 32 - 1, pipeline_mode=pl.Buffered(1))


def middle(place, x, at, w, gains, seq):
    d = x.shape[1]
    heads, n, bt = at.shape
    arrays, specs = output_rows(w)
    return pl.pallas_call(
        middle_kernel,
        grid_spec=pltpu.PrefetchScalarGridSpec(
            num_scalar_prefetch=1,
            grid=(1,),
            in_specs=[pl.BlockSpec((bt, d), lambda i, p: (seq, 0)), fixed(heads, n, bt), *specs, fixed(8, d)],
            out_specs=[fixed(bt, d), fixed(bt, d), fixed(8, d)],
        ),
        out_shape=[
            jax.ShapeDtypeStruct((bt, d), F32),
            jax.ShapeDtypeStruct((bt, d), BF),
            jax.ShapeDtypeStruct((8, d), F32),
        ],
        compiler_params=params(),
        cost_estimate=cost(2 * bt * d * heads * n, 7e6),
        name="middle",
    )(place, x, at, *arrays, gains)


def feed_kernel(*refs, first, steps, parts):
    place_ref, n0_ref, n1_ref, c_ref = refs[:4]
    count = 2 * steps if parts else 2
    weights, refs = refs[4 : 4 + count], refs[4 + count :]
    if not first:
        fb_in, dn_in = refs[:2]
        refs = refs[2:]
    fb_ref, dn_ref, gm_ref, go_ref, nm, nmt, wscr, wsscr, hid, dgu, gsscr = refs
    f = pl.program_id(0)
    core, z = place_ref[0], place_ref[1]
    _, chips, _, per, d = wscr.shape
    rows = gm_ref.shape[2]
    unit = rows - per
    tokens, H = hid.shape
    bt = tokens // 2

    @pl.when(f == 0)
    def _():
        if first:
            fb_ref[...] = jnp.zeros_like(fb_ref)
            dn_ref[...] = jnp.zeros_like(dn_ref)
        else:
            fb_ref[...] = fb_in[...]
            dn_ref[...] = dn_in[...]
        for s, ref in enumerate((n0_ref, n1_ref)):
            for n, at in enumerate(order(core, chips)):
                nm[s * bt : (s + 1) * bt, n * 128 : (n + 1) * 128] = ref[:, lanes(at)]
        nmt[...] = nm[...].T

    for r, c in ((0, core), (1, 1 - core)):
        if parts:
            for s in range(steps):
                at = (z - s + steps) % steps
                ref = weights[r * steps + s]
                wscr[r, :, at] = ref[:, 0:per, :]
                wsscr[c, :, at] = ref[:, per:rows, :]
        else:
            wscr[r] = weights[r][:, :, 0:per, :]
            wsscr[c] = weights[r][:, :, per:rows, :]
    w, ws = flat(wscr[...]), flat(wsscr[...])
    half = tokens // 2
    for t in range(2):
        ts = slice(t * half, (t + 1) * half)
        gate_up = dot(nm[ts, :], w)
        gate, up = gate_up[:, :H], gate_up[:, H:]
        dh = dot(c_ref[ts, :], ws, NT)
        sig = 0.5 * jnp.tanh(0.5 * gate) + 0.5
        silu = gate * sig
        hidden = (silu * up).astype(BF)
        hid[ts, :] = hidden
        dgu[ts, :H] = (dh * up * sig * (1.0 + gate * (1.0 - sig))).astype(BF)
        dgu[ts, H:] = (dh * silu).astype(BF)
        fb_ref[ts, :] += dot(hidden, ws)
        dn_ref[ts, :] += dot(dgu[ts, :], w, NT)
    gsscr[...] = dot(hid[...], c_ref[...], TN).astype(BF).reshape(gsscr.shape)
    for q in (0, 1):
        ge = dot(nmt[...], dgu[:, q * H : (q + 1) * H]).astype(BF).reshape(2, chips, steps, per, H)
        for n, ref in ((0, gm_ref), (1, go_ref)):
            ref[:, :, 0:per, q * H : (q + 1) * H] = ge[n]
    for n, ref in ((core, gm_ref), (1 - core, go_ref)):
        ref[:, :, per:rows, :] = gsscr[n]


def feed(place, nm, c, w, steps, units, carry, extra):
    tokens, d = c.shape
    parts = isinstance(w, tuple) and isinstance(w[0], list)
    if parts:
        arrays = w[0] + w[1]
        chips = arrays[0].shape[0]
        per = d // (chips * 2 * steps)
        specs = [pl.BlockSpec((chips, per + UNIT, d), lambda f, p: (0, f, 0))] * len(arrays)
    else:
        chips = (w[0] if isinstance(w, tuple) else w).shape[0]
        per = d // (chips * 2 * steps)
        arrays, specs = halves(w, per + UNIT, lambda f: f)
    block = pl.BlockSpec((chips, steps, per + UNIT, d), lambda f, p: (0, 0, f, 0))
    whole = fixed(tokens, d)
    first = carry is None
    hidden = chips * 2 * steps * UNIT
    at = 4 + len(arrays)
    grad = jax.ShapeDtypeStruct((chips, steps, (per + UNIT) * units + extra, d), BF)
    return pl.pallas_call(
        functools.partial(feed_kernel, first=first, steps=steps, parts=parts),
        grid_spec=pltpu.PrefetchScalarGridSpec(
            num_scalar_prefetch=1,
            grid=(units,),
            in_specs=[fixed(*nm[0].shape), fixed(*nm[1].shape), whole, *specs] + ([] if first else [whole, whole]),
            out_specs=[whole, whole, block, block],
            scratch_shapes=[
                pltpu.VMEM((tokens, d), BF),
                pltpu.VMEM((d, tokens), BF),
                pltpu.VMEM((2, chips, steps, per, d), BF),
                pltpu.VMEM((2, chips, steps, UNIT, d), BF),
                pltpu.VMEM((tokens, hidden), BF),
                pltpu.VMEM((tokens, 2 * hidden), BF),
                pltpu.VMEM((2, chips, steps, UNIT, d), BF),
            ],
        ),
        out_shape=[jax.ShapeDtypeStruct((tokens, d), F32)] * 2 + [grad, grad],
        input_output_aliases={} if first else {at: 0, at + 1: 1},
        compiler_params=params(),
        cost_estimate=cost(18 * tokens * d * hidden * units, 8e6 * units + 20e6),
        name="feed",
    )(place, *nm, c, *arrays, *(() if first else carry))


def turn_kernel(*refs, last):
    place_ref, mid_ref, fb_ref, dn_ref, c_ref, at_ref, wm_ref, wo_ref, gains_ref = refs[:9]
    refs = refs[9:]
    if last:
        at0_ref, low0_ref = refs[:2]
        res_ref, dmid_ref, da_ref, sums_ref, gm_ref, go_ref, dn_scr, acc = refs[5:]
    else:
        res_ref, dmid_ref, da_ref, sums_ref, low_ref, dn_scr = refs
    heads, n, bt = at_ref.shape
    core = place_ref[0]
    chips, steps, per, d = wm_ref.shape
    for m, at in enumerate(order(core, chips)):
        dn_scr[:, lanes(at)] = dn_ref[:, m * 128 : (m + 1) * 128]
    mid, fb, dn = mid_ref[...], fb_ref[...], dn_scr[...]
    out = mid + fb
    res_ref[...] = out.astype(BF)
    r = lax.rsqrt(jnp.mean(mid * mid, axis=-1, keepdims=True) + epsilon)
    unit = mid * r
    g = dn * gains_ref[1:2]
    dmid = c_ref[...].astype(F32) + r * (g - unit * jnp.mean(g * unit, axis=-1, keepdims=True))
    dmid_ref[...] = dmid
    low = dmid.astype(BF)
    da = dot(both(wm_ref[...], wo_ref[...]), low, NT).astype(BF).reshape(heads, n, bt)
    for m, at in enumerate(order(core, chips)):
        da_ref[at] = da[m]
    sums_ref[...] = jnp.zeros_like(sums_ref)
    sums_ref[0:1, :] = jnp.sum(dn * unit, axis=0, keepdims=True)
    sums_ref[1:2, :] = jnp.sum(fb * fb, axis=0, keepdims=True)
    sums_ref[2:3, :] = jnp.sum(out * out, axis=0, keepdims=True)
    if last:
        a = jnp.concatenate([flat(at0_ref[...]), flat(at_ref[...])], axis=1)
        lows = jnp.concatenate([low0_ref[...], low], axis=0)
        acc[...] = dot(a, lows).astype(BF).reshape(acc.shape)
        for m, ref in ((core, gm_ref), (1 - core, go_ref)):
            ref[...] = jnp.stack([acc[a * 2 + m] for a in range(chips)])
    else:
        low_ref[...] = low


def turn(place, mid, fb, dn, c, at, w, gains, seq, before):
    d = c.shape[1]
    heads, n, bt = at.shape
    chips, _, steps = w.shape[:3]
    per = d // (chips * 2 * steps)
    rows = pl.BlockSpec((bt, d), lambda i, p: (seq, 0), pipeline_mode=pl.Buffered(1))
    here = fixed(bt, d)
    arrays, specs = output_rows(w)
    last = before is not None
    shape = jax.ShapeDtypeStruct
    if last:
        grad = before[2].shape
        behind = pl.BlockSpec(
            (chips, steps, per, d), lambda i, p: (0, 0, grad[2] // per - 1, 0), pipeline_mode=pl.Buffered(1)
        )
        anywhere = pl.BlockSpec(memory_space=pl.ANY)
    return pl.pallas_call(
        functools.partial(turn_kernel, last=last),
        grid_spec=pltpu.PrefetchScalarGridSpec(
            num_scalar_prefetch=1,
            grid=(1,),
            in_specs=[here, rows, rows, rows, fixed(heads, n, bt), *specs, fixed(8, d)]
            + ([fixed(heads, n, bt), here, anywhere, anywhere, anywhere] if last else []),
            out_specs=[rows, here, fixed(heads, n, bt), fixed(8, d)] + ([behind] * 2 if last else [here]),
            scratch_shapes=[pltpu.VMEM((bt, d), F32)]
            + ([pltpu.VMEM((chips * 2, steps, per, d), BF)] if last else []),
        ),
        out_shape=[shape(c.shape, BF), shape((bt, d), F32), shape((heads, n, bt), BF), shape((8, d), F32)]
        + ([shape(grad, BF), shape(grad, BF)] if last else [shape((bt, d), BF)]),
        input_output_aliases={11: 4, 12: 5, 13: 0} if last else {},
        compiler_params=params(),
        cost_estimate=cost((6 if last else 2) * bt * d * heads * n, 15e6),
        name="turn",
    )(place, mid, fb, dn, c, at, *arrays, gains, *(before if last else ()))


def project_back_kernel(*refs, last):
    place_ref, dqkv_ref, raw_ref, cos_ref, sin_ref, hg_ref, x_ref, dmid_ref, wm_ref, wo_ref, gains_ref = refs[:11]
    refs = refs[11:]
    if last:
        nx_ref, nx0_ref, dproj0_ref, sums0_ref, rows0_ref, head0_ref = refs[:6]
        dx_ref, gm_ref, go_ref, dproj, dn_scr, acc, extra = refs[7:]
    else:
        dx_ref, dproj, rows_ref, head_ref, dn_scr = refs
    bt, d = x_ref.shape
    core = place_ref[0]
    chips, steps, per, cols = wm_ref.shape
    wide = cols - 128
    hd, half = HEAD_DIMENSION, HEAD_DIMENSION // 2
    cos, sin = cos_ref[...], sin_ref[...]
    gains = [jnp.broadcast_to(hg_ref[:, j : j + 1], (hd, bt)) for j in (0, 1)]
    head_sums = [jnp.zeros((hd, bt), F32), jnp.zeros((hd, bt), F32)]
    for h in range(KEY_VALUE_HEADS):
        parts = []
        for slot in range(3):
            kind = 0 if slot < 2 else 1
            g = dqkv_ref[h, slot * hd : (slot + 1) * hd, :].astype(F32)
            v = raw_ref[h, slot * hd : (slot + 1) * hd, :].astype(F32)
            a, b = g[:half], g[half:]
            pre = jnp.concatenate([a * cos + b * sin, b * cos - a * sin], axis=0)
            factor = lax.rsqrt(jnp.mean(v * v, axis=0, keepdims=True) + epsilon)
            unit = v * factor
            head_sums[kind] += pre * unit
            pre = pre * gains[kind]
            back = factor * (pre - unit * jnp.mean(pre * unit, axis=0, keepdims=True))
            parts.append(back)
        parts.append(dqkv_ref[h, 3 * hd :, :].astype(F32))
        dproj[:, h * 256 : (h + 1) * 256] = jnp.concatenate(parts, axis=0).T.astype(BF)
    heads = [jnp.broadcast_to(jnp.sum(s, axis=1, keepdims=True), (hd, 128)) for s in head_sums]
    dp = dproj[...]
    dn = dot(dp, both(wm_ref[:, :, :, 0:wide], wo_ref[:, :, :, 0:wide]), NT)
    for n, at in enumerate(order(core, chips)):
        dn_scr[:, lanes(at)] = dn[:, n * 128 : (n + 1) * 128]
    dn = dn_scr[...]
    x = x_ref[...].astype(F32)
    r = lax.rsqrt(jnp.mean(x * x, axis=-1, keepdims=True) + epsilon)
    unit = x * r
    gain_sums = jnp.sum(dn * unit, axis=0, keepdims=True)
    g = dn * gains_ref[0:1]
    dx = dmid_ref[...] + r * (g - unit * jnp.mean(g * unit, axis=-1, keepdims=True))
    dx_ref[...] = dx.astype(BF)
    if not last:
        rows_ref[...] = jnp.broadcast_to(gain_sums, rows_ref.shape)
        for kind in (0, 1):
            head_ref[kind] = heads[kind]
        return
    acc[...] = (dot(nx0_ref[...], dproj0_ref[...], TN) + dot(nx_ref[...], dp, TN)).astype(BF).reshape(acc.shape)
    heads = [heads[kind] + head0_ref[kind] for kind in (0, 1)]
    lane = lax.broadcasted_iota(jnp.int32, (per, 128), 1)
    row = lax.broadcasted_iota(jnp.int32, (per, 128), 0)
    same = jnp.zeros((per, 128), F32)
    for n in range(4):
        same = jnp.where(lane == 2 + n, heads[n // 2][(n % 2) * per : (n % 2 + 1) * per, :], same)
    for n in range(3):
        same = jnp.where((lane == 6) & (row == n), jnp.sum(sums0_ref[n + 1 : n + 2, :], axis=1, keepdims=True), same)
    own = jnp.concatenate([gain_sums + rows0_ref[0:1], sums0_ref[0:1, :], jnp.zeros((126, d), F32)], axis=0)
    own = own.T.reshape(-1, per, 128)
    extra[...] = jnp.where((lane < 2)[None], own, same[None]).astype(BF).reshape(extra.shape)
    for n, ref in ((core, gm_ref), (1 - core, go_ref)):
        for a in range(chips):
            ref[a, :, :, 0:wide] = acc[a * 2 + n]
            ref[a, :, :, wide:] = extra[a * 2 + n]


def project_back(place, dqkv, raw, cos, sin, hg, x, dmid, mine, other, gains, seq, before):
    d = x.shape[1]
    kv, _, bt = raw.shape
    chips, steps, per, cols = mine.shape
    wide = cols - 128
    rows = pl.BlockSpec((bt, d), lambda i: (seq, 0), pipeline_mode=pl.Buffered(1))
    turns = pl.BlockSpec((32, bt), lambda i: (0, seq))
    last = before is not None
    shape = jax.ShapeDtypeStruct
    here = fixed(bt, d)
    grad = fixed(*mine.shape)
    proj = pltpu.VMEM((bt, wide), BF)
    return pl.pallas_call(
        functools.partial(project_back_kernel, last=last),
        grid=(1,),
        in_specs=[
            SMALL, fixed(kv, 256, bt), fixed(kv, 256, bt), turns, turns, fixed(64, 2), rows, here,
            fixed(*mine.shape), fixed(*mine.shape), fixed(8, d),
        ]
        + (
            [here, here, fixed(bt, wide), fixed(8, d), fixed(8, d), fixed(2, 64, 128), pl.BlockSpec(memory_space=pl.ANY)]
            if last
            else []
        ),
        out_specs=[rows] + ([grad, grad] if last else [fixed(bt, wide), fixed(8, d), fixed(2, 64, 128)]),
        input_output_aliases={17: 0} if last else {},
        out_shape=[shape(x.shape, BF)]
        + (
            [shape(mine.shape, BF)] * 2
            if last
            else [shape((bt, wide), BF), shape((8, d), F32), shape((2, 64, 128), F32)]
        ),
        scratch_shapes=(
            [
                proj,
                pltpu.VMEM((bt, d), F32),
                pltpu.VMEM((chips * 2, steps, per, wide), BF),
                pltpu.VMEM((chips * 2, steps, per, 128), BF),
            ]
            if last
            else [pltpu.VMEM((bt, d), F32)]
        ),
        compiler_params=params(),
        cost_estimate=cost((6 if last else 2) * bt * d * kv * 256, 20e6),
        name="project_back",
    )(place, dqkv, raw, cos, sin, hg, x, dmid, mine, other, gains, *(before if last else ()))


def add_kernel(a_ref, b_ref, out_ref):
    out_ref[...] = (a_ref[...].astype(F32) + b_ref[...].astype(F32)).astype(BF)


def add_up(a, b):
    n, rows, columns = a.shape[0] * a.shape[1], a.shape[2], a.shape[3]
    if rows < 128:
        return (a.astype(F32) + b.astype(F32)).astype(BF)
    block = pl.BlockSpec((n // 8, rows, columns), lambda i: (i, 0, 0))
    flat3 = (n, rows, columns)
    out = pl.pallas_call(
        add_kernel,
        grid=(8,),
        in_specs=[block, block],
        out_specs=block,
        out_shape=jax.ShapeDtypeStruct(flat3, BF),
        compiler_params=params(),
        cost_estimate=cost(n * rows * columns, 6 * n * rows * columns),
        name="add_up",
    )(a.reshape(flat3), b.reshape(flat3))
    return out.reshape(a.shape)


def heads_together(w):
    rows = w.shape[0]
    kv, hd = KEY_VALUE_HEADS, HEAD_DIMENSION
    q = w[:, : 2 * kv * hd].reshape(rows, kv, 2 * hd)
    k = w[:, 2 * kv * hd : 3 * kv * hd].reshape(rows, kv, hd)
    v = w[:, 3 * kv * hd :].reshape(rows, kv, hd)
    return jnp.concatenate([q, k, v], axis=2).reshape(rows, 4 * kv * hd)


def heads_apart(w):
    rows = w.shape[0]
    kv, hd = KEY_VALUE_HEADS, HEAD_DIMENSION
    w = w.reshape(rows, kv, 4 * hd)
    return jnp.concatenate(
        [
            w[:, :, : 2 * hd].reshape(rows, -1),
            w[:, :, 2 * hd : 3 * hd].reshape(rows, -1),
            w[:, :, 3 * hd :].reshape(rows, -1),
        ],
        axis=1,
    )


UNIT = 16
PARTS = (2, 3, 4)


def units_of(expand_weight, shrink_weight):
    per, width = expand_weight.shape
    owned, d = shrink_weight.shape
    units = owned // UNIT
    owners = width // (2 * owned)
    e = expand_weight.reshape(per, 2, owners // 8, 2, 4, units, UNIT).transpose(5, 0, 1, 3, 2, 4, 6)
    s = shrink_weight.reshape(units, UNIT, d)
    return jnp.concatenate([e.reshape(units, per, d), s], axis=1).reshape(units * (per + UNIT), d)


def units_apart(g, per):
    d = g.shape[1]
    g = g.reshape(-1, per + UNIT, d)
    units = g.shape[0]
    owners = d // (2 * UNIT)
    e = g[:, :per].reshape(units, per, 2, 2, owners // 8, 4, UNIT).transpose(1, 2, 4, 3, 5, 0, 6)
    return e.reshape(per, -1), g[:, per:].reshape(units * UNIT, d)


def after(x, *others):
    return lax.optimization_barrier((x, *others))[0]


def together(*xs):
    return lax.optimization_barrier(xs)


def heads_per_device(
    tokens, document_ids, mixer_weight, output_weight, mixer_gain, expand_weight, shrink_weight,
    feed_gain, head_gains, cotangent,
):
    seqs, rows, d = tokens.shape
    count = seqs * rows
    ring = ("chip", "core")
    steps = lax.axis_size("fsdp")
    core, z = lax.axis_index("core"), lax.axis_index("fsdp")
    place = jnp.stack([core, z]).astype(jnp.int32)
    device_count = lax.axis_size(ring) * steps
    per = mixer_gain.shape[0]
    swap = lambda a: lax.all_to_all(a, ring, 0, 0)
    across = lambda a: lax.ppermute(a, "core", [(0, 1), (1, 0)])

    def along_z(a):
        parts = [a] + [
            lax.ppermute(a, "fsdp", [(i, (i + s) % steps) for i in range(steps)]) for s in range(1, steps)
        ]
        return parts

    def in_order(parts):
        parts = [parts[-s % steps] for s in range(steps)]
        return lax.dynamic_slice_in_dim(jnp.stack(parts + parts), (steps - z) % steps, steps, 0)

    over_chips = lambda a: lax.all_gather(a, "chip", axis=0)
    reduce_chips = lambda a: lax.psum_scatter(a, "chip", scatter_dimension=0)

    def reduce_z(a):
        block = lambda s: lax.dynamic_index_in_dim(a, (z + s) % steps, 0, keepdims=False)
        out = block(0).astype(F32)
        for s in range(1, steps):
            out += lax.ppermute(block(s), "fsdp", [(i, (i + s) % steps) for i in range(steps)]).astype(F32)
        return out


    gains = jnp.pad(jnp.stack([mixer_gain, feed_gain], axis=1), ((0, 0), (0, 126)))
    mixer_parts = along_z(jnp.concatenate([heads_together(mixer_weight), gains], axis=1))

    below = jnp.sum(document_ids[:, None, :] < jnp.arange(4, dtype=jnp.int32)[None, :, None], axis=2)
    starts = jnp.sum(lax.all_gather(below.astype(jnp.int32), ring, axis=0), axis=0)
    mixer_parts, starts = lax.optimization_barrier((mixer_parts, starts))
    mixer_row = in_order(mixer_parts)
    mixer_mine = over_chips(mixer_row)

    owned = units_of(expand_weight, shrink_weight)
    owned = after(owned, mixer_row)
    pieces, at = [], 0
    for units in PARTS:
        pieces.append(owned[at : at + units * (per + UNIT)])
        at += units * (per + UNIT)
    first_row = in_order(along_z(jnp.concatenate([pieces[0], output_weight], axis=0)))
    first_part = lax.all_gather(first_row, ring, axis=0).reshape(-1, 2, *first_row.shape)
    mixer_other = across(mixer_mine)
    second = over_chips(after(pieces[1], first_row))
    third_z = along_z(after(pieces[2], first_row))

    earlier = jnp.zeros_like(document_ids)
    for n in range(1, 4):
        earlier = jnp.where(document_ids == n, starts[:, n][:, None], earlier)
    first = lax.axis_index(ring) * rows
    positions = first + jnp.arange(rows, dtype=jnp.int32)[None, :] - earlier
    half = HEAD_DIMENSION // 2
    inverse = rope_base ** (-(jnp.arange(half, dtype=F32) * 2.0 / HEAD_DIMENSION))
    angles = inverse[:, None] * positions.reshape(1, count).astype(F32)
    cos, sin = jnp.cos(angles), jnp.sin(angles)
    hg_forward = jnp.stack([head_gains[0] * QUERY_SCALE, head_gains[1]], axis=1)

    x = tokens.reshape(count, d)
    c = cotangent.reshape(count, d)
    projected = [project(place, x, mixer_mine, mixer_other, cos, sin, hg_forward, 0, rows)]
    projected.append(project(place, after(x, projected[0][0]), mixer_mine, mixer_other, cos, sin, hg_forward, 1, rows))
    qkv_heads = [swap(p[0]) for p in projected]
    gains_all = projected[0][3]

    qkv_heads[0], second = together(after(qkv_heads[0], projected[1][0]), second)
    onward = lambda a: lax.ppermute(a, "fsdp", [(i, (i + 1) % steps) for i in range(steps)])
    second_z = [second, onward(second)]
    out0 = attend(starts[0], qkv_heads[0])
    q1, second_z[1] = together(after(qkv_heads[1], out0[0]), second_z[1])
    second_z.append(onward(second_z[1]))
    out1 = attend(starts[1], q1)
    outs = [out0, out1]
    third = over_chips(in_order(after(third_z, qkv_heads[0])))
    attended = [swap(o[0]) for o in outs]
    attended[0], second_z[2] = together(after(attended[0], out1[0]), second_z[2])
    second_z.append(onward(second_z[2]))
    mids = [middle(place, x, attended[0], first_part, gains_all, 0)]
    attended[1] = after(attended[1], mids[0][1])
    mids.append(middle(place, x, attended[1], first_part, gains_all, 1))
    nm = [m[1] for m in mids]
    second_other = [across(t) for t in second_z[:3]]
    nm[1], second_z[3], *second_other = together(nm[1], second_z[3], *second_other)

    units = PARTS
    fb, dn, gm, go = feed(place, nm, c, first_part, steps, units[0], None, 0)
    exchanged = (gm, across(go))
    fb, third, last_other = together(fb, third, across(second_z[3]))
    part = (second_z, second_other + [last_other])
    fb, dn, gm, go = feed(place, nm, c, part, steps, units[1], (fb, dn), 0)
    second_exchanged = (gm, across(go))
    fb, third_other, summed = together(fb, across(third), add_up(*after(exchanged, fb)))
    chip_sums = [reduce_chips(summed)]
    fb, dn, gm, go = feed(place, nm, c, (third, third_other), steps, units[2], (fb, dn), per)
    carry = (fb, dn)

    turned = [turn(place, mids[0][0], *carry, c, attended[0], first_part, gains_all, 0, None)]
    before = (attended[0], turned[0][4], gm, go, turned[0][0])
    d_out_heads = [swap(turned[0][2])]
    turned.append(turn(place, mids[1][0], *carry, c, attended[1], first_part, gains_all, 1, before))
    gm, go = turned[1][4:6]
    d_out_heads.append(swap(turned[1][2]))
    d_out_heads[0], chip_sums[0], summed = together(
        d_out_heads[0], chip_sums[0], add_up(*after(second_exchanged, gm))
    )
    chip_sums.append(reduce_chips(summed))
    sums = turned[0][3] + turned[1][3]
    small = jnp.concatenate([sums[0:1], (mids[0][2] + mids[1][2])[0:1], sums[1:3], jnp.zeros((4, d), F32)], axis=0)

    back0 = attend_back(starts[0], qkv_heads[0], d_out_heads[0], out0[0], out0[1])
    d_out1, summed = together(after(d_out_heads[1], back0), add_up(*after((gm, across(go)), back0)))
    chip_sums.append(reduce_chips(summed))
    back1 = attend_back(starts[1], qkv_heads[1], d_out1, out1[0], out1[1])
    dqkv = [swap(back0), swap(back1)]
    dqkv[0], chip_sums[0], chip_sums[1] = together(after(dqkv[0], back1), chip_sums[0], chip_sums[1])
    z0 = reduce_z(chip_sums[0])
    z1 = reduce_z(chip_sums[1])

    hg = head_gains.T
    step0 = project_back(
        place, dqkv[0], projected[0][1], cos, sin, hg, x, turned[0][1], mixer_mine, mixer_other, gains_all, 0, None
    )
    before = (projected[1][2], projected[0][2], step0[1], small, step0[2], step0[3], step0[0])
    dqkv[1], z0, z1 = together(after(dqkv[1], step0[0]), z0, z1)
    dx1, gm, go = project_back(
        place, dqkv[1], projected[1][1], cos, sin, hg, x, turned[1][1], mixer_mine, mixer_other, gains_all, 1, before
    )
    gm, chip_sums[2] = together(gm, chip_sums[2])
    gradients = [z0, z1, reduce_z(chip_sums[2])]
    output_gradient = gradients[2][-per:]
    gradients[2] = gradients[2][:-per]
    last = reduce_chips(add_up(gm, across(go)))
    expand_gradient, shrink_gradient = units_apart(jnp.concatenate(gradients, axis=0), per)
    last = after(last, dx1)
    last = reduce_z(last)
    wide = mixer_weight.shape[1]
    small = last[:, wide:]
    return (
        turned[1][0].reshape(tokens.shape),
        dx1.reshape(tokens.shape),
        heads_apart(last[:, :wide]),
        output_gradient,
        small[:, 0],
        expand_gradient,
        shrink_gradient,
        small[:, 1],
        small[:, 2:6].T.reshape(2, 2 * per),
        jnp.sqrt(small[:3, 6] / (device_count * count * d)),
    )


def passed_along(block, axis, distance):
    devices = range(lax.axis_size(axis))
    route = [((i - distance) % len(devices), i) for i in devices]
    return lax.ppermute(block, axis, route)


def normalize_rows(values):
    factor = lax.rsqrt(jnp.mean(values * values, axis=-1, keepdims=True) + epsilon)
    return (values * factor, factor)


def normalize_back(values, factor, upstream):
    inner_mean = jnp.mean(upstream * values, axis=-1, keepdims=True)
    return factor * upstream - values * (factor * factor * factor) * inner_mean


def rotary_tables(positions, head_size):
    halfway = head_size // 2
    inverse = rope_base ** (-(jnp.arange(halfway, dtype=jnp.float32) * 2.0 / head_size))
    angles = positions.astype(jnp.float32)[..., None] * inverse
    angles = jnp.concatenate([angles, angles], axis=-1)
    return (jnp.cos(angles), jnp.sin(angles))


def rotate(values, cosine_table, sine_table):
    halfway = values.shape[-1] // 2
    turned = jnp.concatenate([-values[..., halfway:], values[..., :halfway]], axis=-1)
    return values * cosine_table + turned * sine_table


def rotate_back(upstream, cosine_table, sine_table):
    halfway = upstream.shape[-1] // 2
    scaled = upstream * sine_table
    turned = jnp.concatenate([scaled[..., halfway:], -scaled[..., :halfway]], axis=-1)
    return upstream * cosine_table + turned


def document_positions(own_documents, all_documents, offset_rows):
    earlier = jnp.sum(
        (all_documents[:, None, :] < own_documents[:, :, None]).astype(jnp.int32), axis=2
    )
    index_rows = offset_rows + jnp.arange(own_documents.shape[1], dtype=jnp.int32)
    return index_rows[None, :] - earlier


def allowed_pairs(query_docs, key_docs, query_index, key_index):
    same_document = query_docs[:, :, None] == key_docs[:, None, :]
    causal = query_index[:, None] >= key_index[None, :]
    return jnp.logical_and(same_document, causal[None, :, :])[:, None, None, :, :]


def column_product(left, right):
    return jnp.einsum("nd,nf->df", left, right, preferred_element_type=jnp.float32)


def per_device(
    tokens,
    document_ids,
    mixer_weight,
    output_weight,
    mixer_gain,
    expand_weight,
    shrink_weight,
    feed_gain,
    head_gains,
    cotangent,
):
    sequence_count, sequence_rows, model_width = tokens.shape
    count_of_tokens = sequence_count * sequence_rows
    query_groups = QUERY_HEADS // KEY_VALUE_HEADS
    query_feature_width = QUERY_HEADS * HEAD_DIMENSION
    key_feature_width = KEY_VALUE_HEADS * HEAD_DIMENSION
    cycle_size = lax.axis_size("ctx")
    cycle_index = lax.axis_index("ctx")
    device_count = lax.axis_size("ctx") * lax.axis_size("fsdp")
    owner_slot = lax.axis_index(("ctx", "fsdp"))
    gain_rows = mixer_gain.shape[0]
    offset_rows = cycle_index * sequence_rows
    all_documents = lax.all_gather(document_ids, "ctx", axis=1, tiled=True)
    positions = document_positions(document_ids, all_documents, offset_rows)
    cosine_table, sine_table = rotary_tables(positions.reshape(count_of_tokens), HEAD_DIMENSION)
    cosine_table = cosine_table[:, None, :]
    sine_table = sine_table[:, None, :]
    query_index = offset_rows + jnp.arange(sequence_rows, dtype=jnp.int32)
    mixer_all, output_all, mixer_gain_all = (
        lax.all_gather(mixer_weight, ("ctx", "fsdp"), axis=0, tiled=True),
        lax.all_gather(output_weight, ("ctx", "fsdp"), axis=0, tiled=True),
        lax.all_gather(mixer_gain, ("ctx", "fsdp"), axis=0, tiled=True),
    )
    stream = tokens.reshape(count_of_tokens, model_width).astype(jnp.float32)
    unit_in, factor_in = normalize_rows(stream)
    normed_in = (unit_in * mixer_gain_all.astype(jnp.float32)).astype(jnp.bfloat16)
    projected_heads = jnp.dot(normed_in, mixer_all, preferred_element_type=jnp.float32)
    query_raw = projected_heads[:, :query_feature_width].reshape(
        count_of_tokens, QUERY_HEADS, HEAD_DIMENSION
    )
    unrotated_key = projected_heads[
        :, query_feature_width : query_feature_width + key_feature_width
    ].reshape(count_of_tokens, KEY_VALUE_HEADS, HEAD_DIMENSION)
    value_rows = projected_heads[:, query_feature_width + key_feature_width :].astype(jnp.bfloat16)
    query_unit, query_factor = normalize_rows(query_raw)
    key_unit, key_factor = normalize_rows(unrotated_key)
    query_row_block = rotate(query_unit * head_gains[0], cosine_table, sine_table).astype(
        jnp.bfloat16
    )
    key_rows = rotate(key_unit * head_gains[1], cosine_table, sine_table).astype(jnp.bfloat16)
    query_head_rows = query_row_block.reshape(
        sequence_count, sequence_rows, KEY_VALUE_HEADS, query_groups, HEAD_DIMENSION
    ).transpose(0, 2, 3, 1, 4)
    key_send = key_rows.reshape(sequence_count, sequence_rows, key_feature_width)
    value_send = value_rows.reshape(sequence_count, sequence_rows, key_feature_width)
    statistics_shape = (sequence_count, KEY_VALUE_HEADS, query_groups, sequence_rows)
    initial = (
        jnp.full(statistics_shape, masked_score, jnp.float32),
        jnp.zeros(statistics_shape, jnp.float32),
        jnp.zeros(statistics_shape + (HEAD_DIMENSION,), jnp.float32),
    )
    carried = initial
    key_portion = lax.all_gather(key_send, "ctx", axis=1, tiled=True)
    value_portion = lax.all_gather(value_send, "ctx", axis=1, tiled=True)
    piece_rows = key_portion.shape[1]
    block_extent = math.gcd(piece_rows, 512)
    count_of_blocks = piece_rows // block_extent
    split_key_blocks = jnp.moveaxis(
        key_portion.reshape(
            sequence_count, count_of_blocks, block_extent, KEY_VALUE_HEADS, HEAD_DIMENSION
        ),
        1,
        0,
    )
    value_blocks = jnp.moveaxis(
        value_portion.reshape(
            sequence_count, count_of_blocks, block_extent, KEY_VALUE_HEADS, HEAD_DIMENSION
        ),
        1,
        0,
    )
    block_starts = jnp.arange(count_of_blocks, dtype=jnp.int32) * block_extent

    def one_block(running, block_items):
        current_key_block, current_value_block, block_start = block_items
        row_max, total_weight, weighted_sum = running
        key_docs = lax.dynamic_slice_in_dim(all_documents, block_start, block_extent, 1)
        key_index = block_start + jnp.arange(block_extent, dtype=jnp.int32)
        allowed = allowed_pairs(document_ids, key_docs, query_index, key_index)
        scores = (
            jnp.einsum(
                "skgrd,sjkd->skgrj",
                query_head_rows,
                current_key_block,
                preferred_element_type=jnp.float32,
            )
            * 0.125
        )
        masked = jnp.where(allowed, scores, masked_score)
        new_max = jnp.maximum(row_max, jnp.max(masked, axis=-1))
        rescale = jnp.exp(row_max - new_max)
        softmax_terms = jnp.where(allowed, jnp.exp(masked - new_max[..., None]), 0.0)
        total_weight = total_weight * rescale + jnp.sum(softmax_terms, axis=-1)
        weighted_sum = weighted_sum * rescale[..., None] + jnp.einsum(
            "skgrj,sjkd->skgrd",
            softmax_terms.astype(jnp.bfloat16),
            current_value_block,
            preferred_element_type=jnp.float32,
        )
        return ((new_max, total_weight, weighted_sum), None)

    carried, _ = lax.scan(one_block, carried, (split_key_blocks, value_blocks, block_starts))
    row_max, total_weight, weighted_sum = carried
    attn_heads = weighted_sum / total_weight[..., None]
    log_total = row_max + jnp.log(total_weight)
    attended = attn_heads.transpose(0, 3, 1, 2, 4).reshape(count_of_tokens, query_feature_width)
    attended_low = attended.astype(jnp.bfloat16)
    attn_branch = jnp.dot(attended_low, output_all, preferred_element_type=jnp.float32)
    middle = stream + attn_branch
    expand_all, shrink_all, feed_gain_all = (
        lax.all_gather(expand_weight, ("ctx", "fsdp"), axis=0, tiled=True),
        lax.all_gather(shrink_weight, ("ctx", "fsdp"), axis=0, tiled=True),
        lax.all_gather(feed_gain, ("ctx", "fsdp"), axis=0, tiled=True),
    )
    unit_mid, factor_mid = normalize_rows(middle)
    normed_mid = (unit_mid * feed_gain_all.astype(jnp.float32)).astype(jnp.bfloat16)
    gate_up = jnp.dot(normed_mid, expand_all, preferred_element_type=jnp.float32)
    gate_rows = gate_up[:, :FF]
    up_rows = gate_up[:, FF:]
    gate_sigmoid = jax.nn.sigmoid(gate_rows)
    gate_silu = gate_rows * gate_sigmoid
    hidden = (gate_silu * up_rows).astype(jnp.bfloat16)
    feed_branch = jnp.dot(hidden, shrink_all, preferred_element_type=jnp.float32)
    layer_out = middle + feed_branch
    squares = jnp.stack(
        [
            jnp.sum(attn_branch * attn_branch),
            jnp.sum(feed_branch * feed_branch),
            jnp.sum(layer_out * layer_out),
        ]
    )
    stat_totals = lax.psum(squares, ("ctx", "fsdp"))
    grad_branch = cotangent.reshape(count_of_tokens, model_width)
    grad_result = grad_branch.astype(jnp.float32)
    shrink_gradient = lax.psum_scatter(
        column_product(hidden, grad_branch), ("ctx", "fsdp"), scatter_dimension=0, tiled=True
    )
    grad_hidden = jnp.einsum(
        "nd,fd->nf", grad_branch, shrink_all, preferred_element_type=jnp.float32
    )
    grad_gate = grad_hidden * up_rows * gate_sigmoid * (1.0 + gate_rows * (1.0 - gate_sigmoid))
    grad_up = grad_hidden * gate_silu
    grad_gate_up = jnp.concatenate([grad_gate, grad_up], axis=1).astype(jnp.bfloat16)
    expand_gradient = lax.psum_scatter(
        column_product(normed_mid, grad_gate_up), ("ctx", "fsdp"), scatter_dimension=0, tiled=True
    )
    grad_normed_mid = jnp.einsum(
        "nf,df->nd", grad_gate_up, expand_all, preferred_element_type=jnp.float32
    )
    feed_gain_term = jnp.sum(grad_normed_mid * unit_mid, axis=0)
    grad_middle = grad_result + normalize_back(
        middle, factor_mid, grad_normed_mid * feed_gain_all.astype(jnp.float32)
    )
    grad_attn_low = grad_middle.astype(jnp.bfloat16)
    output_gradient = lax.psum_scatter(
        column_product(attended_low, grad_attn_low),
        ("ctx", "fsdp"),
        scatter_dimension=0,
        tiled=True,
    )
    attended_gradient = jnp.einsum(
        "nd,qd->nq", grad_attn_low, output_all, preferred_element_type=jnp.float32
    ).astype(jnp.bfloat16)
    heads_gradient = attended_gradient.reshape(
        sequence_count, sequence_rows, KEY_VALUE_HEADS, query_groups, HEAD_DIMENSION
    ).transpose(0, 2, 3, 1, 4)
    delta_rows = jnp.sum(heads_gradient.astype(jnp.float32) * attn_heads, axis=-1)
    zero_query = jnp.zeros(query_head_rows.shape, jnp.float32)

    def pair_terms(current_key_block, current_value_block, block_start):
        rows_per_block = current_key_block.shape[1]
        key_reshaped = current_key_block.reshape(
            sequence_count, rows_per_block, KEY_VALUE_HEADS, HEAD_DIMENSION
        )
        value_reshaped = current_value_block.reshape(
            sequence_count, rows_per_block, KEY_VALUE_HEADS, HEAD_DIMENSION
        )
        key_docs = lax.dynamic_slice_in_dim(all_documents, block_start, rows_per_block, 1)
        key_index = block_start + jnp.arange(rows_per_block, dtype=jnp.int32)
        allowed = allowed_pairs(document_ids, key_docs, query_index, key_index)
        scores = (
            jnp.einsum(
                "skgrd,sjkd->skgrj",
                query_head_rows,
                key_reshaped,
                preferred_element_type=jnp.float32,
            )
            * 0.125
        )
        probability = jnp.where(
            allowed, jnp.exp(jnp.where(allowed, scores, 0.0) - log_total[..., None]), 0.0
        )
        value_term = jnp.einsum(
            "skgrj,skgrd->sjkd",
            probability.astype(jnp.bfloat16),
            heads_gradient,
            preferred_element_type=jnp.float32,
        )
        grad_probability = jnp.einsum(
            "skgrd,sjkd->skgrj", heads_gradient, value_reshaped, preferred_element_type=jnp.float32
        )
        grad_scores = (probability * (grad_probability - delta_rows[..., None])).astype(
            jnp.bfloat16
        )
        query_term = (
            jnp.einsum(
                "skgrj,sjkd->skgrd", grad_scores, key_reshaped, preferred_element_type=jnp.float32
            )
            * 0.125
        )
        key_term = (
            jnp.einsum(
                "skgrj,skgrd->sjkd",
                grad_scores,
                query_head_rows,
                preferred_element_type=jnp.float32,
            )
            * 0.125
        )
        return (
            query_term,
            key_term.reshape(sequence_count, rows_per_block, key_feature_width),
            value_term.reshape(sequence_count, rows_per_block, key_feature_width),
        )

    zero_keys = jnp.zeros((sequence_count, sequence_rows, key_feature_width), jnp.float32)

    def cycle_step(cycle_turn, running):
        (
            current_key_block,
            current_value_block,
            key_gradient_accumulator,
            value_accum,
            query_accum,
        ) = running
        owner_index = (cycle_index - cycle_turn) % cycle_size
        query_term, key_term, value_term = pair_terms(
            current_key_block.astype(jnp.bfloat16),
            current_value_block.astype(jnp.bfloat16),
            owner_index * sequence_rows,
        )
        query_accum = query_accum + query_term
        key_gradient_accumulator = key_gradient_accumulator + key_term
        value_accum = value_accum + value_term
        current_key_block, current_value_block, key_gradient_accumulator, value_accum = (
            passed_along(current_key_block.astype(jnp.bfloat16), "ctx", 1).astype(
                current_key_block.dtype
            ),
            passed_along(current_value_block.astype(jnp.bfloat16), "ctx", 1).astype(
                current_value_block.dtype
            ),
            passed_along(key_gradient_accumulator.astype(jnp.bfloat16), "ctx", 1).astype(
                key_gradient_accumulator.dtype
            ),
            passed_along(value_accum.astype(jnp.bfloat16), "ctx", 1).astype(value_accum.dtype),
        )
        return (
            current_key_block,
            current_value_block,
            key_gradient_accumulator,
            value_accum,
            query_accum,
        )

    carried = lax.fori_loop(
        0,
        cycle_size,
        cycle_step,
        (
            key_send.astype(jnp.float32),
            value_send.astype(jnp.float32),
            zero_keys,
            zero_keys,
            zero_query,
        ),
    )
    key_gradient_accumulator, value_accum, query_accum = (carried[2], carried[3], carried[4])
    grad_query = query_accum.transpose(0, 3, 1, 2, 4).reshape(
        count_of_tokens, QUERY_HEADS, HEAD_DIMENSION
    )
    key_grad_total = key_gradient_accumulator.reshape(
        count_of_tokens, KEY_VALUE_HEADS, HEAD_DIMENSION
    )
    grad_value = value_accum.reshape(count_of_tokens, key_feature_width)
    grad_query_pre = rotate_back(grad_query, cosine_table, sine_table)
    grad_key_pre = rotate_back(key_grad_total, cosine_table, sine_table)
    head_terms = jnp.stack(
        [
            jnp.sum(grad_query_pre * query_unit, axis=(0, 1)),
            jnp.sum(grad_key_pre * key_unit, axis=(0, 1)),
        ]
    )
    grad_query_raw = normalize_back(query_raw, query_factor, grad_query_pre * head_gains[0])
    grad_key_raw = normalize_back(unrotated_key, key_factor, grad_key_pre * head_gains[1])
    grad_projected = jnp.concatenate(
        [
            grad_query_raw.reshape(count_of_tokens, query_feature_width),
            grad_key_raw.reshape(count_of_tokens, key_feature_width),
            grad_value,
        ],
        axis=1,
    ).astype(jnp.bfloat16)
    mixer_gradient = lax.psum_scatter(
        column_product(normed_in, grad_projected), ("ctx", "fsdp"), scatter_dimension=0, tiled=True
    )
    grad_normed_in = jnp.einsum(
        "nq,dq->nd", grad_projected, mixer_all, preferred_element_type=jnp.float32
    )
    mixer_gain_term = jnp.sum(grad_normed_in * unit_in, axis=0)
    grad_stream = grad_middle + normalize_back(
        stream, factor_in, grad_normed_in * mixer_gain_all.astype(jnp.float32)
    )
    feed_gain_total, mixer_gain_total, head_total = lax.psum(
        (feed_gain_term, mixer_gain_term, head_terms), ("ctx", "fsdp")
    )
    feed_gain_gradient = lax.dynamic_slice_in_dim(
        feed_gain_total, owner_slot * gain_rows, gain_rows, 0
    )
    mixer_gain_gradient = lax.dynamic_slice_in_dim(
        mixer_gain_total, owner_slot * gain_rows, gain_rows, 0
    )
    statistics = jnp.sqrt(stat_totals / (device_count * count_of_tokens * model_width))
    result = layer_out.astype(jnp.bfloat16).reshape(sequence_count, sequence_rows, model_width)
    tokens_gradient = grad_stream.astype(jnp.bfloat16).reshape(
        sequence_count, sequence_rows, model_width
    )
    return (
        result,
        tokens_gradient,
        mixer_gradient,
        output_gradient,
        mixer_gain_gradient,
        expand_gradient,
        shrink_gradient,
        feed_gain_gradient,
        head_total,
        statistics,
    )


def solution(mesh):
    function, ring = per_device, "ctx"
    if mesh.shape["ctx"] == KEY_VALUE_HEADS:
        shape = (KEY_VALUE_HEADS // 2, 2, mesh.shape["fsdp"])
        mesh = jax.sharding.Mesh(mesh.devices.reshape(shape), ("chip", "core", "fsdp"))
        function, ring = heads_per_device, ("chip", "core")
    every = (ring, "fsdp") if isinstance(ring, str) else ring + ("fsdp",)
    tokens, rows, vector = P("fsdp", ring, None), P(every, None), P(every)
    return jax.shard_map(
        function,
        mesh=mesh,
        in_specs=(
            tokens,
            P("fsdp", ring),
            rows,
            rows,
            vector,
            rows,
            rows,
            vector,
            P(),
            tokens,
        ),
        out_specs=(tokens, tokens, rows, rows, vector, rows, rows, vector, P(), P()),
        check_vma=False,
    )
```
